128 devices in a mesh: run: 16 (over z_lo, y, core), seg: 8 (over x, z_hi).
Axes of the slice: x: 4, y: 4, z: 4 (z_hi: 2, z_lo: 2; z = z_hi * 2 + z_lo), core: 2. Of those that a mesh axis runs over, the one named last changes fastest.
Arguments:
- diag_blocks: float32 [8, 32, 256, 256], P('seg', 'run'), as said below
- coupling: float32 [8, 32, 256, 256], P('seg', 'run')
- rhs: float32 [8, 32, 256, 128], P('seg', 'run'), may hold values from -0.65 to 0.65
Outputs:
- solution: float32 [8, 32, 256, 128], P('seg', 'run')
The draws below stay inside these ranges and needn't reach their ends.
Inputs may be any that keep to these rules, and one draw needn't show every extreme that they name: Together with coupling, diag_blocks makes A symmetric positive definite.
All inputs are finite; a program needn't handle non-finite values.
Results may differ from the reference program's by a relative error of at most 0.0003.
Values sent between devices are 32-bit elements; how exact they have to be, the bound alone decides.
No kernel may reach another device: no remote copies, remote signals or barrier semaphores. Data moves between devices by JAX's collectives and lax.ppermute only.
A program may use at most 128 MiB of HBM per device.

```python
import math
import jax
import jax.numpy as jnp
from jax import lax

B = 256
R = 128
SEGMENTS = 8
SEG_SLABS = 32


def conductances(key):
    slab_total = SEGMENTS * SEG_SLABS
    noise_key = jax.random.fold_in(key, 7)
    noise_raw = jax.random.normal(noise_key, (slab_total, B, B), jnp.float32)
    gram_part = jnp.einsum('sij,skj->sik', noise_raw, noise_raw) / B
    return 0.5 * jnp.eye(B, dtype=jnp.float32) + 0.5 * gram_part


def draw_diag_blocks(key, part):
    slab_total = SEGMENTS * SEG_SLABS
    conduct = conductances(key)
    rolled = jnp.roll(conduct, -1, axis=0)
    log_low = math.log(0.001)
    log_high = math.log(0.01)
    masses = jnp.exp(jax.random.uniform(jax.random.fold_in(key, 9), (slab_total, B), jnp.float32, log_low, log_high))
    blocks = conduct + rolled + masses[:, :, None] * jnp.eye(B, dtype=jnp.float32)
    return blocks.reshape(SEGMENTS, SEG_SLABS, B, B)


def draw_coupling(key, part):
    return (-conductances(key)).reshape(SEGMENTS, SEG_SLABS, B, B)


def draw_rhs(key, part):
    slab_total = SEGMENTS * SEG_SLABS
    rough_key = jax.random.fold_in(key, 21)
    rough = jnp.clip(0.1 * jax.random.normal(rough_key, (slab_total, B, R), jnp.float32), -0.6, 0.6)
    amplitude = 0.003
    phase = jax.random.uniform(jax.random.fold_in(key, 22), (), jnp.float32, 0.0, 2.0 * math.pi)
    position = jnp.arange(slab_total, dtype=jnp.float32) / slab_total
    profile = 1.0 + 0.6 * jnp.cos(3.0 * math.pi * position + phase)
    weights = jax.random.uniform(jax.random.fold_in(key, 23), (1, B, R), jnp.float32, 0.5, 1.5)
    values = rough + amplitude * profile[:, None, None] * weights
    return values.reshape(SEGMENTS, SEG_SLABS, B, R)


def setup_inputs(seed: int = 0) -> dict:
    seeds = jax.random.split(jax.random.key(seed), 4)
    diag_blocks = draw_diag_blocks(jax.random.fold_in(seeds[3], 71), 0)
    coupling = draw_coupling(jax.random.fold_in(seeds[3], 71), 0)
    rhs = draw_rhs(jax.random.fold_in(seeds[3], 71), 0)
    return {"diag_blocks": diag_blocks, "coupling": coupling, "rhs": rhs}


HIGH = lax.Precision.HIGHEST

def product(operand, second):
    return jnp.dot(operand, second, precision=HIGH, preferred_element_type=operand.dtype)

def apply_inverse(factor, columns):
    return jax.scipy.linalg.cho_solve((factor, True), columns)

def reference(diag_blocks, coupling, rhs):
    order_b = diag_blocks.shape[-1]
    slab_total = diag_blocks.shape[0] * diag_blocks.shape[1]
    diagonal = diag_blocks.reshape(slab_total, order_b, order_b)
    couples = coupling.reshape(slab_total, order_b, order_b)
    couples = couples.at[0].set(jnp.zeros_like(couples[0]))
    sources = rhs.reshape(slab_total, order_b, rhs.shape[-1])
    couples_after = jnp.concatenate([couples[1:], jnp.zeros_like(couples[:1])], axis=0)

    def forward(state_now, slab_item):
        solved_link, solved_prev = state_now
        diag_here, coup_here, coup_next, source_here = slab_item
        factor = jnp.linalg.cholesky(diag_here - product(coup_here, solved_link))
        link_here = apply_inverse(factor, coup_next.T)
        value_here = apply_inverse(factor, source_here - product(coup_here, solved_prev))
        return ((link_here, value_here), (link_here, value_here))
    initial = (jnp.zeros_like(diagonal[0]), jnp.zeros_like(sources[0]))
    _, (links, partials) = lax.scan(forward, initial, (diagonal, couples, couples_after, sources))

    def backward(later, slab_item):
        link_here, partial_value = slab_item
        result = partial_value - product(link_here, later)
        return (result, result)
    _, values = lax.scan(backward, jnp.zeros_like(sources[0]), (links, partials), reverse=True)
    return values.reshape(rhs.shape)
```

```python
import functools

import jax
import jax.numpy as jnp
from jax import lax
from jax.experimental import pallas as pl
from jax.experimental.pallas import tpu as pltpu
from jax.sharding import PartitionSpec as P

HIGH = lax.Precision.HIGHEST
f32 = jnp.float32
bf16 = jnp.bfloat16
LEVELS = 7
SQUARINGS = 5
TOLERANCE = 1e-3
AXES = ("run", "seg")


def chain_coords(flat):
    run, seg = flat >> 3, flat & 7
    return seg >> 1, ((seg & 1) << 1) | (run >> 3), (run >> 1) & 3, run & 1


def flat_index(x, z, y, core):
    return ((((z & 1) << 3) | (y << 1) | core) << 3) | (x << 1) | (z >> 1)


def partner(level, flat):
    x, z, y, core = chain_coords(flat)
    if level == 1:
        core = core ^ 1
    elif level == 2:
        y = y ^ 1
    elif level == 3:
        y = 3 - y
    elif level == 4:
        z = z ^ 1
    elif level == 5:
        z = 3 - z
    elif level == 6:
        x = x ^ 1
    else:
        x = 3 - x
    return flat_index(x, z, y, core)


def exchange(value, level):
    return lax.ppermute(value, AXES, [(flat, partner(level, flat)) for flat in range(128)])


def chain_index():
    run, seg = lax.axis_index("run"), lax.axis_index("seg")
    return seg * 16 + run


def bit(value, place):
    return lax.rem(lax.div(value, 1 << place), 2)


def own_stays(level):
    chain = chain_index()
    if level == LEVELS:
        return bit(chain, LEVELS - 1) == 0
    return bit(chain, level - 1) == bit(chain, level)


def nn(left, right, precision=None):
    return lax.dot_general(
        left, right, (((1,), (0,)), ((), ())), precision=precision, preferred_element_type=f32
    )


def nt(left, right, precision=None):
    return lax.dot_general(
        left, right, (((1,), (1,)), ((), ())), precision=precision, preferred_element_type=f32
    )


def split(value):
    upper = value.astype(bf16)
    return upper, (value - upper.astype(f32)).astype(bf16)


def three_pass(left, right):
    lh, ll = left
    rh, rl = right
    return nn(lh, rh) + (nn(lh, rl) + nn(ll, rh))


def inverse_into(matrix, out_ref):
    order = matrix.shape[0]
    rows = lax.broadcasted_iota(jnp.int32, (order, order), 0)
    identity = (rows == lax.broadcasted_iota(jnp.int32, (order, order), 1)).astype(f32)
    norm = jnp.max(jnp.sum(jnp.abs(matrix), axis=0, keepdims=True), axis=1, keepdims=True)
    scale = 1.75 / norm
    rest = identity - matrix * scale
    found = (identity + rest) * scale
    rest = rest.astype(bf16)
    rest = nn(rest, rest).astype(bf16)
    for step in range(1, SQUARINGS):
        found = found + nn(found.astype(bf16), rest)
        if step < SQUARINGS - 1:
            rest = nn(rest, rest).astype(bf16)
    upper = split(found)
    rest = identity - three_pass(split(matrix), upper)
    found = found + nn(upper[0], rest.astype(bf16))
    rest = identity - nn(matrix, found, HIGH)
    miss = jnp.sum(rest * rest)
    out_ref[...] = found + three_pass(split(found), split(rest))

    @pl.when(jnp.logical_not(miss < TOLERANCE * TOLERANCE))
    def _():
        out_ref[...] = identity * scale

        def unfinished(state):
            step, miss_now = state
            return jnp.logical_and(step < 64, miss_now >= TOLERANCE * TOLERANCE)

        def improve(state):
            now = out_ref[...]
            gap = identity - nn(matrix, now, HIGH)
            out_ref[...] = now + nn(now, gap, HIGH)
            return state[0] + 1, jnp.sum(gap * gap)

        lax.while_loop(unfinished, improve, (jnp.int32(0), jnp.float32(jnp.inf)))


def whole(other_refs, order, index=None):
    def part(ref):
        return ref[...] if index is None else ref[index * (order // 2) : (index + 1) * (order // 2), :]

    if len(other_refs) == 1:
        ref = other_refs[0]
        return ref[...] if index is None else ref[index * order : (index + 1) * order, :]
    first_core = lax.rem(lax.axis_index("run"), 2) == 0
    direct, swapped = part(other_refs[0]), part(other_refs[1])
    return jnp.concatenate(
        [jnp.where(first_core, direct, swapped), jnp.where(first_core, swapped, direct)], axis=0
    )


def own_half(ref, base, order):
    half = order // 2
    core = lax.rem(lax.axis_index("run"), 2)
    return ref[pl.ds(pl.multiple_of(base + core * half, half), half), :]


def send_matrices(own_ss, own_ps, send_ss, send_ps, order):
    half = order // 2
    send_ss[...] = own_half(own_ss, 0, order)
    send_ps[:half, :] = own_half(own_ps, 0, order)
    send_ps[half:, :] = own_half(own_ps, order, order)


def first_matrices_kernel(diag, couple, inv, gain, ss, ps):
    order = inv.shape[0]
    inverse_into(diag[0], inv)
    start = chain_index() == 0
    above = jnp.where(start, 0.0, couple[0]).T
    below = couple[1]
    inverse = inv[...]
    gain_above = nn(above, inverse, HIGH)
    gain_below = nn(below, inverse, HIGH)
    own_above = -nt(gain_above, above, HIGH)
    own_below = diag[1] - nt(gain_below, below, HIGH)
    link = -nt(gain_above, below, HIGH)
    left = lax.rem(lax.axis_index("run"), 2) == 0
    gain[0] = gain_above
    gain[1] = gain_below
    ss[...] = jnp.where(left, own_below, own_above)
    ps[order:, :] = jnp.where(left, own_above, own_below)
    ps[:order, :] = jnp.where(left, link, link.T)


def first_sources_kernel(source, inv, gain, sources, back, partial):
    columns = partial.shape[1]
    order = inv.shape[0]
    held = source[0]
    source_above = -nn(gain[0], held, HIGH)
    source_below = source[1] - nn(gain[1], held, HIGH)
    left = lax.rem(lax.axis_index("run"), 2) == 0
    sources[:, :columns] = jnp.where(left, source_above, source_below)
    sources[:, columns:] = jnp.where(left, source_below, source_above)
    partial[...] = nn(inv[...], held, HIGH)
    back[:, :order] = gain[0].T
    back[:, order:] = gain[1].T


def invert_kernel(count, own_ss, own_ps, *refs):
    others, (inv, gain_own, reduced_own) = refs[:count], refs[count:]
    order = inv.shape[0]
    inverse_into(own_ss[...] + whole(others, order), inv)
    link_own = own_ps[:order, :]
    gain_own[...] = nn(link_own, inv[...], HIGH)
    reduced_own[...] = own_ps[order:, :] - nt(gain_own[...], link_own, HIGH)


def merge_kernel(level, count, inv, gain_own, reduced_own, *refs):
    others, outs = refs[:count], refs[count:]
    gain_other, ss, ps = outs[:3]
    order = inv.shape[0]
    stays = own_stays(level)
    link_other = whole(others, order, 0)
    gain_other[...] = nn(link_other, inv[...], HIGH)
    cross = -nt(gain_own[...], link_other, HIGH)
    reduced_other = whole(others, order, 1) - nt(gain_other[...], link_other, HIGH)
    own = reduced_own[...]
    ss[...] = jnp.where(stays, reduced_other, own)
    ps[order:, :] = jnp.where(stays, own, reduced_other)
    ps[:order, :] = jnp.where(stays, cross, cross.T)
    if len(outs) > 3:
        send_matrices(ss, ps, outs[3], outs[4], order)


def sources_kernel(level, count, inv, gain_own, gain_other, own_f, *refs):
    others, outs = refs[:count], refs[count:]
    sources, back, partial = outs[:3]
    order, columns = partial.shape
    stays = own_stays(level)
    own = own_f[...]
    other = whole(others, order)
    held = own[:, columns:] + other[:, columns:]
    after_own = own[:, :columns] - nn(gain_own[...], held, HIGH)
    after_other = other[:, :columns] - nn(gain_other[...], held, HIGH)
    sources[:, :columns] = jnp.where(stays, after_own, after_other)
    sources[:, columns:] = jnp.where(stays, after_other, after_own)
    if len(outs) > 3:
        outs[3][...] = own_half(sources, 0, order)
    partial[...] = nn(inv[...], held, HIGH)
    back_own, back_other = gain_own[...].T, gain_other[...].T
    back[:, :order] = jnp.where(stays, back_own, back_other)
    back[:, order:] = jnp.where(stays, back_other, back_own)


def last_inverse_kernel(ss, inv):
    inverse_into(ss[...], inv)


def back_kernel(inv, sources, *refs):
    backs, partials, result = refs[: LEVELS + 1], refs[LEVELS + 1 : -1], refs[-1]
    columns = result.shape[-1]
    outer = jnp.zeros(result.shape[1:], f32)
    inner = nn(inv[...], sources[:, columns:], HIGH)
    for level in range(LEVELS, -1, -1):
        if level == 0:
            left = lax.rem(lax.axis_index("run"), 2) == 0
            outer, inner = jnp.where(left, outer, inner), jnp.where(left, inner, outer)
            result[1] = inner
        middle = partials[level][...] - nn(
            backs[level][...], jnp.concatenate([outer, inner], axis=0), HIGH
        )
        if level == 0:
            result[0] = middle
        else:
            outer = jnp.where(own_stays(level), outer, inner)
            inner = middle


def call(kernel, name, operands, shapes, flops=0):
    vmem = pl.BlockSpec(memory_space=pltpu.VMEM)
    moved = sum(value.size for value in operands) * 4
    return pl.pallas_call(
        kernel,
        out_shape=[jax.ShapeDtypeStruct(shape, f32) for shape in shapes],
        in_specs=[vmem] * len(operands),
        out_specs=[vmem] * len(shapes),
        name=name,
        compiler_params=pltpu.CompilerParams(vmem_limit_bytes=40 * 1024 * 1024),
        cost_estimate=pl.CostEstimate(flops=flops, bytes_accessed=moved, transcendentals=0),
    )(*operands)


def local(diag_blocks, coupling, rhs):
    order, columns = rhs.shape[2:]
    square, tall, wide = (order, order), (2 * order, order), (order, 2 * order)
    half, thin = (order // 2, order), (order // 2, 2 * columns)
    flat, slim = (order, 2 * columns), (order, columns)
    cube = 2 * order**3 * 6
    inv, gains, ss, ps = call(
        first_matrices_kernel, "first_matrices", (diag_blocks[0], coupling[0]),
        (square, (2, order, order), square, tall), 12 * cube,
    )
    sources, back, partial = call(
        first_sources_kernel, "first_sources", (rhs[0], inv, gains), (flat, wide, slim), 2 * cube
    )
    backs, partials = [back], [partial]
    sends = (ss, ps, sources)
    for level in range(1, LEVELS + 1):
        def arrived(value):
            direct = exchange(value, level)
            return (direct,) if level == 1 else (direct, exchange(direct, 1))

        last = level == LEVELS
        others_ss = arrived(sends[0])
        others_ps = arrived(sends[1])
        others_f = arrived(sends[2])
        count = len(others_ss)
        inv, gain_own, reduced_own = call(
            functools.partial(invert_kernel, count), f"invert_{level}", (ss, ps) + others_ss,
            (square, square, square), 8 * cube,
        )
        gain_other, ss, ps, *send_mats = call(
            functools.partial(merge_kernel, level, count), f"merge_{level}",
            (inv, gain_own, reduced_own) + others_ps,
            (square, square, tall) + (() if last else (half, square)), 3 * cube,
        )
        sources, back, partial, *send_f = call(
            functools.partial(sources_kernel, level, count), f"sources_{level}",
            (inv, gain_own, gain_other, sources) + others_f,
            (flat, wide, slim) + (() if last else (thin,)), 2 * cube,
        )
        backs.append(back)
        partials.append(partial)
        sends = tuple(send_mats) + tuple(send_f)
    (inv,) = call(last_inverse_kernel, "last_inverse", (ss,), (square,), 6 * cube)
    (result,) = call(
        back_kernel, "back", (inv, sources, *backs, *partials), ((2, order, columns),), 8 * cube
    )
    return result[None]


def solution(mesh):
    spec = P("seg", "run", None, None)
    return jax.shard_map(
        local, mesh=mesh, in_specs=(spec, spec, spec), out_specs=spec, check_vma=False
    )
```

```python
import functools

import jax
import jax.numpy as jnp
from jax import lax
from jax.experimental import pallas as pl
from jax.experimental.pallas import tpu as pltpu
from jax.sharding import PartitionSpec as P

HIGH = lax.Precision.HIGHEST
f32 = jnp.float32
bf16 = jnp.bfloat16
LEVELS = 7
TOLERANCE = 1e-3
AXES = ("run", "seg")


def chain_coords(flat):
    run, seg = flat >> 3, flat & 7
    return seg >> 1, ((seg & 1) << 1) | (run >> 3), (run >> 1) & 3, run & 1


def flat_index(x, z, y, core):
    return ((((z & 1) << 3) | (y << 1) | core) << 3) | (x << 1) | (z >> 1)


def partner(level, flat):
    x, z, y, core = chain_coords(flat)
    if level == 1:
        core = core ^ 1
    elif level == 2:
        y = y ^ 1
    elif level == 3:
        y = 3 - y
    elif level == 4:
        z = z ^ 1
    elif level == 5:
        z = 3 - z
    elif level == 6:
        x = x ^ 1
    else:
        x = 3 - x
    return flat_index(x, z, y, core)


def exchange(value, level):
    return lax.ppermute(value, AXES, [(flat, partner(level, flat)) for flat in range(128)])


def chain_index():
    run, seg = lax.axis_index("run"), lax.axis_index("seg")
    return seg * 16 + run


def bit(value, place):
    return lax.rem(lax.div(value, 1 << place), 2)


def own_stays(level):
    chain = chain_index()
    if level == LEVELS:
        return bit(chain, LEVELS - 1) == 0
    return bit(chain, level - 1) == bit(chain, level)


def nn(left, right, precision=None):
    return lax.dot_general(
        left, right, (((1,), (0,)), ((), ())), precision=precision, preferred_element_type=f32
    )


def nt(left, right, precision=None):
    return lax.dot_general(
        left, right, (((1,), (1,)), ((), ())), precision=precision, preferred_element_type=f32
    )


def split(value):
    upper = value.astype(bf16)
    return upper, (value - upper.astype(f32)).astype(bf16)


def three_pass(left, right):
    lh, ll = left
    rh, rl = right
    return nn(lh, rh) + (nn(lh, rl) + nn(ll, rh))


def inverse_into(matrix, out_ref, squarings=5):
    order = matrix.shape[0]
    rows = lax.broadcasted_iota(jnp.int32, (order, order), 0)
    identity = (rows == lax.broadcasted_iota(jnp.int32, (order, order), 1)).astype(f32)
    norm = jnp.max(jnp.sum(jnp.abs(matrix), axis=0, keepdims=True), axis=1, keepdims=True)
    scale = 1.75 / norm
    rest = identity - matrix * scale
    found = (identity + rest) * scale
    rest = rest.astype(bf16)
    rest = nn(rest, rest).astype(bf16)
    for step in range(1, squarings):
        found = found + nn(found.astype(bf16), rest)
        if step < squarings - 1:
            rest = nn(rest, rest).astype(bf16)
    upper = split(found)
    rest = identity - three_pass(split(matrix), upper)
    found = found + nn(upper[0], rest.astype(bf16))
    rest = identity - nn(matrix, found, HIGH)
    miss = jnp.sum(rest * rest)
    out_ref[...] = found + three_pass(split(found), split(rest))

    @pl.when(jnp.logical_not(miss < TOLERANCE * TOLERANCE))
    def _():
        out_ref[...] = identity * scale

        def unfinished(state):
            step, miss_now = state
            return jnp.logical_and(step < 64, miss_now >= TOLERANCE * TOLERANCE)

        def improve(state):
            now = out_ref[...]
            gap = identity - nn(matrix, now, HIGH)
            out_ref[...] = now + nn(now, gap, HIGH)
            return state[0] + 1, jnp.sum(gap * gap)

        lax.while_loop(unfinished, improve, (jnp.int32(0), jnp.float32(jnp.inf)))


HALF = 128
PACKED = HALF + 8


def on_first_core():
    return lax.rem(lax.axis_index("run"), 2) == 0


def ordered(direct, swapped):
    first = on_first_core()
    return jnp.where(first, direct, swapped), jnp.where(first, swapped, direct)


def triangle():
    rows = lax.broadcasted_iota(jnp.int32, (HALF, HALF), 0)
    columns = lax.broadcasted_iota(jnp.int32, (HALF, HALF), 1)
    return rows, columns


def pack_symmetric(value, first):
    rows, columns = triangle()
    upper_left, lower_right = value[:HALF, :HALF], value[HALF:, HALF:]
    diagonal = jnp.sum(jnp.where(rows == columns, lower_right, 0.0), axis=0, keepdims=True)
    both = jnp.where(rows >= columns, upper_left, lower_right)
    main = jnp.where(first, value[HALF:, :HALF], both)
    return main, jnp.broadcast_to(diagonal, (8, HALF))


def unpack_symmetric(from_first, from_second):
    rows, columns = triangle()
    lower_left, diagonal = from_first[:HALF], from_first[HALF : HALF + 1]
    both = from_second[:HALF]
    turned = both.T
    upper_left = jnp.where(rows >= columns, both, turned)
    lower_right = jnp.where(rows < columns, both, turned)
    lower_right = jnp.where(rows == columns, diagonal, lower_right)
    return jnp.concatenate(
        [
            jnp.concatenate([upper_left, lower_left.T], axis=1),
            jnp.concatenate([lower_left, lower_right], axis=1),
        ],
        axis=0,
    )


def send_separator(value, send):
    main, diagonal = pack_symmetric(value, on_first_core())
    send[:HALF, :] = main
    send[HALF:, :] = diagonal


def send_link(link, outer, send):
    first = on_first_core()
    rows = jnp.where(first, link[:HALF], link[HALF:])
    send[:HALF, :] = rows[:, :HALF]
    send[HALF : 2 * HALF, :] = rows[:, HALF:]
    main, diagonal = pack_symmetric(outer, first)
    send[2 * HALF : 3 * HALF, :] = main
    send[3 * HALF :, :] = diagonal


def received_separator(refs):
    if len(refs) == 1:
        return refs[0][...]
    return unpack_symmetric(*ordered(refs[0][...], refs[1][...]))


def received_link(refs):
    if len(refs) == 1:
        order = refs[0].shape[1]
        return refs[0][:order, :], refs[0][order:, :]
    upper, lower = ordered(refs[0][...], refs[1][...])
    link = jnp.concatenate(
        [
            jnp.concatenate([upper[:HALF], upper[HALF : 2 * HALF]], axis=1),
            jnp.concatenate([lower[:HALF], lower[HALF : 2 * HALF]], axis=1),
        ],
        axis=0,
    )
    return link, unpack_symmetric(upper[2 * HALF :], lower[2 * HALF :])


def first_invert_kernel(diag, inv):
    inverse_into(diag[0], inv)


def first_merge_kernel(inv, diag, couple, gain_own, gain_other, ss, ps):
    order = inv.shape[0]
    start = chain_index() == 0
    above = jnp.where(start, 0.0, couple[0]).T
    below = couple[1]
    inverse = inv[...]
    gain_above = nn(above, inverse, HIGH)
    gain_below = nn(below, inverse, HIGH)
    own_above = -nt(gain_above, above, HIGH)
    own_below = diag[1] - nt(gain_below, below, HIGH)
    link = -nt(gain_above, below, HIGH)
    left = on_first_core()
    gain_own[...] = jnp.where(left, gain_above, gain_below)
    gain_other[...] = jnp.where(left, gain_below, gain_above)
    ss[...] = jnp.where(left, own_below, own_above)
    ps[order:, :] = jnp.where(left, own_above, own_below)
    ps[:order, :] = jnp.where(left, link, link.T)


def first_sources_kernel(source, inv, gain_own, gain_other, _, sources, partial):
    columns = partial.shape[1]
    held = source[0]
    left = on_first_core()
    sources[:, :columns] = jnp.where(left, 0.0, source[1]) - nn(gain_own[...], held, HIGH)
    sources[:, columns:] = jnp.where(left, source[1], 0.0) - nn(gain_other[...], held, HIGH)
    partial[...] = nn(inv[...], held, HIGH)


def first_factors_kernel(gain_own, gain_other, partial, _, factors, offset):
    order, columns = partial.shape
    rows = lax.broadcasted_iota(jnp.int32, (order, order), 0)
    identity = (rows == lax.broadcasted_iota(jnp.int32, (order, order), 1)).astype(f32)
    left = on_first_core()
    factors[0, :order, :] = gain_own[...].T
    factors[1, :order, :] = gain_other[...].T
    factors[0, order:, :] = jnp.where(left, 0.0, -identity)
    factors[1, order:, :] = jnp.where(left, -identity, 0.0)
    offset[:order, :] = partial[...]
    offset[order:, :] = jnp.zeros((order, columns), f32)


def invert_kernel(count, own_ss, own_ps, _, *refs):
    others, (inv, gain_own, reduced_own) = refs[:count], refs[count:]
    order = inv.shape[0]
    inverse_into(own_ss[...] + received_separator(others), inv)
    link_own = own_ps[:order, :]
    gain_own[...] = nn(link_own, inv[...], HIGH)
    reduced_own[...] = own_ps[order:, :] - nt(gain_own[...], link_own, HIGH)


def relay_kernel(_, arrived, sources, passed, send_f):
    passed[...] = arrived[...]
    send_f[...] = sources[...]


def merge_kernel(level, count, inv, gain_own, reduced_own, *refs):
    others, (gain_other, ss, ps, send_ss, send_ps) = refs[:count], refs[count:]
    order = inv.shape[0]
    stays = own_stays(level)
    link_other, outer_other = received_link(others)
    gain = nn(link_other, inv[...], HIGH)
    gain_other[...] = gain
    cross = -nt(gain_own[...], link_other, HIGH)
    reduced_other = outer_other - nt(gain, link_other, HIGH)
    own = reduced_own[...]
    separator = jnp.where(stays, reduced_other, own)
    outer = jnp.where(stays, own, reduced_other)
    link = jnp.where(stays, cross, cross.T)
    ss[...] = separator
    ps[order:, :] = outer
    ps[:order, :] = link
    send_separator(separator, send_ss)
    send_link(link, outer, send_ps)


def sources_step(level, inv, gain_own, gain_other, own_f, other_f):
    columns = own_f.shape[1] // 2
    stays = own_stays(level)
    own, other = own_f[...], other_f[...]
    held = own[:, columns:] + other[:, columns:]
    after_own = own[:, :columns] - nn(gain_own[...], held, HIGH)
    after_other = other[:, :columns] - nn(gain_other[...], held, HIGH)
    partial = nn(inv[...], held, HIGH)
    return jnp.where(stays, after_own, after_other), jnp.where(stays, after_other, after_own), partial


def sources_kernel(level, inv, gain_own, gain_other, own_f, other_f, _, sources, partial):
    columns = partial.shape[1]
    outer, inner, found = sources_step(level, inv, gain_own, gain_other, own_f, other_f)
    sources[:, :columns] = outer
    sources[:, columns:] = inner
    partial[...] = found


def factors_step(level, gain_own, gain_other, partial, factors, offset):
    stays = own_stays(level)
    inner = factors[1]
    new_offset = offset[...] - nn(inner, partial[...], HIGH)
    own_end = factors[0] - nt(inner, gain_own[...], HIGH)
    other_end = -nt(inner, gain_other[...], HIGH)
    return jnp.where(stays, own_end, other_end), jnp.where(stays, other_end, own_end), new_offset


def factors_kernel(level, gain_own, gain_other, partial, _, factors, offset, new_factors, new_offset):
    outer, inner, moved = factors_step(level, gain_own, gain_other, partial, factors, offset)
    new_factors[0] = outer
    new_factors[1] = inner
    new_offset[...] = moved


def end_kernel(ss, ps, end_inv, end_gain, new_ss, send_ss):
    order = ss.shape[0]
    rows = lax.broadcasted_iota(jnp.int32, (order, order), 0)
    identity = (rows == lax.broadcasted_iota(jnp.int32, (order, order), 1)).astype(f32)
    right = bit(chain_index(), LEVELS - 1) == 1
    inverse_into(jnp.where(right, ps[order:, :], identity), end_inv, 6)
    turned = ps[:order, :].T
    gain = nn(turned, end_inv[...], HIGH)
    end_gain[...] = gain
    separator = ss[...] - nt(gain, turned, HIGH)
    new_ss[...] = separator
    send_separator(separator, send_ss)


def end_sources_kernel(
    level, inv, gain_own, gain_other, own_f, other_f, end_inv, end_gain, _, sources, partial, end_partial
):
    outer, inner, found = sources_step(level, inv, gain_own, gain_other, own_f, other_f)
    sources[...] = inner - nn(end_gain[...], outer, HIGH)
    partial[...] = found
    end_partial[...] = nn(end_inv[...], outer, HIGH)


def end_factors_kernel(
    level, gain_own, gain_other, partial, _, factors, offset, end_gain, end_partial,
    new_factors, new_offset,
):
    outer, inner, moved = factors_step(level, gain_own, gain_other, partial, factors, offset)
    new_offset[...] = moved - nn(outer, end_partial[...], HIGH)
    new_factors[...] = inner - nt(outer, end_gain[...], HIGH)


def last_invert_kernel(count, own_ss, _, *refs):
    inverse_into(own_ss[...] + received_separator(refs[:count]), refs[count])


def back_kernel(inv, own_f, other_f, factors, offset, result):
    order = inv.shape[0]
    middle = nn(inv[...], own_f[...] + other_f[...], HIGH)
    both = offset[...] - nn(factors[...], middle, HIGH)
    result[0] = both[:order]
    result[1] = both[order:]


def call(kernel, name, operands, shapes, flops):
    vmem = pl.BlockSpec(memory_space=pltpu.VMEM)
    return pl.pallas_call(
        kernel,
        out_shape=[jax.ShapeDtypeStruct(shape, f32) for shape in shapes],
        in_specs=[vmem] * len(operands),
        out_specs=[vmem] * len(shapes),
        name=name,
        compiler_params=pltpu.CompilerParams(vmem_limit_bytes=40 << 20),
        cost_estimate=pl.CostEstimate(flops=flops, bytes_accessed=4096, transcendentals=0),
    )(*operands)


MICRO = 1_000_000_000


def local(diag_blocks, coupling, rhs):
    order, columns = rhs.shape[2:]
    square, tall = (order, order), (2 * order, order)
    small, medium = (PACKED, HALF), (2 * HALF + PACKED, HALF)
    flat, slim = (order, 2 * columns), (order, columns)
    double, long = (2, 2 * order, order), (2 * order, columns)
    (inv,) = call(first_invert_kernel, "first_invert", (diag_blocks[0],), (square,), 4 * MICRO)
    gain_own, gain_other, ss, ps = call(
        first_merge_kernel, "first_merge", (inv, diag_blocks[0], coupling[0]),
        (square, square, square, tall), MICRO,
    )
    others_ss = (exchange(ss, 1),)
    others_ps = (exchange(ps, 1),)
    sources, partial = call(
        first_sources_kernel, "first_sources", (rhs[0], inv, gain_own, gain_other, ss),
        (flat, slim), MICRO // 2,
    )
    other_f = exchange(sources, 1)
    before = (gain_own, gain_other, partial)
    factors = offset = None
    waited = partial
    for level in range(1, LEVELS):
        count = len(others_ss)
        inv, gain_own, reduced_own = call(
            functools.partial(invert_kernel, count), f"invert_{level}",
            (ss, ps, waited) + others_ss, (square, square, square), 10 * MICRO,
        )
        if level > 1:
            passed, send_f = call(
                relay_kernel, f"relay_{level}", (inv, direct_ps, sources), (medium, flat), MICRO // 10
            )
            others_ps = (direct_ps, exchange(passed, 1))
            other_f = exchange(send_f, level)
        gain_other, ss, ps, send_ss, send_ps = call(
            functools.partial(merge_kernel, level, count), f"merge_{level}",
            (inv, gain_own, reduced_own) + others_ps, (square, square, tall, small, medium), MICRO,
        )
        if level == LEVELS - 1:
            end_inv, end_gain, ss, send_ss = call(
                end_kernel, "end", (ss, ps), (square, square, square, small), 4 * MICRO
            )
        direct_ss = exchange(send_ss, level + 1)
        others_ss = (direct_ss, exchange(direct_ss, 1))
        if level < LEVELS - 1:
            direct_ps = exchange(send_ps, level + 1)
        if factors is None:
            factors, offset = call(
                first_factors_kernel, "first_factors", before + (send_ss,), (double, long), MICRO
            )
        else:
            factors, offset = call(
                functools.partial(factors_kernel, level - 1), f"factors_{level - 1}",
                before + (send_ss, factors, offset), (double, long), MICRO,
            )
        if level < LEVELS - 1:
            sources, partial = call(
                functools.partial(sources_kernel, level), f"sources_{level}",
                (inv, gain_own, gain_other, sources, other_f, offset), (flat, slim), MICRO // 2,
            )
        else:
            sources, partial, end_partial = call(
                functools.partial(end_sources_kernel, level), "end_sources",
                (inv, gain_own, gain_other, sources, other_f, end_inv, end_gain, offset),
                (slim, slim, slim), MICRO,
            )
        before = (gain_own, gain_other, partial)
        waited = sources
    other_f = exchange(sources, LEVELS)
    factors, offset = call(
        functools.partial(end_factors_kernel, level), "end_factors",
        before + (sources, factors, offset, end_gain, end_partial), (tall, long), MICRO,
    )
    (inv,) = call(
        functools.partial(last_invert_kernel, 2), "last_invert", (ss, offset) + others_ss,
        (square,), 10 * MICRO,
    )
    (result,) = call(
        back_kernel, "back", (inv, sources, other_f, factors, offset), ((2, order, columns),), MICRO
    )
    return result[None]


def solution(mesh):
    spec = P("seg", "run", None, None)
    return jax.shard_map(
        local, mesh=mesh, in_specs=(spec, spec, spec), out_specs=spec, check_vma=False
    )
```

```python
import functools

import jax
import jax.numpy as jnp
from jax import lax
from jax.experimental import pallas as pl
from jax.experimental.pallas import tpu as pltpu
from jax.sharding import PartitionSpec as P

HIGH = lax.Precision.HIGHEST
f32 = jnp.float32
bf16 = jnp.bfloat16
LEVELS = 7
TOLERANCE = 4e-3
AXES = ("run", "seg")


def chain_coords(flat):
    run, seg = flat >> 3, flat & 7
    return seg >> 1, ((seg & 1) << 1) | (run >> 3), (run >> 1) & 3, run & 1


def flat_index(x, z, y, core):
    return ((((z & 1) << 3) | (y << 1) | core) << 3) | (x << 1) | (z >> 1)


def partner(level, flat):
    x, z, y, core = chain_coords(flat)
    if level == 1:
        core = core ^ 1
    elif level == 2:
        y = y ^ 1
    elif level == 3:
        y = 3 - y
    elif level == 4:
        z = z ^ 1
    elif level == 5:
        z = 3 - z
    elif level == 6:
        x = x ^ 1
    else:
        x = 3 - x
    return flat_index(x, z, y, core)


def exchange(value, level):
    return lax.ppermute(value, AXES, [(flat, partner(level, flat)) for flat in range(128)])


def chain_index():
    run, seg = lax.axis_index("run"), lax.axis_index("seg")
    return seg * 16 + run


def bit(value, place):
    return lax.rem(lax.div(value, 1 << place), 2)


def own_stays(level):
    chain = chain_index()
    if level == LEVELS:
        return bit(chain, LEVELS - 1) == 0
    return bit(chain, level - 1) == bit(chain, level)


def nn(left, right, precision=None):
    return lax.dot_general(
        left, right, (((1,), (0,)), ((), ())), precision=precision, preferred_element_type=f32
    )


def nt(left, right, precision=None):
    return lax.dot_general(
        left, right, (((1,), (1,)), ((), ())), precision=precision, preferred_element_type=f32
    )


def split(value):
    upper = value.astype(bf16)
    return upper, (value - upper.astype(f32)).astype(bf16)


def three_pass(left, right):
    lh, ll = left
    rh, rl = right
    return nn(lh, rh) + (nn(lh, rl) + nn(ll, rh))


def inverse_into(matrix, out_ref, squarings=5):
    order = matrix.shape[0]
    rows = lax.broadcasted_iota(jnp.int32, (order, order), 0)
    identity = (rows == lax.broadcasted_iota(jnp.int32, (order, order), 1)).astype(f32)
    norm = jnp.max(jnp.sum(jnp.abs(matrix), axis=0, keepdims=True), axis=1, keepdims=True)
    scale = 1.75 / norm
    rest = identity - matrix * scale
    found = (identity + rest) * scale
    rest = rest.astype(bf16)
    rest = nn(rest, rest).astype(bf16)
    for step in range(1, squarings):
        found = found + nn(found.astype(bf16), rest)
        if step < squarings - 1:
            rest = nn(rest, rest).astype(bf16)
    upper = split(found)
    rest = identity - three_pass(split(matrix), upper)
    found = found + nn(upper[0], rest.astype(bf16))
    rest = identity - nn(matrix, found, HIGH)
    miss = jnp.sum(rest * rest)
    out_ref[...] = found + three_pass(split(found), split(rest))

    @pl.when(jnp.logical_not(miss < TOLERANCE * TOLERANCE))
    def _():
        near = jnp.logical_and(miss < 0.25, scale > 0.0)
        out_ref[...] = jnp.where(near, out_ref[...], identity * scale)

        def unfinished(state):
            step, miss_now = state
            return jnp.logical_and(step < 64, miss_now >= TOLERANCE * TOLERANCE)

        def improve(state):
            now = out_ref[...]
            gap = identity - nn(matrix, now, HIGH)
            out_ref[...] = now + nn(now, gap, HIGH)
            return state[0] + 1, jnp.sum(gap * gap)

        lax.while_loop(unfinished, improve, (jnp.int32(0), jnp.float32(jnp.inf)))


HALF = 128
PACKED = HALF + 8


def on_first_core():
    return lax.rem(lax.axis_index("run"), 2) == 0


def ordered(direct, swapped):
    first = on_first_core()
    return jnp.where(first, direct, swapped), jnp.where(first, swapped, direct)


def triangle():
    rows = lax.broadcasted_iota(jnp.int32, (HALF, HALF), 0)
    columns = lax.broadcasted_iota(jnp.int32, (HALF, HALF), 1)
    return rows, columns


def pack_symmetric(value, first):
    rows, columns = triangle()
    upper_left, lower_right = value[:HALF, :HALF], value[HALF:, HALF:]
    diagonal = jnp.sum(jnp.where(rows == columns, lower_right, 0.0), axis=0, keepdims=True)
    both = jnp.where(rows >= columns, upper_left, lower_right)
    main = jnp.where(first, value[HALF:, :HALF], both)
    return main, jnp.broadcast_to(diagonal, (8, HALF))


def unpack_symmetric(from_first, from_second):
    rows, columns = triangle()
    lower_left, diagonal = from_first[:HALF], from_first[HALF : HALF + 1]
    both = from_second[:HALF]
    turned = both.T
    upper_left = jnp.where(rows >= columns, both, turned)
    lower_right = jnp.where(rows < columns, both, turned)
    lower_right = jnp.where(rows == columns, diagonal, lower_right)
    return jnp.concatenate(
        [
            jnp.concatenate([upper_left, lower_left.T], axis=1),
            jnp.concatenate([lower_left, lower_right], axis=1),
        ],
        axis=0,
    )


def send_separator(value, send):
    main, diagonal = pack_symmetric(value, on_first_core())
    send[:HALF, :] = main
    send[HALF:, :] = diagonal


def send_link(link, outer, send):
    first = on_first_core()
    rows = jnp.where(first, link[:HALF], link[HALF:])
    send[:HALF, :] = rows[:, :HALF]
    send[HALF : 2 * HALF, :] = rows[:, HALF:]
    main, diagonal = pack_symmetric(outer, first)
    send[2 * HALF : 3 * HALF, :] = main
    send[3 * HALF :, :] = diagonal


def received_separator(refs):
    if len(refs) == 1:
        return refs[0][...]
    return unpack_symmetric(*ordered(refs[0][...], refs[1][...]))


def received_link(refs):
    if len(refs) == 1:
        order = refs[0].shape[1]
        return refs[0][:order, :], refs[0][order:, :]
    upper, lower = ordered(refs[0][...], refs[1][...])
    link = jnp.concatenate(
        [
            jnp.concatenate([upper[:HALF], upper[HALF : 2 * HALF]], axis=1),
            jnp.concatenate([lower[:HALF], lower[HALF : 2 * HALF]], axis=1),
        ],
        axis=0,
    )
    return link, unpack_symmetric(upper[2 * HALF :], lower[2 * HALF :])


def first_invert_kernel(diag, inv):
    inverse_into(diag[0], inv)


def first_merge_kernel(inv, diag, couple, gain_own, gain_other, ss, ps):
    order = inv.shape[0]
    start = chain_index() == 0
    above = jnp.where(start, 0.0, couple[0]).T
    below = couple[1]
    inverse = inv[...]
    gain_above = nn(above, inverse, HIGH)
    gain_below = nn(below, inverse, HIGH)
    own_above = -nt(gain_above, above, HIGH)
    own_below = diag[1] - nt(gain_below, below, HIGH)
    link = -nt(gain_above, below, HIGH)
    left = on_first_core()
    gain_own[...] = jnp.where(left, gain_above, gain_below)
    gain_other[...] = jnp.where(left, gain_below, gain_above)
    ss[...] = jnp.where(left, own_below, own_above)
    ps[order:, :] = jnp.where(left, own_above, own_below)
    ps[:order, :] = jnp.where(left, link, link.T)


def first_sources_kernel(source, inv, gain_own, gain_other, _, sources, partial):
    columns = partial.shape[1]
    held = source[0]
    left = on_first_core()
    sources[:, :columns] = jnp.where(left, 0.0, source[1]) - nn(gain_own[...], held, HIGH)
    sources[:, columns:] = jnp.where(left, source[1], 0.0) - nn(gain_other[...], held, HIGH)
    partial[...] = nn(inv[...], held, HIGH)


def first_factors_kernel(gain_own, gain_other, partial, _, factors, offset):
    order, columns = partial.shape
    rows = lax.broadcasted_iota(jnp.int32, (order, order), 0)
    identity = (rows == lax.broadcasted_iota(jnp.int32, (order, order), 1)).astype(f32)
    left = on_first_core()
    factors[0, :order, :] = gain_own[...].T
    factors[1, :order, :] = gain_other[...].T
    factors[0, order:, :] = jnp.where(left, 0.0, -identity)
    factors[1, order:, :] = jnp.where(left, -identity, 0.0)
    offset[:order, :] = partial[...]
    offset[order:, :] = jnp.zeros((order, columns), f32)


def invert_kernel(count, own_ss, _, *refs):
    inverse_into(own_ss[...] + received_separator(refs[:count]), refs[count])


def pass_kernel(_, arrived, passed):
    passed[...] = arrived[...]


def own_kernel(inv, own_ps, _, gain_own, reduced_own):
    order = inv.shape[0]
    link_own = own_ps[:order, :]
    gain_own[...] = nn(link_own, inv[...], HIGH)
    reduced_own[...] = own_ps[order:, :] - nt(gain_own[...], link_own, HIGH)


def merge_kernel(level, count, inv, gain_own, reduced_own, *refs):
    others, (gain_other, ss, ps, send_ss, send_ps) = refs[:count], refs[count:]
    order = inv.shape[0]
    stays = own_stays(level)
    link_other, outer_other = received_link(others)
    gain = nn(link_other, inv[...], HIGH)
    gain_other[...] = gain
    cross = -nt(gain_own[...], link_other, HIGH)
    reduced_other = outer_other - nt(gain, link_other, HIGH)
    own = reduced_own[...]
    separator = jnp.where(stays, reduced_other, own)
    outer = jnp.where(stays, own, reduced_other)
    link = jnp.where(stays, cross, cross.T)
    ss[...] = separator
    ps[order:, :] = outer
    ps[:order, :] = link
    send_separator(separator, send_ss)
    send_link(link, outer, send_ps)


def sources_step(level, inv, gain_own, gain_other, own_f, other_f):
    columns = own_f.shape[1] // 2
    stays = own_stays(level)
    own, other = own_f[...], other_f[...]
    held = own[:, columns:] + other[:, columns:]
    after_own = own[:, :columns] - nn(gain_own[...], held, HIGH)
    after_other = other[:, :columns] - nn(gain_other[...], held, HIGH)
    partial = nn(inv[...], held, HIGH)
    return jnp.where(stays, after_own, after_other), jnp.where(stays, after_other, after_own), partial


def sources_kernel(level, inv, gain_own, gain_other, own_f, other_f, _, sources, partial):
    columns = partial.shape[1]
    outer, inner, found = sources_step(level, inv, gain_own, gain_other, own_f, other_f)
    sources[:, :columns] = outer
    sources[:, columns:] = inner
    partial[...] = found


def factors_step(level, gain_own, gain_other, partial, factors, offset):
    stays = own_stays(level)
    inner = factors[1]
    new_offset = offset[...] - nn(inner, partial[...], HIGH)
    own_end = factors[0] - nt(inner, gain_own[...], HIGH)
    other_end = -nt(inner, gain_other[...], HIGH)
    return jnp.where(stays, own_end, other_end), jnp.where(stays, other_end, own_end), new_offset


def factors_kernel(level, gain_own, gain_other, partial, _, factors, offset, new_factors, new_offset):
    outer, inner, moved = factors_step(level, gain_own, gain_other, partial, factors, offset)
    new_factors[0] = outer
    new_factors[1] = inner
    new_offset[...] = moved


def end_kernel(ss, ps, end_inv, end_gain, new_ss, send_ss):
    order = ss.shape[0]
    rows = lax.broadcasted_iota(jnp.int32, (order, order), 0)
    identity = (rows == lax.broadcasted_iota(jnp.int32, (order, order), 1)).astype(f32)
    right = bit(chain_index(), LEVELS - 1) == 1
    inverse_into(jnp.where(right, ps[order:, :], identity), end_inv, 6)
    turned = ps[:order, :].T
    gain = nn(turned, end_inv[...], HIGH)
    end_gain[...] = gain
    separator = ss[...] - nt(gain, turned, HIGH)
    new_ss[...] = separator
    send_separator(separator, send_ss)


def end_sources_kernel(
    level, inv, gain_own, gain_other, own_f, other_f, end_inv, end_gain, _, sources, partial, end_partial
):
    outer, inner, found = sources_step(level, inv, gain_own, gain_other, own_f, other_f)
    sources[...] = inner - nn(end_gain[...], outer, HIGH)
    partial[...] = found
    end_partial[...] = nn(end_inv[...], outer, HIGH)


def end_factors_kernel(
    level, gain_own, gain_other, partial, _, factors, offset, end_gain, end_partial,
    new_factors, new_offset,
):
    outer, inner, moved = factors_step(level, gain_own, gain_other, partial, factors, offset)
    new_offset[...] = moved - nn(outer, end_partial[...], HIGH)
    new_factors[...] = inner - nt(outer, end_gain[...], HIGH)


def back_kernel(inv, own_f, other_f, factors, offset, result):
    order = inv.shape[0]
    middle = nn(inv[...], own_f[...] + other_f[...], HIGH)
    both = offset[...] - nn(factors[...], middle, HIGH)
    result[0] = both[:order]
    result[1] = both[order:]


def call(kernel, name, operands, shapes, flops):
    vmem = pl.BlockSpec(memory_space=pltpu.VMEM)
    return pl.pallas_call(
        kernel,
        out_shape=[jax.ShapeDtypeStruct(shape, f32) for shape in shapes],
        in_specs=[vmem] * len(operands),
        out_specs=[vmem] * len(shapes),
        name=name,
        compiler_params=pltpu.CompilerParams(vmem_limit_bytes=40 << 20),
        cost_estimate=pl.CostEstimate(flops=flops, bytes_accessed=4096, transcendentals=0),
    )(*operands)


MICRO = 1_000_000_000


def local(diag_blocks, coupling, rhs):
    order, columns = rhs.shape[2:]
    square, tall = (order, order), (2 * order, order)
    small, medium = (PACKED, HALF), (2 * HALF + PACKED, HALF)
    flat, slim = (order, 2 * columns), (order, columns)
    double, long = (2, 2 * order, order), (2 * order, columns)
    (inv,) = call(first_invert_kernel, "first_invert", (diag_blocks[0],), (square,), 4 * MICRO)
    gain_own, gain_other, ss, ps = call(
        first_merge_kernel, "first_merge", (inv, diag_blocks[0], coupling[0]),
        (square, square, square, tall), MICRO,
    )
    others_ss = (exchange(ss, 1),)
    others_ps = (exchange(ps, 1),)
    sources, partial = call(
        first_sources_kernel, "first_sources", (rhs[0], inv, gain_own, gain_other, ss),
        (flat, slim), MICRO // 2,
    )
    other_f = exchange(sources, 1)
    factors, offset = call(
        first_factors_kernel, "first_factors", (gain_own, gain_other, partial, ss),
        (double, long), MICRO // 2,
    )

    def swapped(direct, after, name):
        (passed,) = call(pass_kernel, name, (after, direct), (direct.shape,), MICRO // 20)
        return (direct, exchange(passed, 1))

    for level in range(1, LEVELS):
        last = level == LEVELS - 1
        (inv,) = call(
            functools.partial(invert_kernel, len(others_ss)), f"invert_{level}",
            (ss, offset) + others_ss, (square,), int(0.85 * MICRO),
        )
        if level > 1:
            others_ps = swapped(direct_ps, inv, f"pass_ps_{level}")
        gain_own, reduced_own = call(
            own_kernel, f"own_{level}", (inv, ps, others_ps[0]), (square, square), int(0.1 * MICRO)
        )
        gain_other, ss, ps, send_ss, send_ps = call(
            functools.partial(merge_kernel, level, len(others_ps)), f"merge_{level}",
            (inv, gain_own, reduced_own) + others_ps, (square, square, tall, small, medium), int(0.1 * MICRO),
        )
        if last:
            end_inv, end_gain, ss, send_ss = call(
                end_kernel, "end", (ss, ps), (square, square, square, small), 4 * MICRO
            )
        direct_ss = exchange(send_ss, level + 1)
        held = (inv, gain_own, gain_other, sources, other_f)
        if last:
            sources, partial, end_partial = call(
                functools.partial(end_sources_kernel, level), "end_sources",
                held + (end_inv, end_gain, send_ss), (slim, slim, slim), MICRO,
            )
        else:
            direct_ps = exchange(send_ps, level + 1)
            sources, partial = call(
                functools.partial(sources_kernel, level), f"sources_{level}",
                held + (send_ss,), (flat, slim), int(0.1 * MICRO),
            )
        other_f = exchange(sources, level + 1)
        before = (gain_own, gain_other, partial, send_ss, factors, offset)
        if last:
            factors, offset = call(
                functools.partial(end_factors_kernel, level), "end_factors",
                before + (end_gain, end_partial), (tall, long), 2 * MICRO,
            )
        else:
            factors, offset = call(
                functools.partial(factors_kernel, level), f"factors_{level}", before,
                (double, long), int(0.1 * MICRO),
            )
        others_ss = swapped(direct_ss, offset, f"pass_ss_{level + 1}")
    (inv,) = call(
        functools.partial(invert_kernel, 2), "last_invert", (ss, offset) + others_ss,
        (square,), 8 * MICRO,
    )
    (result,) = call(
        back_kernel, "back", (inv, sources, other_f, factors, offset), ((2, order, columns),), MICRO
    )
    return result[None]


def solution(mesh):
    spec = P("seg", "run", None, None)
    return jax.shard_map(
        local, mesh=mesh, in_specs=(spec, spec, spec), out_specs=spec, check_vma=False
    )
```

```python
import functools

import jax
import jax.numpy as jnp
from jax import lax
from jax.experimental import pallas as pl
from jax.experimental.pallas import tpu as pltpu
from jax.sharding import PartitionSpec as P

HIGH = lax.Precision.HIGHEST
f32 = jnp.float32
bf16 = jnp.bfloat16
LEVELS = 7
TOLERANCE = 4e-3
SQUARINGS = (5, 5, 4, 3, 3, 3, 3, 3)
AXES = ("run", "seg")


def chain_coords(flat):
    run, seg = flat >> 3, flat & 7
    return seg >> 1, ((seg & 1) << 1) | (run >> 3), (run >> 1) & 3, run & 1


def flat_index(x, z, y, core):
    return ((((z & 1) << 3) | (y << 1) | core) << 3) | (x << 1) | (z >> 1)


def partner(level, flat):
    x, z, y, core = chain_coords(flat)
    if level == 1:
        core = core ^ 1
    elif level == 2:
        y = y ^ 1
    elif level == 3:
        y = 3 - y
    elif level == 4:
        z = z ^ 1
    elif level == 5:
        z = 3 - z
    elif level == 6:
        x = x ^ 1
    else:
        x = 3 - x
    return flat_index(x, z, y, core)


def exchange(value, level):
    return lax.ppermute(value, AXES, [(flat, partner(level, flat)) for flat in range(128)])


def chain_index():
    run, seg = lax.axis_index("run"), lax.axis_index("seg")
    return seg * 16 + run


def bit(value, place):
    return lax.rem(lax.div(value, 1 << place), 2)


def own_stays(level):
    chain = chain_index()
    if level == LEVELS:
        return bit(chain, LEVELS - 1) == 0
    return bit(chain, level - 1) == bit(chain, level)


def nn(left, right, precision=None):
    return lax.dot_general(
        left, right, (((1,), (0,)), ((), ())), precision=precision, preferred_element_type=f32
    )


def nt(left, right, precision=None):
    return lax.dot_general(
        left, right, (((1,), (1,)), ((), ())), precision=precision, preferred_element_type=f32
    )


def split(value):
    upper = value.astype(bf16)
    return upper, (value - upper.astype(f32)).astype(bf16)


def three_pass(left, right, dot=nn):
    lh, ll = left
    rh, rl = right
    return dot(lh, rh) + (dot(lh, rl) + dot(ll, rh))


def inverse_into(matrix, out_ref, squarings=5):
    order = matrix.shape[0]
    rows = lax.broadcasted_iota(jnp.int32, (order, order), 0)
    identity = (rows == lax.broadcasted_iota(jnp.int32, (order, order), 1)).astype(f32)
    norm = jnp.max(jnp.sum(jnp.abs(matrix), axis=0, keepdims=True), axis=1, keepdims=True)
    scale = 1.75 / norm
    rest = identity - matrix * scale
    found = (identity + rest) * scale
    rest = rest.astype(bf16)
    rest = nn(rest, rest).astype(bf16)
    for step in range(1, squarings):
        found = found + nn(found.astype(bf16), rest)
        if step < squarings - 1:
            rest = nn(rest, rest).astype(bf16)
    upper = split(found)
    rest = identity - three_pass(split(matrix), upper)
    found = found + nn(upper[0], rest.astype(bf16))
    rest = identity - nn(matrix, found, HIGH)
    miss = jnp.sum(rest * rest)
    out_ref[...] = found + three_pass(split(found), split(rest))

    @pl.when(jnp.logical_not(miss < TOLERANCE * TOLERANCE))
    def _():
        near = jnp.logical_and(miss < 0.25, scale > 0.0)
        out_ref[...] = jnp.where(near, out_ref[...], identity * scale)

        def unfinished(state):
            step, miss_now = state
            return jnp.logical_and(step < 64, miss_now >= TOLERANCE * TOLERANCE)

        def improve(state):
            now = out_ref[...]
            gap = identity - nn(matrix, now, HIGH)
            out_ref[...] = now + nn(now, gap, HIGH)
            return state[0] + 1, jnp.sum(gap * gap)

        lax.while_loop(unfinished, improve, (jnp.int32(0), jnp.float32(jnp.inf)))


HALF = 128
PACKED = HALF + 8


def on_first_core():
    return lax.rem(lax.axis_index("run"), 2) == 0


def ordered(direct, swapped):
    first = on_first_core()
    return jnp.where(first, direct, swapped), jnp.where(first, swapped, direct)


def triangle():
    rows = lax.broadcasted_iota(jnp.int32, (HALF, HALF), 0)
    columns = lax.broadcasted_iota(jnp.int32, (HALF, HALF), 1)
    return rows, columns


def pack_symmetric(value, first):
    rows, columns = triangle()
    upper_left, lower_right = value[:HALF, :HALF], value[HALF:, HALF:]
    diagonal = jnp.sum(jnp.where(rows == columns, lower_right, 0.0), axis=0, keepdims=True)
    both = jnp.where(rows >= columns, upper_left, lower_right)
    lower_left = value[HALF:, :HALF]
    main = (lower_left if first else both) if isinstance(first, bool) else jnp.where(first, lower_left, both)
    return main, jnp.broadcast_to(diagonal, (8, HALF))


def unpack_symmetric(from_first, from_second):
    rows, columns = triangle()
    lower_left, diagonal = from_first[:HALF], from_first[HALF : HALF + 1]
    both = from_second[:HALF]
    turned = both.T
    upper_left = jnp.where(rows >= columns, both, turned)
    lower_right = jnp.where(rows < columns, both, turned)
    lower_right = jnp.where(rows == columns, diagonal, lower_right)
    return jnp.concatenate(
        [
            jnp.concatenate([upper_left, lower_left.T], axis=1),
            jnp.concatenate([lower_left, lower_right], axis=1),
        ],
        axis=0,
    )


def send_separator(value, send):
    main, diagonal = pack_symmetric(value, on_first_core())
    send[:HALF, :] = main
    send[HALF:, :] = diagonal


def send_link(link, outer, send):
    first = on_first_core()
    rows = jnp.where(first, link[:HALF], link[HALF:])
    send[:HALF, :] = rows[:, :HALF]
    send[HALF : 2 * HALF, :] = rows[:, HALF:]
    main, diagonal = pack_symmetric(outer, first)
    send[2 * HALF : 3 * HALF, :] = main
    send[3 * HALF :, :] = diagonal


def received_separator(refs):
    if len(refs) == 1:
        value = refs[0][...]
        return value if value.shape[1] > HALF else unpack_symmetric(value[:PACKED], value[PACKED:])
    return unpack_symmetric(*ordered(refs[0][...], refs[1][...]))


def received_link(refs):
    if len(refs) == 1:
        order = refs[0].shape[1]
        return refs[0][:order, :], refs[0][order:, :]
    upper, lower = ordered(refs[0][...], refs[1][...])
    link = jnp.concatenate(
        [
            jnp.concatenate([upper[:HALF], upper[HALF : 2 * HALF]], axis=1),
            jnp.concatenate([lower[:HALF], lower[HALF : 2 * HALF]], axis=1),
        ],
        axis=0,
    )
    return link, unpack_symmetric(upper[2 * HALF :], lower[2 * HALF :])


def first_invert_kernel(diag, inv):
    inverse_into(diag[0], inv)


def first_merge_kernel(inv, diag, couple, gain_own, gain_other, ss, ps):
    order = inv.shape[0]
    start = chain_index() == 0
    above = jnp.where(start, 0.0, couple[0]).T
    below = couple[1]
    inverse = inv[...]
    gain_above = nn(above, inverse, HIGH)
    gain_below = nn(below, inverse, HIGH)
    own_above = -nt(gain_above, above, HIGH)
    own_below = diag[1] - nt(gain_below, below, HIGH)
    link = -nt(gain_above, below, HIGH)
    left = on_first_core()
    gain_own[...] = jnp.where(left, gain_above, gain_below)
    gain_other[...] = jnp.where(left, gain_below, gain_above)
    ss[...] = jnp.where(left, own_below, own_above)
    ps[order:, :] = jnp.where(left, own_above, own_below)
    ps[:order, :] = jnp.where(left, link, link.T)


def first_sources_kernel(source, inv, gain_own, gain_other, _, sources, partial):
    columns = partial.shape[1]
    held = source[0]
    left = on_first_core()
    sources[:, :columns] = jnp.where(left, 0.0, source[1]) - nn(gain_own[...], held, HIGH)
    sources[:, columns:] = jnp.where(left, source[1], 0.0) - nn(gain_other[...], held, HIGH)
    partial[...] = nn(inv[...], held, HIGH)


def first_factors_kernel(gain_own, gain_other, partial, _, factors, offset):
    order, columns = partial.shape
    rows = lax.broadcasted_iota(jnp.int32, (order, order), 0)
    identity = (rows == lax.broadcasted_iota(jnp.int32, (order, order), 1)).astype(f32)
    left = on_first_core()
    factors[0, :order, :] = gain_own[...].T
    factors[1, :order, :] = gain_other[...].T
    factors[0, order:, :] = jnp.where(left, 0.0, -identity)
    factors[1, order:, :] = jnp.where(left, -identity, 0.0)
    offset[:order, :] = partial[...]
    offset[order:, :] = jnp.zeros((order, columns), f32)


def invert_kernel(squarings, own_ss, _, *refs):
    inverse_into(own_ss[...] + received_separator(refs[:-1]), refs[-1], squarings)


def pass_kernel(_, arrived, passed):
    passed[...] = arrived[...]


def own_kernel(inv, own_ps, _, gain_own, reduced_own):
    order = inv.shape[0]
    link_own = own_ps[:order, :]
    gain_own[...] = nn(link_own, inv[...], HIGH)
    reduced_own[...] = own_ps[order:, :] - nt(gain_own[...], link_own, HIGH)


def merge_kernel(level, count, inv, gain_own, reduced_own, *refs):
    others, (gain_other, ss, ps, *sends) = refs[:count], refs[count:]
    order = inv.shape[0]
    stays = own_stays(level)
    link_other, outer_other = received_link(others)
    gain = nn(link_other, inv[...], HIGH)
    gain_other[...] = gain
    cross = -nt(gain_own[...], link_other, HIGH)
    reduced_other = outer_other - nt(gain, link_other, HIGH)
    own = reduced_own[...]
    separator = jnp.where(stays, reduced_other, own)
    outer = jnp.where(stays, own, reduced_other)
    link = jnp.where(stays, cross, cross.T)
    ss[...] = separator
    ps[order:, :] = outer
    ps[:order, :] = link
    if sends:
        send_separator(separator, sends[0])
        send_link(link, outer, sends[1])


def sources_step(level, inv, gain_own, gain_other, own_f, other_f):
    columns = own_f.shape[1] // 2
    stays = own_stays(level)
    own, other = own_f[...], other_f[...]
    held = own[:, columns:] + other[:, columns:]
    after_own = own[:, :columns] - nn(gain_own[...], held, HIGH)
    after_other = other[:, :columns] - nn(gain_other[...], held, HIGH)
    partial = nn(inv[...], held, HIGH)
    return jnp.where(stays, after_own, after_other), jnp.where(stays, after_other, after_own), partial


def sources_kernel(level, inv, gain_own, gain_other, own_f, other_f, _, sources, partial):
    columns = partial.shape[1]
    outer, inner, found = sources_step(level, inv, gain_own, gain_other, own_f, other_f)
    sources[:, :columns] = outer
    sources[:, columns:] = inner
    partial[...] = found


def factors_step(level, gain_own, gain_other, partial, factors, offset):
    stays = own_stays(level)
    inner = split(factors[1])
    new_offset = offset[...] - three_pass(inner, split(partial[...]))
    own_end = factors[0] - three_pass(inner, split(gain_own[...]), nt)
    other_end = -three_pass(inner, split(gain_other[...]), nt)
    return jnp.where(stays, own_end, other_end), jnp.where(stays, other_end, own_end), new_offset


def factors_kernel(level, gain_own, gain_other, partial, _, factors, offset, new_factors, new_offset):
    outer, inner, moved = factors_step(level, gain_own, gain_other, partial, factors, offset)
    new_factors[0] = outer
    new_factors[1] = inner
    new_offset[...] = moved


def end_kernel(ss, ps, end_inv, end_gain, new_ss, send_ss):
    order = ss.shape[0]
    rows = lax.broadcasted_iota(jnp.int32, (order, order), 0)
    identity = (rows == lax.broadcasted_iota(jnp.int32, (order, order), 1)).astype(f32)
    right = bit(chain_index(), LEVELS - 1) == 1
    inverse_into(jnp.where(right, ps[order:, :], identity), end_inv, 6)
    turned = ps[:order, :].T
    gain = nn(turned, end_inv[...], HIGH)
    end_gain[...] = gain
    separator = ss[...] - nt(gain, turned, HIGH)
    new_ss[...] = separator
    for place, first in ((0, True), (PACKED, False)):
        main, diagonal = pack_symmetric(separator, first)
        send_ss[place : place + HALF, :] = main
        send_ss[place + HALF : place + PACKED, :] = diagonal


def end_sources_kernel(
    level, inv, gain_own, gain_other, own_f, other_f, end_inv, end_gain, _, sources, partial, end_partial
):
    outer, inner, found = sources_step(level, inv, gain_own, gain_other, own_f, other_f)
    sources[...] = inner - nn(end_gain[...], outer, HIGH)
    partial[...] = found
    end_partial[...] = nn(end_inv[...], outer, HIGH)


def end_factors_kernel(
    level, gain_own, gain_other, partial, _, factors, offset, end_gain, end_partial,
    new_factors, new_offset,
):
    outer, inner, moved = factors_step(level, gain_own, gain_other, partial, factors, offset)
    outer = split(outer)
    new_offset[...] = moved - three_pass(outer, split(end_partial[...]))
    new_factors[...] = inner - three_pass(outer, split(end_gain[...]), nt)


def back_kernel(inv, own_f, other_f, factors, offset, result):
    order = inv.shape[0]
    middle = nn(inv[...], own_f[...] + other_f[...], HIGH)
    both = offset[...] - three_pass(split(factors[...]), split(middle))
    result[0] = both[:order]
    result[1] = both[order:]


WEIGHTS = {"invert": 0.85, "own": 0.1, "merge": 0.1, "sources": 0.3, "factors": 0.1, "pass": 0.05, "end": 4.0, "tail": 0.1, "last": 0.1, "first": 2.0}


def call(kernel, name, operands, shapes):
    vmem = pl.BlockSpec(memory_space=pltpu.VMEM)
    flops = int(WEIGHTS[name.split("_")[0]] * 1e9)
    return pl.pallas_call(
        kernel,
        out_shape=[jax.ShapeDtypeStruct(shape, f32) for shape in shapes],
        in_specs=[vmem] * len(operands),
        out_specs=[vmem] * len(shapes),
        name=name,
        compiler_params=pltpu.CompilerParams(vmem_limit_bytes=40 << 20),
        cost_estimate=pl.CostEstimate(flops=flops, bytes_accessed=4096, transcendentals=0),
    )(*operands)


def local(diag_blocks, coupling, rhs):
    order, columns = rhs.shape[2:]
    square, tall = (order, order), (2 * order, order)
    small, medium = (PACKED, HALF), (2 * HALF + PACKED, HALF)
    flat, slim = (order, 2 * columns), (order, columns)
    double, long = (2, 2 * order, order), (2 * order, columns)
    (inv,) = call(first_invert_kernel, "first_invert", (diag_blocks[0],), (square,))
    gain_own, gain_other, ss, ps = call(
        first_merge_kernel, "first_merge", (inv, diag_blocks[0], coupling[0]),
        (square, square, square, tall)
    )
    others_ss = (exchange(ss, 1),)
    others_ps = (exchange(ps, 1),)
    sources, partial = call(
        first_sources_kernel, "first_sources", (rhs[0], inv, gain_own, gain_other, ss),
        (flat, slim)
    )
    other_f = exchange(sources, 1)
    factors, offset = call(
        first_factors_kernel, "first_factors", (gain_own, gain_other, partial, ss),
        (double, long)
    )

    def swapped(direct, after, name):
        (passed,) = call(pass_kernel, name, (after, direct), (direct.shape,))
        return (direct, exchange(passed, 1))

    for level in range(1, LEVELS):
        last = level == LEVELS - 1
        (inv,) = call(
            functools.partial(invert_kernel, SQUARINGS[level]), f"invert_{level}",
            (ss, offset) + others_ss, (square,)
        )
        if level > 1:
            others_ps = swapped(direct_ps, inv, f"pass_ps_{level}")
        gain_own, reduced_own = call(
            own_kernel, f"own_{level}", (inv, ps, others_ps[0]), (square, square)
        )
        gain_other, ss, ps, *sends = call(
            functools.partial(merge_kernel, level, len(others_ps)), f"merge_{level}",
            (inv, gain_own, reduced_own) + others_ps, (square, square, tall) + (() if last else (small, medium)),
        )
        if last:
            end_inv, end_gain, ss, send_ss = call(
                end_kernel, "end", (ss, ps), (square, square, square, (2 * PACKED, HALF))
            )
        else:
            send_ss, send_ps = sends
        direct_ss = exchange(send_ss, level + 1)
        held = (inv, gain_own, gain_other, sources, other_f)
        if last:
            sources, partial, end_partial = call(
                functools.partial(end_sources_kernel, level), "tail_sources",
                held + (end_inv, end_gain, send_ss), (slim, slim, slim)
            )
        else:
            direct_ps = exchange(send_ps, level + 1)
            sources, partial = call(
                functools.partial(sources_kernel, level), f"sources_{level}",
                held + (send_ss,), (flat, slim)
            )
        other_f = exchange(sources, level + 1)
        before = (gain_own, gain_other, partial, send_ss, factors, offset)
        if last:
            factors, offset = call(
                functools.partial(end_factors_kernel, level), "tail_factors",
                before + (end_gain, end_partial), (tall, long)
            )
        else:
            factors, offset = call(
                functools.partial(factors_kernel, level), f"factors_{level}", before,
                (double, long)
            )
        others_ss = (direct_ss,) if last else swapped(direct_ss, offset, f"pass_ss_{level + 1}")
    (inv,) = call(
        functools.partial(invert_kernel, SQUARINGS[LEVELS]), "last_invert", (ss, offset) + others_ss,
        (square,)
    )
    (result,) = call(
        back_kernel, "tail_back", (inv, sources, other_f, factors, offset), ((2, order, columns),)
    )
    return result[None]


def solution(mesh):
    spec = P("seg", "run", None, None)
    return jax.shard_map(
        local, mesh=mesh, in_specs=(spec, spec, spec), out_specs=spec, check_vma=False
    )
```

```python
import functools

import jax
import jax.numpy as jnp
from jax import lax
from jax.experimental import pallas as pl
from jax.experimental.pallas import tpu as pltpu
from jax.sharding import PartitionSpec as P

HIGH = lax.Precision.HIGHEST
f32 = jnp.float32
bf16 = jnp.bfloat16
LEVELS = 7
TOLERANCE = 4e-3
SQUARINGS = (5, 4, 4, 3, 2, 2, 2, 2)
AXES = ("run", "seg")


def chain_coords(flat):
    run, seg = flat >> 3, flat & 7
    return seg >> 1, ((seg & 1) << 1) | (run >> 3), (run >> 1) & 3, run & 1


def flat_index(x, z, y, core):
    return ((((z & 1) << 3) | (y << 1) | core) << 3) | (x << 1) | (z >> 1)


def partner(level, flat):
    x, z, y, core = chain_coords(flat)
    if level == 1:
        core = core ^ 1
    elif level == 2:
        y = y ^ 1
    elif level == 3:
        y = 3 - y
    elif level == 4:
        z = z ^ 1
    elif level == 5:
        z = 3 - z
    elif level == 6:
        x = x ^ 1
    else:
        x = 3 - x
    return flat_index(x, z, y, core)


def exchange(value, level):
    return lax.ppermute(value, AXES, [(flat, partner(level, flat)) for flat in range(128)])


def chain_index():
    run, seg = lax.axis_index("run"), lax.axis_index("seg")
    return seg * 16 + run


def bit(value, place):
    return lax.rem(lax.div(value, 1 << place), 2)


def own_stays(level):
    chain = chain_index()
    if level == LEVELS:
        return bit(chain, LEVELS - 1) == 0
    return bit(chain, level - 1) == bit(chain, level)


def nn(left, right, precision=None):
    return lax.dot_general(
        left, right, (((1,), (0,)), ((), ())), precision=precision, preferred_element_type=f32
    )


def nt(left, right, precision=None):
    return lax.dot_general(
        left, right, (((1,), (1,)), ((), ())), precision=precision, preferred_element_type=f32
    )


def split(value):
    upper = value.astype(bf16)
    return upper, (value - upper.astype(f32)).astype(bf16)


def three_pass(left, right, dot=nn):
    lh, ll = left
    rh, rl = right
    return dot(lh, rh) + (dot(lh, rl) + dot(ll, rh))


def inverse_into(matrix, out_ref, squarings=5):
    order = matrix.shape[0]
    rows = lax.broadcasted_iota(jnp.int32, (order, order), 0)
    identity = (rows == lax.broadcasted_iota(jnp.int32, (order, order), 1)).astype(f32)
    norm = jnp.max(jnp.sum(jnp.abs(matrix), axis=0, keepdims=True), axis=1, keepdims=True)
    scale = 1.75 / norm
    rest = identity - matrix * scale
    found = (identity + rest) * scale
    rest = rest.astype(bf16)
    rest = nn(rest, rest).astype(bf16)
    for step in range(1, squarings):
        found = found + nn(found.astype(bf16), rest)
        if step < squarings - 1:
            rest = nn(rest, rest).astype(bf16)
    upper = split(found)
    rest = identity - three_pass(split(matrix), upper)
    found = found + nn(upper[0], rest.astype(bf16))
    rest = identity - nn(matrix, found, HIGH)
    miss = jnp.sum(rest * rest)
    out_ref[...] = found + three_pass(split(found), split(rest))

    @pl.when(jnp.logical_not(miss < TOLERANCE * TOLERANCE))
    def _():
        near = jnp.logical_and(miss < 0.25, scale > 0.0)
        out_ref[...] = jnp.where(near, out_ref[...], identity * scale)

        def unfinished(state):
            step, miss_now = state
            return jnp.logical_and(step < 64, miss_now >= TOLERANCE * TOLERANCE)

        def improve(state):
            now = out_ref[...]
            gap = identity - nn(matrix, now, HIGH)
            out_ref[...] = now + nn(now, gap, HIGH)
            return state[0] + 1, jnp.sum(gap * gap)

        lax.while_loop(unfinished, improve, (jnp.int32(0), jnp.float32(jnp.inf)))


HALF = 128
PACKED = HALF + 8


def on_first_core():
    return lax.rem(lax.axis_index("run"), 2) == 0


def ordered(direct, swapped):
    first = on_first_core()
    return jnp.where(first, direct, swapped), jnp.where(first, swapped, direct)


def triangle():
    rows = lax.broadcasted_iota(jnp.int32, (HALF, HALF), 0)
    columns = lax.broadcasted_iota(jnp.int32, (HALF, HALF), 1)
    return rows, columns


def pack_symmetric(value, first):
    rows, columns = triangle()
    upper_left, lower_right = value[:HALF, :HALF], value[HALF:, HALF:]
    diagonal = jnp.sum(jnp.where(rows == columns, lower_right, 0.0), axis=0, keepdims=True)
    both = jnp.where(rows >= columns, upper_left, lower_right)
    lower_left = value[HALF:, :HALF]
    main = (lower_left if first else both) if isinstance(first, bool) else jnp.where(first, lower_left, both)
    return main, jnp.broadcast_to(diagonal, (8, HALF))


def unpack_symmetric(from_first, from_second):
    rows, columns = triangle()
    lower_left, diagonal = from_first[:HALF], from_first[HALF : HALF + 1]
    both = from_second[:HALF]
    turned = both.T
    upper_left = jnp.where(rows >= columns, both, turned)
    lower_right = jnp.where(rows < columns, both, turned)
    lower_right = jnp.where(rows == columns, diagonal, lower_right)
    return jnp.concatenate(
        [
            jnp.concatenate([upper_left, lower_left.T], axis=1),
            jnp.concatenate([lower_left, lower_right], axis=1),
        ],
        axis=0,
    )


def send_separator(value, send):
    main, diagonal = pack_symmetric(value, on_first_core())
    send[:HALF, :] = main
    send[HALF:, :] = diagonal


def send_link(link, outer, send):
    first = on_first_core()
    rows = jnp.where(first, link[:HALF], link[HALF:])
    send[:HALF, :] = rows[:, :HALF]
    send[HALF : 2 * HALF, :] = rows[:, HALF:]
    main, diagonal = pack_symmetric(outer, first)
    send[2 * HALF : 3 * HALF, :] = main
    send[3 * HALF :, :] = diagonal


def received_separator(refs):
    if len(refs) == 1:
        value = refs[0][...]
        return value if value.shape[1] > HALF else unpack_symmetric(value[:PACKED], value[PACKED:])
    return unpack_symmetric(*ordered(refs[0][...], refs[1][...]))


def received_link(refs):
    if len(refs) == 1:
        order = refs[0].shape[1]
        return refs[0][:order, :], refs[0][order:, :]
    upper, lower = ordered(refs[0][...], refs[1][...])
    link = jnp.concatenate(
        [
            jnp.concatenate([upper[:HALF], upper[HALF : 2 * HALF]], axis=1),
            jnp.concatenate([lower[:HALF], lower[HALF : 2 * HALF]], axis=1),
        ],
        axis=0,
    )
    return link, unpack_symmetric(upper[2 * HALF :], lower[2 * HALF :])


def first_invert_kernel(diag, inv):
    inverse_into(diag[0], inv)


def first_merge_kernel(inv, diag, couple, gain_own, gain_other, ss, ps):
    order = inv.shape[0]
    start = chain_index() == 0
    above = jnp.where(start, 0.0, couple[0]).T
    below = couple[1]
    inverse = inv[...]
    gain_above = nn(above, inverse, HIGH)
    gain_below = nn(below, inverse, HIGH)
    own_above = -nt(gain_above, above, HIGH)
    own_below = diag[1] - nt(gain_below, below, HIGH)
    link = -nt(gain_above, below, HIGH)
    left = on_first_core()
    gain_own[...] = jnp.where(left, gain_above, gain_below)
    gain_other[...] = jnp.where(left, gain_below, gain_above)
    ss[...] = jnp.where(left, own_below, own_above)
    ps[order:, :] = jnp.where(left, own_above, own_below)
    ps[:order, :] = jnp.where(left, link, link.T)


def first_sources_kernel(source, inv, gain_own, gain_other, _, sources, partial):
    columns = partial.shape[1]
    held = source[0]
    left = on_first_core()
    sources[:, :columns] = jnp.where(left, 0.0, source[1]) - nn(gain_own[...], held, HIGH)
    sources[:, columns:] = jnp.where(left, source[1], 0.0) - nn(gain_other[...], held, HIGH)
    partial[...] = nn(inv[...], held, HIGH)


def first_factors_kernel(gain_own, gain_other, partial, _, factors, offset):
    order, columns = partial.shape
    rows = lax.broadcasted_iota(jnp.int32, (order, order), 0)
    identity = (rows == lax.broadcasted_iota(jnp.int32, (order, order), 1)).astype(f32)
    left = on_first_core()
    factors[0, :order, :] = gain_own[...].T
    factors[1, :order, :] = gain_other[...].T
    factors[0, order:, :] = jnp.where(left, 0.0, -identity)
    factors[1, order:, :] = jnp.where(left, -identity, 0.0)
    offset[:order, :] = partial[...]
    offset[order:, :] = jnp.zeros((order, columns), f32)


def invert_kernel(squarings, own_ss, _, *refs):
    inverse_into(own_ss[...] + received_separator(refs[:-1]), refs[-1], squarings)


def store_element(stays, own, other, cross, ss, ps, sends):
    order = cross.shape[0]
    separator = jnp.where(stays, other, own)
    outer = jnp.where(stays, own, other)
    link = jnp.where(stays, cross, cross.T)
    ss[...] = separator
    ps[order:, :] = outer
    ps[:order, :] = link
    if sends:
        send_separator(separator, sends[0])
        send_link(link, outer, sends[1])


def pair_kernel(level, inv, own_ps, other_ps, gain_own, gain_other, ss, ps, *sends):
    order = inv.shape[0]
    stays = own_stays(level)
    inverse = inv[...]
    link_own, link_other = own_ps[:order, :], other_ps[:order, :]
    own_gain = nn(link_own, inverse, HIGH)
    other_gain = nn(link_other, inverse, HIGH)
    gain_own[...] = own_gain
    gain_other[...] = other_gain
    own = own_ps[order:, :] - nt(own_gain, link_own, HIGH)
    other = other_ps[order:, :] - nt(other_gain, link_other, HIGH)
    cross = -nt(own_gain, link_other, HIGH)
    store_element(stays, own, other, cross, ss, ps, sends)


def pass_kernel(_, arrived, passed):
    passed[...] = arrived[...]


def own_kernel(inv, own_ps, _, gain_own, reduced_own):
    order = inv.shape[0]
    link_own = own_ps[:order, :]
    gain_own[...] = nn(link_own, inv[...], HIGH)
    reduced_own[...] = own_ps[order:, :] - nt(gain_own[...], link_own, HIGH)


def merge_kernel(level, count, inv, gain_own, reduced_own, *refs):
    others, (gain_other, ss, ps, *sends) = refs[:count], refs[count:]
    order = inv.shape[0]
    stays = own_stays(level)
    link_other, outer_other = received_link(others)
    gain = nn(link_other, inv[...], HIGH)
    gain_other[...] = gain
    cross = -nt(gain_own[...], link_other, HIGH)
    reduced_other = outer_other - nt(gain, link_other, HIGH)
    store_element(stays, reduced_own[...], reduced_other, cross, ss, ps, sends)


def sources_step(level, inv, gain_own, gain_other, own_f, other_f):
    columns = own_f.shape[1] // 2
    stays = own_stays(level)
    own, other = own_f[...], other_f[...]
    held = own[:, columns:] + other[:, columns:]
    after_own = own[:, :columns] - nn(gain_own[...], held, HIGH)
    after_other = other[:, :columns] - nn(gain_other[...], held, HIGH)
    partial = nn(inv[...], held, HIGH)
    return jnp.where(stays, after_own, after_other), jnp.where(stays, after_other, after_own), partial


def sources_kernel(level, inv, gain_own, gain_other, own_f, other_f, _, sources, partial):
    columns = partial.shape[1]
    outer, inner, found = sources_step(level, inv, gain_own, gain_other, own_f, other_f)
    sources[:, :columns] = outer
    sources[:, columns:] = inner
    partial[...] = found


def factors_step(level, gain_own, gain_other, partial, factors, offset):
    stays = own_stays(level)
    inner = split(factors[1])
    new_offset = offset[...] - three_pass(inner, split(partial[...]))
    own_end = factors[0] - three_pass(inner, split(gain_own[...]), nt)
    other_end = -three_pass(inner, split(gain_other[...]), nt)
    return jnp.where(stays, own_end, other_end), jnp.where(stays, other_end, own_end), new_offset


def factors_kernel(level, gain_own, gain_other, partial, _, factors, offset, new_factors, new_offset):
    outer, inner, moved = factors_step(level, gain_own, gain_other, partial, factors, offset)
    new_factors[0] = outer
    new_factors[1] = inner
    new_offset[...] = moved


def end_kernel(ss, ps, end_inv, end_gain, new_ss, send_ss):
    order = ss.shape[0]
    rows = lax.broadcasted_iota(jnp.int32, (order, order), 0)
    identity = (rows == lax.broadcasted_iota(jnp.int32, (order, order), 1)).astype(f32)
    right = bit(chain_index(), LEVELS - 1) == 1
    inverse_into(jnp.where(right, ps[order:, :], identity), end_inv, 6)
    turned = ps[:order, :].T
    gain = nn(turned, end_inv[...], HIGH)
    end_gain[...] = gain
    separator = ss[...] - nt(gain, turned, HIGH)
    new_ss[...] = separator
    for place, first in ((0, True), (PACKED, False)):
        main, diagonal = pack_symmetric(separator, first)
        send_ss[place : place + HALF, :] = main
        send_ss[place + HALF : place + PACKED, :] = diagonal


def end_sources_kernel(
    level, inv, gain_own, gain_other, own_f, other_f, end_inv, end_gain, _, sources, partial, end_partial
):
    outer, inner, found = sources_step(level, inv, gain_own, gain_other, own_f, other_f)
    sources[...] = inner - nn(end_gain[...], outer, HIGH)
    partial[...] = found
    end_partial[...] = nn(end_inv[...], outer, HIGH)


def end_factors_kernel(
    level, gain_own, gain_other, partial, _, factors, offset, end_gain, end_partial,
    new_factors, new_offset,
):
    outer, inner, moved = factors_step(level, gain_own, gain_other, partial, factors, offset)
    outer = split(outer)
    new_offset[...] = moved - three_pass(outer, split(end_partial[...]))
    new_factors[...] = inner - three_pass(outer, split(end_gain[...]), nt)


def back_kernel(inv, own_f, other_f, factors, offset, result):
    order = inv.shape[0]
    middle = nn(inv[...], own_f[...] + other_f[...], HIGH)
    both = offset[...] - three_pass(split(factors[...]), split(middle))
    result[0] = both[:order]
    result[1] = both[order:]


WEIGHTS = {"invert": 0.85, "own": 0.1, "merge": 0.1, "sources": 0.3, "factors": 0.1, "pass": 0.05, "end": 4.0, "tail": 0.1, "last": 0.1, "first": 2.0}


def call(kernel, name, operands, shapes):
    vmem = pl.BlockSpec(memory_space=pltpu.VMEM)
    flops = int(WEIGHTS[name.split("_")[0]] * 1e9)
    return pl.pallas_call(
        kernel,
        out_shape=[jax.ShapeDtypeStruct(shape, f32) for shape in shapes],
        in_specs=[vmem] * len(operands),
        out_specs=[vmem] * len(shapes),
        name=name,
        compiler_params=pltpu.CompilerParams(vmem_limit_bytes=40 << 20),
        cost_estimate=pl.CostEstimate(flops=flops, bytes_accessed=4096, transcendentals=0),
    )(*operands)


def local(diag_blocks, coupling, rhs):
    order, columns = rhs.shape[2:]
    square, tall = (order, order), (2 * order, order)
    small, medium = (PACKED, HALF), (2 * HALF + PACKED, HALF)
    flat, slim = (order, 2 * columns), (order, columns)
    double, long = (2, 2 * order, order), (2 * order, columns)
    (inv,) = call(first_invert_kernel, "first_invert", (diag_blocks[0],), (square,))
    gain_own, gain_other, ss, ps = call(
        first_merge_kernel, "first_merge", (inv, diag_blocks[0], coupling[0]),
        (square, square, square, tall)
    )
    others_ss = (exchange(ss, 1),)
    others_ps = (exchange(ps, 1),)
    sources, partial = call(
        first_sources_kernel, "first_sources", (rhs[0], inv, gain_own, gain_other, ss),
        (flat, slim)
    )
    other_f = exchange(sources, 1)
    factors, offset = call(
        first_factors_kernel, "first_factors", (gain_own, gain_other, partial, ss),
        (double, long)
    )

    def swapped(direct, after, name):
        (passed,) = call(pass_kernel, name, (after, direct), (direct.shape,))
        return (direct, exchange(passed, 1))

    for level in range(1, LEVELS):
        last = level == LEVELS - 1
        (inv,) = call(
            functools.partial(invert_kernel, SQUARINGS[level]), f"invert_{level}",
            (ss, offset) + others_ss, (square,)
        )
        if level > 1:
            others_ps = swapped(direct_ps, inv, f"pass_ps_{level}")
            gain_own, reduced_own = call(
                own_kernel, f"own_{level}", (inv, ps, others_ps[0]), (square, square)
            )
            gain_other, ss, ps, *sends = call(
                functools.partial(merge_kernel, level, len(others_ps)), f"merge_{level}",
                (inv, gain_own, reduced_own) + others_ps,
                (square, square, tall) + (() if last else (small, medium)),
            )
        else:
            gain_own, gain_other, ss, ps, *sends = call(
                functools.partial(pair_kernel, level), f"merge_{level}", (inv, ps) + others_ps,
                (square, square, square, tall, small, medium),
            )
        if last:
            end_inv, end_gain, ss, send_ss = call(
                end_kernel, "end", (ss, ps), (square, square, square, (2 * PACKED, HALF))
            )
        else:
            send_ss, send_ps = sends
        direct_ss = exchange(send_ss, level + 1)
        held = (inv, gain_own, gain_other, sources, other_f)
        if last:
            sources, partial, end_partial = call(
                functools.partial(end_sources_kernel, level), "tail_sources",
                held + (end_inv, end_gain, send_ss), (slim, slim, slim)
            )
        else:
            direct_ps = exchange(send_ps, level + 1)
            sources, partial = call(
                functools.partial(sources_kernel, level), f"sources_{level}",
                held + (send_ss,), (flat, slim)
            )
        other_f = exchange(sources, level + 1)
        before = (gain_own, gain_other, partial, send_ss, factors, offset)
        if last:
            factors, offset = call(
                functools.partial(end_factors_kernel, level), "tail_factors",
                before + (end_gain, end_partial), (tall, long)
            )
        else:
            factors, offset = call(
                functools.partial(factors_kernel, level), f"factors_{level}", before,
                (double, long)
            )
        others_ss = (direct_ss,) if last else swapped(direct_ss, offset, f"pass_ss_{level + 1}")
    (inv,) = call(
        functools.partial(invert_kernel, SQUARINGS[LEVELS]), "last_invert", (ss, offset) + others_ss,
        (square,)
    )
    (result,) = call(
        back_kernel, "tail_back", (inv, sources, other_f, factors, offset), ((2, order, columns),)
    )
    return result[None]


def solution(mesh):
    spec = P("seg", "run", None, None)
    return jax.shard_map(
        local, mesh=mesh, in_specs=(spec, spec, spec), out_specs=spec, check_vma=False
    )
```

```python
import functools

import jax
import jax.numpy as jnp
from jax import lax
from jax.experimental import pallas as pl
from jax.experimental.pallas import tpu as pltpu
from jax.sharding import PartitionSpec as P

HIGH = lax.Precision.HIGHEST
f32 = jnp.float32
bf16 = jnp.bfloat16
LEVELS = 7
TOLERANCE = 4e-3
SQUARINGS = (5, 4, 4, 3, 2, 2, 2, 2)
AXES = ("run", "seg")


def chain_coords(flat):
    run, seg = flat >> 3, flat & 7
    return seg >> 1, ((seg & 1) << 1) | (run >> 3), (run >> 1) & 3, run & 1


def flat_index(x, z, y, core):
    return ((((z & 1) << 3) | (y << 1) | core) << 3) | (x << 1) | (z >> 1)


def partner(level, flat):
    x, z, y, core = chain_coords(flat)
    if level == 1:
        core = core ^ 1
    elif level == 2:
        y = y ^ 1
    elif level == 3:
        y = 3 - y
    elif level == 4:
        z = z ^ 1
    elif level == 5:
        z = 3 - z
    elif level == 6:
        x = x ^ 1
    else:
        x = 3 - x
    return flat_index(x, z, y, core)


def exchange(value, level):
    return lax.ppermute(value, AXES, [(flat, partner(level, flat)) for flat in range(128)])


def chain_index():
    run, seg = lax.axis_index("run"), lax.axis_index("seg")
    return seg * 16 + run


def bit(value, place):
    return lax.rem(lax.div(value, 1 << place), 2)


def own_stays(level):
    chain = chain_index()
    if level == LEVELS:
        return bit(chain, LEVELS - 1) == 0
    return bit(chain, level - 1) == bit(chain, level)


def nn(left, right, precision=None):
    return lax.dot_general(
        left, right, (((1,), (0,)), ((), ())), precision=precision, preferred_element_type=f32
    )


def nt(left, right, precision=None):
    return lax.dot_general(
        left, right, (((1,), (1,)), ((), ())), precision=precision, preferred_element_type=f32
    )


def split(value):
    upper = value.astype(bf16)
    return upper, (value - upper.astype(f32)).astype(bf16)


def three_pass(left, right, dot=nn):
    lh, ll = left
    rh, rl = right
    return dot(lh, rh) + (dot(lh, rl) + dot(ll, rh))


def inverse_into(matrix, out_ref, squarings=5):
    order = matrix.shape[0]
    rows = lax.broadcasted_iota(jnp.int32, (order, order), 0)
    identity = (rows == lax.broadcasted_iota(jnp.int32, (order, order), 1)).astype(f32)
    norm = jnp.max(jnp.sum(jnp.abs(matrix), axis=0, keepdims=True), axis=1, keepdims=True)
    scale = 1.75 / norm
    rest = identity - matrix * scale
    found = (identity + rest) * scale
    rest = rest.astype(bf16)
    rest = nn(rest, rest).astype(bf16)
    for step in range(1, squarings):
        found = found + nn(found.astype(bf16), rest)
        if step < squarings - 1:
            rest = nn(rest, rest).astype(bf16)
    upper = split(found)
    rest = identity - three_pass(split(matrix), upper)
    found = found + nn(upper[0], rest.astype(bf16))
    rest = identity - nn(matrix, found, HIGH)
    miss = jnp.sum(rest * rest)
    out_ref[...] = found + three_pass(split(found), split(rest))

    @pl.when(jnp.logical_not(miss < TOLERANCE * TOLERANCE))
    def _():
        near = jnp.logical_and(miss < 0.25, scale > 0.0)
        out_ref[...] = jnp.where(near, out_ref[...], identity * scale)

        def unfinished(state):
            step, miss_now = state
            return jnp.logical_and(step < 64, miss_now >= TOLERANCE * TOLERANCE)

        def improve(state):
            now = out_ref[...]
            gap = identity - nn(matrix, now, HIGH)
            out_ref[...] = now + nn(now, gap, HIGH)
            return state[0] + 1, jnp.sum(gap * gap)

        lax.while_loop(unfinished, improve, (jnp.int32(0), jnp.float32(jnp.inf)))


HALF = 128
PACKED = HALF + 8


def on_first_core():
    return lax.rem(lax.axis_index("run"), 2) == 0


def ordered(direct, swapped):
    first = on_first_core()
    return jnp.where(first, direct, swapped), jnp.where(first, swapped, direct)


def triangle():
    rows = lax.broadcasted_iota(jnp.int32, (HALF, HALF), 0)
    columns = lax.broadcasted_iota(jnp.int32, (HALF, HALF), 1)
    return rows, columns


def pack_symmetric(value, first):
    rows, columns = triangle()
    upper_left, lower_right = value[:HALF, :HALF], value[HALF:, HALF:]
    diagonal = jnp.sum(jnp.where(rows == columns, lower_right, 0.0), axis=0, keepdims=True)
    both = jnp.where(rows >= columns, upper_left, lower_right)
    lower_left = value[HALF:, :HALF]
    main = (lower_left if first else both) if isinstance(first, bool) else jnp.where(first, lower_left, both)
    return main, jnp.broadcast_to(diagonal, (8, HALF))


def unpack_symmetric(from_first, from_second):
    rows, columns = triangle()
    lower_left, diagonal = from_first[:HALF], from_first[HALF : HALF + 1]
    both = from_second[:HALF]
    turned = both.T
    upper_left = jnp.where(rows >= columns, both, turned)
    lower_right = jnp.where(rows < columns, both, turned)
    lower_right = jnp.where(rows == columns, diagonal, lower_right)
    return jnp.concatenate(
        [
            jnp.concatenate([upper_left, lower_left.T], axis=1),
            jnp.concatenate([lower_left, lower_right], axis=1),
        ],
        axis=0,
    )


def send_separator(value, send):
    for place, first in ((0, True), (PACKED, False)):
        main, diagonal = pack_symmetric(value, first)
        send[place : place + HALF, :] = main
        send[place + HALF : place + PACKED, :] = diagonal


def send_link(link, outer, send):
    first = on_first_core()
    rows = jnp.where(first, link[:HALF], link[HALF:])
    send[:HALF, :] = rows[:, :HALF]
    send[HALF : 2 * HALF, :] = rows[:, HALF:]
    main, diagonal = pack_symmetric(outer, first)
    send[2 * HALF : 3 * HALF, :] = main
    send[3 * HALF :, :] = diagonal


def received_separator(ref):
    value = ref[...]
    return value if value.shape[1] > HALF else unpack_symmetric(value[:PACKED], value[PACKED:])


def received_link(refs):
    upper, lower = ordered(refs[0][...], refs[1][...])
    link = jnp.concatenate(
        [
            jnp.concatenate([upper[:HALF], upper[HALF : 2 * HALF]], axis=1),
            jnp.concatenate([lower[:HALF], lower[HALF : 2 * HALF]], axis=1),
        ],
        axis=0,
    )
    return link, unpack_symmetric(upper[2 * HALF :], lower[2 * HALF :])


def first_invert_kernel(diag, inv):
    inverse_into(diag[0], inv)


def first_merge_kernel(inv, diag, couple, gain_own, gain_other, ss, ps):
    order = inv.shape[0]
    start = chain_index() == 0
    above = jnp.where(start, 0.0, couple[0]).T
    below = couple[1]
    inverse = inv[...]
    gain_above = nn(above, inverse, HIGH)
    gain_below = nn(below, inverse, HIGH)
    own_above = -nt(gain_above, above, HIGH)
    own_below = diag[1] - nt(gain_below, below, HIGH)
    link = -nt(gain_above, below, HIGH)
    left = on_first_core()
    gain_own[...] = jnp.where(left, gain_above, gain_below)
    gain_other[...] = jnp.where(left, gain_below, gain_above)
    ss[...] = jnp.where(left, own_below, own_above)
    ps[order:, :] = jnp.where(left, own_above, own_below)
    ps[:order, :] = jnp.where(left, link, link.T)


def first_sources_kernel(source, inv, gain_own, gain_other, _, sources, partial):
    columns = partial.shape[1]
    held = source[0]
    left = on_first_core()
    sources[:, :columns] = jnp.where(left, 0.0, source[1]) - nn(gain_own[...], held, HIGH)
    sources[:, columns:] = jnp.where(left, source[1], 0.0) - nn(gain_other[...], held, HIGH)
    partial[...] = nn(inv[...], held, HIGH)


def first_factors_kernel(gain_own, gain_other, partial, _, factors, offset):
    order, columns = partial.shape
    rows = lax.broadcasted_iota(jnp.int32, (order, order), 0)
    identity = (rows == lax.broadcasted_iota(jnp.int32, (order, order), 1)).astype(f32)
    left = on_first_core()
    factors[0, :order, :] = gain_own[...].T
    factors[1, :order, :] = gain_other[...].T
    factors[0, order:, :] = jnp.where(left, 0.0, -identity)
    factors[1, order:, :] = jnp.where(left, -identity, 0.0)
    offset[:order, :] = partial[...]
    offset[order:, :] = jnp.zeros((order, columns), f32)


def invert_kernel(squarings, own_ss, _, other_ss, inv):
    inverse_into(own_ss[...] + received_separator(other_ss), inv, squarings)


def store_element(stays, own, other, cross, ss, ps, sends):
    order = cross.shape[0]
    separator = jnp.where(stays, other, own)
    outer = jnp.where(stays, own, other)
    link = jnp.where(stays, cross, cross.T)
    ss[...] = separator
    ps[order:, :] = outer
    ps[:order, :] = link
    if sends:
        send_separator(separator, sends[0])
        send_link(link, outer, sends[1])


def pair_kernel(level, inv, own_ps, other_ps, gain_own, gain_other, ss, ps, *sends):
    order = inv.shape[0]
    stays = own_stays(level)
    inverse = inv[...]
    link_own, link_other = own_ps[:order, :], other_ps[:order, :]
    own_gain = nn(link_own, inverse, HIGH)
    other_gain = nn(link_other, inverse, HIGH)
    gain_own[...] = own_gain
    gain_other[...] = other_gain
    own = own_ps[order:, :] - nt(own_gain, link_own, HIGH)
    other = other_ps[order:, :] - nt(other_gain, link_other, HIGH)
    cross = -nt(own_gain, link_other, HIGH)
    store_element(stays, own, other, cross, ss, ps, sends)


def pass_kernel(_, arrived, passed):
    passed[...] = arrived[...]


def own_kernel(inv, own_ps, gain_own, reduced_own):
    order = inv.shape[0]
    link_own = own_ps[:order, :]
    gain_own[...] = nn(link_own, inv[...], HIGH)
    reduced_own[...] = own_ps[order:, :] - nt(gain_own[...], link_own, HIGH)


def merge_kernel(level, inv, gain_own, reduced_own, _, direct, swapped, gain_other, ss, ps, *sends):
    order = inv.shape[0]
    stays = own_stays(level)
    link_other, outer_other = received_link((direct, swapped))
    gain = nn(link_other, inv[...], HIGH)
    gain_other[...] = gain
    cross = -nt(gain_own[...], link_other, HIGH)
    reduced_other = outer_other - nt(gain, link_other, HIGH)
    store_element(stays, reduced_own[...], reduced_other, cross, ss, ps, sends)


def sources_step(level, inv, gain_own, gain_other, own_f, other_f):
    columns = own_f.shape[1] // 2
    stays = own_stays(level)
    own, other = own_f[...], other_f[...]
    held = own[:, columns:] + other[:, columns:]
    after_own = own[:, :columns] - nn(gain_own[...], held, HIGH)
    after_other = other[:, :columns] - nn(gain_other[...], held, HIGH)
    partial = nn(inv[...], held, HIGH)
    return jnp.where(stays, after_own, after_other), jnp.where(stays, after_other, after_own), partial


def sources_kernel(level, inv, gain_own, gain_other, own_f, other_f, _, sources, partial):
    columns = partial.shape[1]
    outer, inner, found = sources_step(level, inv, gain_own, gain_other, own_f, other_f)
    sources[:, :columns] = outer
    sources[:, columns:] = inner
    partial[...] = found


def factors_step(level, gain_own, gain_other, partial, factors, offset):
    stays = own_stays(level)
    inner = split(factors[1])
    new_offset = offset[...] - three_pass(inner, split(partial[...]))
    own_end = factors[0] - three_pass(inner, split(gain_own[...]), nt)
    other_end = -three_pass(inner, split(gain_other[...]), nt)
    return jnp.where(stays, own_end, other_end), jnp.where(stays, other_end, own_end), new_offset


def factors_kernel(level, gain_own, gain_other, partial, _, factors, offset, new_factors, new_offset):
    outer, inner, moved = factors_step(level, gain_own, gain_other, partial, factors, offset)
    new_factors[0] = outer
    new_factors[1] = inner
    new_offset[...] = moved


def end_kernel(ss, ps, end_inv, end_gain, new_ss, send_ss):
    order = ss.shape[0]
    rows = lax.broadcasted_iota(jnp.int32, (order, order), 0)
    identity = (rows == lax.broadcasted_iota(jnp.int32, (order, order), 1)).astype(f32)
    right = bit(chain_index(), LEVELS - 1) == 1
    inverse_into(jnp.where(right, ps[order:, :], identity), end_inv, 6)
    turned = ps[:order, :].T
    gain = nn(turned, end_inv[...], HIGH)
    end_gain[...] = gain
    separator = ss[...] - nt(gain, turned, HIGH)
    new_ss[...] = separator
    send_separator(separator, send_ss)


def end_sources_kernel(
    level, inv, gain_own, gain_other, own_f, other_f, end_inv, end_gain, _, sources, partial, end_partial
):
    outer, inner, found = sources_step(level, inv, gain_own, gain_other, own_f, other_f)
    sources[...] = inner - nn(end_gain[...], outer, HIGH)
    partial[...] = found
    end_partial[...] = nn(end_inv[...], outer, HIGH)


def end_factors_kernel(
    level, gain_own, gain_other, partial, _, factors, offset, end_gain, end_partial,
    new_factors, new_offset,
):
    outer, inner, moved = factors_step(level, gain_own, gain_other, partial, factors, offset)
    outer = split(outer)
    new_offset[...] = moved - three_pass(outer, split(end_partial[...]))
    new_factors[...] = inner - three_pass(outer, split(end_gain[...]), nt)


def back_kernel(inv, own_f, other_f, factors, offset, result):
    order = inv.shape[0]
    middle = nn(inv[...], own_f[...] + other_f[...], HIGH)
    both = offset[...] - three_pass(split(factors[...]), split(middle))
    result[0] = both[:order]
    result[1] = both[order:]


WEIGHTS = {"invert": 0.85, "own": 0.1, "merge": 0.1, "sources": 1.0, "factors": 0.1, "pass": 0.05, "end": 4.0, "tail": 0.1, "last": 0.1, "first": 2.0}


def call(kernel, name, operands, shapes):
    vmem = pl.BlockSpec(memory_space=pltpu.VMEM)
    flops = int(WEIGHTS[name.split("_")[0]] * 1e9)
    return pl.pallas_call(
        kernel,
        out_shape=[jax.ShapeDtypeStruct(shape, f32) for shape in shapes],
        in_specs=[vmem] * len(operands),
        out_specs=[vmem] * len(shapes),
        name=name,
        compiler_params=pltpu.CompilerParams(vmem_limit_bytes=40 << 20),
        cost_estimate=pl.CostEstimate(flops=flops, bytes_accessed=4096, transcendentals=0),
    )(*operands)


def local(diag_blocks, coupling, rhs):
    order, columns = rhs.shape[2:]
    square, tall = (order, order), (2 * order, order)
    small, medium = (2 * PACKED, HALF), (2 * HALF + PACKED, HALF)
    flat, slim = (order, 2 * columns), (order, columns)
    double, long = (2, 2 * order, order), (2 * order, columns)
    (inv,) = call(first_invert_kernel, "first_invert", (diag_blocks[0],), (square,))
    gain_own, gain_other, ss, ps = call(
        first_merge_kernel, "first_merge", (inv, diag_blocks[0], coupling[0]),
        (square, square, square, tall)
    )
    other_ss, other_ps = exchange(ss, 1), exchange(ps, 1)
    sources, partial = call(
        first_sources_kernel, "first_sources", (rhs[0], inv, gain_own, gain_other, ss), (flat, slim)
    )
    other_f = exchange(sources, 1)
    factors, offset = call(
        first_factors_kernel, "first_factors", (gain_own, gain_other, partial, ss), (double, long)
    )
    for level in range(1, LEVELS):
        last = level == LEVELS - 1
        (inv,) = call(
            functools.partial(invert_kernel, SQUARINGS[level]), f"invert_{level}",
            (ss, sources, other_ss), (square,),
        )
        if level > 1:
            before = (gain_own, gain_other, partial)
            gain_own, reduced_own = call(own_kernel, f"own_{level}", (inv, ps), (square, square))
            (passed,) = call(pass_kernel, f"pass_{level}", (reduced_own, direct_ps), (medium,))
            swapped_ps = exchange(passed, 1)
            factors, offset = call(
                functools.partial(factors_kernel, level - 1), f"factors_{level - 1}",
                before + (passed, factors, offset), (double, long),
            )
            gain_other, ss, ps, *sends = call(
                functools.partial(merge_kernel, level), f"merge_{level}",
                (inv, gain_own, reduced_own, offset, direct_ps, swapped_ps),
                (square, square, tall) + (() if last else (small, medium)),
            )
        else:
            gain_own, gain_other, ss, ps, *sends = call(
                functools.partial(pair_kernel, level), f"merge_{level}", (inv, ps, other_ps),
                (square, square, square, tall, small, medium),
            )
        if last:
            end_inv, end_gain, ss, send_ss = call(
                end_kernel, "end", (ss, ps), (square, square, square, small)
            )
        else:
            send_ss, send_ps = sends
            direct_ps = exchange(send_ps, level + 1)
        other_ss = exchange(send_ss, level + 1)
        held = (inv, gain_own, gain_other, sources, other_f)
        if last:
            sources, partial, end_partial = call(
                functools.partial(end_sources_kernel, level), "tail_sources",
                held + (end_inv, end_gain, send_ss), (slim, slim, slim),
            )
        else:
            sources, partial = call(
                functools.partial(sources_kernel, level), f"sources_{level}",
                held + (send_ss,), (flat, slim),
            )
        other_f = exchange(sources, level + 1)
    factors, offset = call(
        functools.partial(end_factors_kernel, level), "tail_factors",
        (gain_own, gain_other, partial, sources, factors, offset, end_gain, end_partial), (tall, long),
    )
    (inv,) = call(
        functools.partial(invert_kernel, SQUARINGS[LEVELS]), "last_invert", (ss, offset, other_ss),
        (square,),
    )
    (result,) = call(
        back_kernel, "tail_back", (inv, sources, other_f, factors, offset), ((2, order, columns),)
    )
    return result[None]


def solution(mesh):
    spec = P("seg", "run", None, None)
    return jax.shard_map(
        local, mesh=mesh, in_specs=(spec, spec, spec), out_specs=spec, check_vma=False
    )
```

```python
import functools

import jax
import jax.numpy as jnp
from jax import lax
from jax.experimental import pallas as pl
from jax.experimental.pallas import tpu as pltpu
from jax.sharding import PartitionSpec as P

HIGH = lax.Precision.HIGHEST
f32 = jnp.float32
bf16 = jnp.bfloat16
LEVELS = 7
TOLERANCE = 4e-3
SQUARINGS = (5, 4, 4, 3, 2, 2, 2, 2)
AXES = ("run", "seg")


def chain_coords(flat):
    run, seg = flat >> 3, flat & 7
    return seg >> 1, ((seg & 1) << 1) | (run >> 3), (run >> 1) & 3, run & 1


def flat_index(x, z, y, core):
    return ((((z & 1) << 3) | (y << 1) | core) << 3) | (x << 1) | (z >> 1)


def partner(level, flat):
    x, z, y, core = chain_coords(flat)
    if level == 1:
        core = core ^ 1
    elif level == 2:
        y = y ^ 1
    elif level == 3:
        y = 3 - y
    elif level == 4:
        z = z ^ 1
    elif level == 5:
        z = 3 - z
    elif level == 6:
        x = x ^ 1
    else:
        x = 3 - x
    return flat_index(x, z, y, core)


def exchange(value, level):
    return lax.ppermute(value, AXES, [(flat, partner(level, flat)) for flat in range(128)])


def chain_index():
    run, seg = lax.axis_index("run"), lax.axis_index("seg")
    return seg * 16 + run


def bit(value, place):
    return lax.rem(lax.div(value, 1 << place), 2)


def own_stays(level):
    chain = chain_index()
    if level == LEVELS:
        return bit(chain, LEVELS - 1) == 0
    return bit(chain, level - 1) == bit(chain, level)


def nn(left, right, precision=None):
    return lax.dot_general(
        left, right, (((1,), (0,)), ((), ())), precision=precision, preferred_element_type=f32
    )


def nt(left, right, precision=None):
    return lax.dot_general(
        left, right, (((1,), (1,)), ((), ())), precision=precision, preferred_element_type=f32
    )


def split(value):
    upper = value.astype(bf16)
    return upper, (value - upper.astype(f32)).astype(bf16)


def three_pass(left, right, dot=nn):
    lh, ll = left
    rh, rl = right
    return dot(lh, rh) + (dot(lh, rl) + dot(ll, rh))


def inverse_into(matrix, out_ref, squarings=5):
    order = matrix.shape[0]
    rows = lax.broadcasted_iota(jnp.int32, (order, order), 0)
    identity = (rows == lax.broadcasted_iota(jnp.int32, (order, order), 1)).astype(f32)
    norm = jnp.max(jnp.sum(jnp.abs(matrix), axis=0, keepdims=True), axis=1, keepdims=True)
    scale = 1.75 / norm
    rest = identity - matrix * scale
    found = (identity + rest) * scale
    rest = rest.astype(bf16)
    rest = nn(rest, rest).astype(bf16)
    for step in range(1, squarings):
        found = found + nn(found.astype(bf16), rest)
        if step < squarings - 1:
            rest = nn(rest, rest).astype(bf16)
    upper = split(found)
    rest = identity - three_pass(split(matrix), upper)
    found = found + nn(upper[0], rest.astype(bf16))
    rest = identity - nn(matrix, found, HIGH)
    miss = jnp.sum(rest * rest)
    out_ref[...] = found + three_pass(split(found), split(rest))

    @pl.when(jnp.logical_not(miss < TOLERANCE * TOLERANCE))
    def _():
        near = jnp.logical_and(miss < 0.25, scale > 0.0)
        out_ref[...] = jnp.where(near, out_ref[...], identity * scale)

        def unfinished(state):
            step, miss_now = state
            return jnp.logical_and(step < 64, miss_now >= TOLERANCE * TOLERANCE)

        def improve(state):
            now = out_ref[...]
            gap = identity - nn(matrix, now, HIGH)
            out_ref[...] = now + nn(now, gap, HIGH)
            return state[0] + 1, jnp.sum(gap * gap)

        lax.while_loop(unfinished, improve, (jnp.int32(0), jnp.float32(jnp.inf)))


HALF = 128
PACKED = HALF + 8


def on_first_core():
    return lax.rem(lax.axis_index("run"), 2) == 0


def ordered(direct, swapped):
    first = on_first_core()
    return jnp.where(first, direct, swapped), jnp.where(first, swapped, direct)


def triangle():
    rows = lax.broadcasted_iota(jnp.int32, (HALF, HALF), 0)
    columns = lax.broadcasted_iota(jnp.int32, (HALF, HALF), 1)
    return rows, columns


def pack_symmetric(value, first):
    rows, columns = triangle()
    upper_left, lower_right = value[:HALF, :HALF], value[HALF:, HALF:]
    diagonal = jnp.sum(jnp.where(rows == columns, lower_right, 0.0), axis=0, keepdims=True)
    both = jnp.where(rows >= columns, upper_left, lower_right)
    lower_left = value[HALF:, :HALF]
    main = (lower_left if first else both) if isinstance(first, bool) else jnp.where(first, lower_left, both)
    return main, jnp.broadcast_to(diagonal, (8, HALF))


def unpack_symmetric(from_first, from_second):
    rows, columns = triangle()
    lower_left, diagonal = from_first[:HALF], from_first[HALF : HALF + 1]
    both = from_second[:HALF]
    turned = both.T
    upper_left = jnp.where(rows >= columns, both, turned)
    lower_right = jnp.where(rows < columns, both, turned)
    lower_right = jnp.where(rows == columns, diagonal, lower_right)
    return jnp.concatenate(
        [
            jnp.concatenate([upper_left, lower_left.T], axis=1),
            jnp.concatenate([lower_left, lower_right], axis=1),
        ],
        axis=0,
    )


def send_separator(value, send):
    main, diagonal = pack_symmetric(value, on_first_core())
    send[:HALF, :] = main
    send[HALF:, :] = diagonal


def send_link(link, outer, send):
    first = on_first_core()
    rows = jnp.where(first, link[:HALF], link[HALF:])
    send[:HALF, :] = rows[:, :HALF]
    send[HALF : 2 * HALF, :] = rows[:, HALF:]
    main, diagonal = pack_symmetric(outer, first)
    send[2 * HALF : 3 * HALF, :] = main
    send[3 * HALF :, :] = diagonal


def received_separator(refs):
    if len(refs) == 1:
        value = refs[0][...]
        return value if value.shape[1] > HALF else unpack_symmetric(value[:PACKED], value[PACKED:])
    return unpack_symmetric(*ordered(refs[0][...], refs[1][...]))


def received_link(refs):
    if len(refs) == 1:
        order = refs[0].shape[1]
        return refs[0][:order, :], refs[0][order:, :]
    upper, lower = ordered(refs[0][...], refs[1][...])
    link = jnp.concatenate(
        [
            jnp.concatenate([upper[:HALF], upper[HALF : 2 * HALF]], axis=1),
            jnp.concatenate([lower[:HALF], lower[HALF : 2 * HALF]], axis=1),
        ],
        axis=0,
    )
    return link, unpack_symmetric(upper[2 * HALF :], lower[2 * HALF :])


def first_invert_kernel(diag, inv):
    inverse_into(diag[0], inv)


def first_merge_kernel(inv, diag, couple, gain_own, gain_other, ss, ps):
    order = inv.shape[0]
    start = chain_index() == 0
    above = jnp.where(start, 0.0, couple[0]).T
    below = couple[1]
    inverse = inv[...]
    gain_above = nn(above, inverse, HIGH)
    gain_below = nn(below, inverse, HIGH)
    own_above = -nt(gain_above, above, HIGH)
    own_below = diag[1] - nt(gain_below, below, HIGH)
    link = -nt(gain_above, below, HIGH)
    left = on_first_core()
    gain_own[...] = jnp.where(left, gain_above, gain_below)
    gain_other[...] = jnp.where(left, gain_below, gain_above)
    ss[...] = jnp.where(left, own_below, own_above)
    ps[order:, :] = jnp.where(left, own_above, own_below)
    ps[:order, :] = jnp.where(left, link, link.T)


def first_sources_kernel(source, inv, gain_own, gain_other, _, sources, partial):
    columns = partial.shape[1]
    held = source[0]
    left = on_first_core()
    sources[:, :columns] = jnp.where(left, 0.0, source[1]) - nn(gain_own[...], held, HIGH)
    sources[:, columns:] = jnp.where(left, source[1], 0.0) - nn(gain_other[...], held, HIGH)
    partial[...] = nn(inv[...], held, HIGH)


def first_factors_kernel(gain_own, gain_other, partial, _, factors, offset):
    order, columns = partial.shape
    rows = lax.broadcasted_iota(jnp.int32, (order, order), 0)
    identity = (rows == lax.broadcasted_iota(jnp.int32, (order, order), 1)).astype(f32)
    left = on_first_core()
    factors[0, :order, :] = gain_own[...].T
    factors[1, :order, :] = gain_other[...].T
    factors[0, order:, :] = jnp.where(left, 0.0, -identity)
    factors[1, order:, :] = jnp.where(left, -identity, 0.0)
    offset[:order, :] = partial[...]
    offset[order:, :] = jnp.zeros((order, columns), f32)


def invert_kernel(squarings, own_ss, _, *refs):
    inverse_into(own_ss[...] + received_separator(refs[:-1]), refs[-1], squarings)


def store_element(stays, own, other, cross, ss, ps, sends):
    order = cross.shape[0]
    separator = jnp.where(stays, other, own)
    outer = jnp.where(stays, own, other)
    link = jnp.where(stays, cross, cross.T)
    ss[...] = separator
    ps[order:, :] = outer
    ps[:order, :] = link
    if sends:
        send_separator(separator, sends[0])
        send_link(link, outer, sends[1])


def pair_kernel(level, inv, own_ps, other_ps, gain_own, gain_other, ss, ps, *sends):
    order = inv.shape[0]
    stays = own_stays(level)
    inverse = inv[...]
    link_own, link_other = own_ps[:order, :], other_ps[:order, :]
    own_gain = nn(link_own, inverse, HIGH)
    other_gain = nn(link_other, inverse, HIGH)
    gain_own[...] = own_gain
    gain_other[...] = other_gain
    own = own_ps[order:, :] - nt(own_gain, link_own, HIGH)
    other = other_ps[order:, :] - nt(other_gain, link_other, HIGH)
    cross = -nt(own_gain, link_other, HIGH)
    store_element(stays, own, other, cross, ss, ps, sends)


def pass_kernel(_, arrived, passed):
    passed[...] = arrived[...]


def own_kernel(inv, own_ps, _, gain_own, reduced_own):
    order = inv.shape[0]
    link_own = own_ps[:order, :]
    gain_own[...] = nn(link_own, inv[...], HIGH)
    reduced_own[...] = own_ps[order:, :] - nt(gain_own[...], link_own, HIGH)


def merge_kernel(level, count, inv, gain_own, reduced_own, *refs):
    others, (gain_other, ss, ps, *sends) = refs[:count], refs[count:]
    order = inv.shape[0]
    stays = own_stays(level)
    link_other, outer_other = received_link(others)
    gain = nn(link_other, inv[...], HIGH)
    gain_other[...] = gain
    cross = -nt(gain_own[...], link_other, HIGH)
    reduced_other = outer_other - nt(gain, link_other, HIGH)
    store_element(stays, reduced_own[...], reduced_other, cross, ss, ps, sends)


def sources_step(level, inv, gain_own, gain_other, own_f, other_f):
    columns = own_f.shape[1] // 2
    stays = own_stays(level)
    own, other = own_f[...], other_f[...]
    held = own[:, columns:] + other[:, columns:]
    after_own = own[:, :columns] - nn(gain_own[...], held, HIGH)
    after_other = other[:, :columns] - nn(gain_other[...], held, HIGH)
    partial = nn(inv[...], held, HIGH)
    return jnp.where(stays, after_own, after_other), jnp.where(stays, after_other, after_own), partial


def sources_kernel(level, inv, gain_own, gain_other, own_f, other_f, _, sources, partial):
    columns = partial.shape[1]
    outer, inner, found = sources_step(level, inv, gain_own, gain_other, own_f, other_f)
    sources[:, :columns] = outer
    sources[:, columns:] = inner
    partial[...] = found


def factors_step(level, gain_own, gain_other, partial, factors, offset):
    stays = own_stays(level)
    inner = split(factors[1])
    new_offset = offset[...] - three_pass(inner, split(partial[...]))
    own_end = factors[0] - three_pass(inner, split(gain_own[...]), nt)
    other_end = -three_pass(inner, split(gain_other[...]), nt)
    return jnp.where(stays, own_end, other_end), jnp.where(stays, other_end, own_end), new_offset


def factors_kernel(level, gain_own, gain_other, partial, _, factors, offset, new_factors, new_offset):
    outer, inner, moved = factors_step(level, gain_own, gain_other, partial, factors, offset)
    new_factors[0] = outer
    new_factors[1] = inner
    new_offset[...] = moved


def end_kernel(ss, ps, end_inv, end_gain, new_ss, send_ss):
    order = ss.shape[0]
    rows = lax.broadcasted_iota(jnp.int32, (order, order), 0)
    identity = (rows == lax.broadcasted_iota(jnp.int32, (order, order), 1)).astype(f32)
    right = bit(chain_index(), LEVELS - 1) == 1
    inverse_into(jnp.where(right, ps[order:, :], identity), end_inv, 6)
    turned = ps[:order, :].T
    gain = nn(turned, end_inv[...], HIGH)
    end_gain[...] = gain
    separator = ss[...] - nt(gain, turned, HIGH)
    new_ss[...] = separator
    for place, first in ((0, True), (PACKED, False)):
        main, diagonal = pack_symmetric(separator, first)
        send_ss[place : place + HALF, :] = main
        send_ss[place + HALF : place + PACKED, :] = diagonal


def end_sources_kernel(
    level, inv, gain_own, gain_other, own_f, other_f, end_inv, end_gain, _, sources, partial, end_partial
):
    outer, inner, found = sources_step(level, inv, gain_own, gain_other, own_f, other_f)
    sources[...] = inner - nn(end_gain[...], outer, HIGH)
    partial[...] = found
    end_partial[...] = nn(end_inv[...], outer, HIGH)


def end_factors_kernel(
    level, gain_own, gain_other, partial, _, factors, offset, end_gain, end_partial,
    new_factors, new_offset,
):
    outer, inner, moved = factors_step(level, gain_own, gain_other, partial, factors, offset)
    outer = split(outer)
    new_offset[...] = moved - three_pass(outer, split(end_partial[...]))
    new_factors[...] = inner - three_pass(outer, split(end_gain[...]), nt)


def back_kernel(inv, own_f, other_f, factors, offset, result):
    order = inv.shape[0]
    middle = nn(inv[...], own_f[...] + other_f[...], HIGH)
    both = offset[...] - three_pass(split(factors[...]), split(middle))
    result[0] = both[:order]
    result[1] = both[order:]


WEIGHTS = {"invert": 0.85, "own": 0.1, "merge": 0.1, "sources": 2.0, "factors": 1.0, "pass": 0.05, "end": 4.0, "tail": 0.1, "last": 0.1, "first": 2.0}


def call(kernel, name, operands, shapes):
    vmem = pl.BlockSpec(memory_space=pltpu.VMEM)
    flops = int(WEIGHTS[name.split("_")[0]] * 1e9)
    return pl.pallas_call(
        kernel,
        out_shape=[jax.ShapeDtypeStruct(shape, f32) for shape in shapes],
        in_specs=[vmem] * len(operands),
        out_specs=[vmem] * len(shapes),
        name=name,
        compiler_params=pltpu.CompilerParams(vmem_limit_bytes=40 << 20),
        cost_estimate=pl.CostEstimate(flops=flops, bytes_accessed=4096, transcendentals=0),
    )(*operands)


def local(diag_blocks, coupling, rhs):
    order, columns = rhs.shape[2:]
    square, tall = (order, order), (2 * order, order)
    small, medium = (PACKED, HALF), (2 * HALF + PACKED, HALF)
    flat, slim = (order, 2 * columns), (order, columns)
    double, long = (2, 2 * order, order), (2 * order, columns)
    (inv,) = call(first_invert_kernel, "first_invert", (diag_blocks[0],), (square,))
    gain_own, gain_other, ss, ps = call(
        first_merge_kernel, "first_merge", (inv, diag_blocks[0], coupling[0]),
        (square, square, square, tall)
    )
    others_ss = (exchange(ss, 1),)
    others_ps = (exchange(ps, 1),)
    sources, partial = call(
        first_sources_kernel, "first_sources", (rhs[0], inv, gain_own, gain_other, ss),
        (flat, slim)
    )
    other_f = exchange(sources, 1)
    factors, offset = call(
        first_factors_kernel, "first_factors", (gain_own, gain_other, partial, ss),
        (double, long)
    )

    def swapped(direct, after, name):
        (passed,) = call(pass_kernel, name, (after, direct), (direct.shape,))
        return (direct, exchange(passed, 1))

    for level in range(1, LEVELS):
        last = level == LEVELS - 1
        (inv,) = call(
            functools.partial(invert_kernel, SQUARINGS[level]), f"invert_{level}",
            (ss, offset) + others_ss, (square,)
        )
        if level > 1:
            others_ps = swapped(direct_ps, inv, f"pass_ps_{level}")
            gain_own, reduced_own = call(
                own_kernel, f"own_{level}", (inv, ps, others_ps[0]), (square, square)
            )
            gain_other, ss, ps, *sends = call(
                functools.partial(merge_kernel, level, len(others_ps)), f"merge_{level}",
                (inv, gain_own, reduced_own) + others_ps,
                (square, square, tall) + (() if last else (small, medium)),
            )
        else:
            gain_own, gain_other, ss, ps, *sends = call(
                functools.partial(pair_kernel, level), f"merge_{level}", (inv, ps) + others_ps,
                (square, square, square, tall, small, medium),
            )
        if last:
            end_inv, end_gain, ss, send_ss = call(
                end_kernel, "end", (ss, ps), (square, square, square, (2 * PACKED, HALF))
            )
        else:
            send_ss, send_ps = sends
        direct_ss = exchange(send_ss, level + 1)
        held = (inv, gain_own, gain_other, sources, other_f)
        if last:
            sources, partial, end_partial = call(
                functools.partial(end_sources_kernel, level), "tail_sources",
                held + (end_inv, end_gain, send_ss), (slim, slim, slim)
            )
        else:
            direct_ps = exchange(send_ps, level + 1)
            sources, partial = call(
                functools.partial(sources_kernel, level), f"sources_{level}",
                held + (send_ss,), (flat, slim)
            )
        other_f = exchange(sources, level + 1)
        if last:
            others_ss = (direct_ss,)
            factors, offset = call(
                functools.partial(end_factors_kernel, level), "tail_factors",
                (gain_own, gain_other, partial, send_ss, factors, offset, end_gain, end_partial),
                (tall, long),
            )
        else:
            others_ss = swapped(direct_ss, sources, f"pass_ss_{level + 1}")
            factors, offset = call(
                functools.partial(factors_kernel, level), f"factors_{level}",
                (gain_own, gain_other, partial, direct_ss, factors, offset), (double, long),
            )
    (inv,) = call(
        functools.partial(invert_kernel, SQUARINGS[LEVELS]), "last_invert", (ss, offset) + others_ss,
        (square,)
    )
    (result,) = call(
        back_kernel, "tail_back", (inv, sources, other_f, factors, offset), ((2, order, columns),)
    )
    return result[None]


def solution(mesh):
    spec = P("seg", "run", None, None)
    return jax.shard_map(
        local, mesh=mesh, in_specs=(spec, spec, spec), out_specs=spec, check_vma=False
    )
```

```python
import functools

import jax
import jax.numpy as jnp
from jax import lax
from jax.experimental import pallas as pl
from jax.experimental.pallas import tpu as pltpu
from jax.sharding import PartitionSpec as P

HIGH = lax.Precision.HIGHEST
f32 = jnp.float32
bf16 = jnp.bfloat16
LEVELS = 7
TOLERANCE = 4e-3
SQUARINGS = (5, 4, 4, 3, 2, 2, 2, 2)
AXES = ("run", "seg")


def chain_coords(flat):
    run, seg = flat >> 3, flat & 7
    return seg >> 1, ((seg & 1) << 1) | (run >> 3), (run >> 1) & 3, run & 1


def flat_index(x, z, y, core):
    return ((((z & 1) << 3) | (y << 1) | core) << 3) | (x << 1) | (z >> 1)


def partner(level, flat):
    x, z, y, core = chain_coords(flat)
    if level == 1:
        core = core ^ 1
    elif level == 2:
        y = y ^ 1
    elif level == 3:
        y = 3 - y
    elif level == 4:
        z = z ^ 1
    elif level == 5:
        z = 3 - z
    elif level == 6:
        x = x ^ 1
    else:
        x = 3 - x
    return flat_index(x, z, y, core)


def exchange(value, level):
    return lax.ppermute(value, AXES, [(flat, partner(level, flat)) for flat in range(128)])


def chain_index():
    run, seg = lax.axis_index("run"), lax.axis_index("seg")
    return seg * 16 + run


def bit(value, place):
    return lax.rem(lax.div(value, 1 << place), 2)


def own_stays(level):
    chain = chain_index()
    if level == LEVELS:
        return bit(chain, LEVELS - 1) == 0
    return bit(chain, level - 1) == bit(chain, level)


def nn(left, right, precision=None):
    return lax.dot_general(
        left, right, (((1,), (0,)), ((), ())), precision=precision, preferred_element_type=f32
    )


def nt(left, right, precision=None):
    return lax.dot_general(
        left, right, (((1,), (1,)), ((), ())), precision=precision, preferred_element_type=f32
    )


def split(value):
    upper = value.astype(bf16)
    return upper, (value - upper.astype(f32)).astype(bf16)


def three_pass(left, right, dot=nn):
    lh, ll = left
    rh, rl = right
    return dot(lh, rh) + (dot(lh, rl) + dot(ll, rh))


def inverse_into(matrix, out_ref, squarings=5):
    order = matrix.shape[0]
    rows = lax.broadcasted_iota(jnp.int32, (order, order), 0)
    identity = (rows == lax.broadcasted_iota(jnp.int32, (order, order), 1)).astype(f32)
    norm = jnp.max(jnp.sum(jnp.abs(matrix), axis=0, keepdims=True), axis=1, keepdims=True)
    scale = 1.75 / norm
    rest = identity - matrix * scale
    found = (identity + rest) * scale
    rest = rest.astype(bf16)
    rest = nn(rest, rest).astype(bf16)
    for step in range(1, squarings):
        found = found + nn(found.astype(bf16), rest)
        if step < squarings - 1:
            rest = nn(rest, rest).astype(bf16)
    upper = split(found)
    rest = identity - three_pass(split(matrix), upper)
    found = found + nn(upper[0], rest.astype(bf16))
    rest = identity - nn(matrix, found, HIGH)
    miss = jnp.sum(rest * rest)
    out_ref[...] = found + three_pass(split(found), split(rest))

    @pl.when(jnp.logical_not(miss < TOLERANCE * TOLERANCE))
    def _():
        near = jnp.logical_and(miss < 0.25, scale > 0.0)
        out_ref[...] = jnp.where(near, out_ref[...], identity * scale)

        def unfinished(state):
            step, miss_now = state
            return jnp.logical_and(step < 64, miss_now >= TOLERANCE * TOLERANCE)

        def improve(state):
            now = out_ref[...]
            gap = identity - nn(matrix, now, HIGH)
            out_ref[...] = now + nn(now, gap, HIGH)
            return state[0] + 1, jnp.sum(gap * gap)

        lax.while_loop(unfinished, improve, (jnp.int32(0), jnp.float32(jnp.inf)))


HALF = 128
PACKED = HALF + 8


def on_first_core():
    return lax.rem(lax.axis_index("run"), 2) == 0


def ordered(direct, swapped):
    first = on_first_core()
    return jnp.where(first, direct, swapped), jnp.where(first, swapped, direct)


def triangle():
    rows = lax.broadcasted_iota(jnp.int32, (HALF, HALF), 0)
    columns = lax.broadcasted_iota(jnp.int32, (HALF, HALF), 1)
    return rows, columns


def pack_symmetric(value, first):
    rows, columns = triangle()
    upper_left, lower_right = value[:HALF, :HALF], value[HALF:, HALF:]
    diagonal = jnp.sum(jnp.where(rows == columns, lower_right, 0.0), axis=0, keepdims=True)
    both = jnp.where(rows >= columns, upper_left, lower_right)
    lower_left = value[HALF:, :HALF]
    main = (lower_left if first else both) if isinstance(first, bool) else jnp.where(first, lower_left, both)
    return main, jnp.broadcast_to(diagonal, (8, HALF))


def unpack_symmetric(from_first, from_second):
    rows, columns = triangle()
    lower_left, diagonal = from_first[:HALF], from_first[HALF : HALF + 1]
    both = from_second[:HALF]
    turned = both.T
    upper_left = jnp.where(rows >= columns, both, turned)
    lower_right = jnp.where(rows < columns, both, turned)
    lower_right = jnp.where(rows == columns, diagonal, lower_right)
    return jnp.concatenate(
        [
            jnp.concatenate([upper_left, lower_left.T], axis=1),
            jnp.concatenate([lower_left, lower_right], axis=1),
        ],
        axis=0,
    )


def send_separator(value, send):
    main, diagonal = pack_symmetric(value, on_first_core())
    send[:HALF, :] = main
    send[HALF:, :] = diagonal


def send_link(link, outer, send):
    first = on_first_core()
    rows = jnp.where(first, link[:HALF], link[HALF:])
    send[:HALF, :] = rows[:, :HALF]
    send[HALF : 2 * HALF, :] = rows[:, HALF:]
    main, diagonal = pack_symmetric(outer, first)
    send[2 * HALF : 3 * HALF, :] = main
    send[3 * HALF :, :] = diagonal


def received_separator(refs):
    if len(refs) == 1:
        value = refs[0][...]
        return value if value.shape[1] > HALF else unpack_symmetric(value[:PACKED], value[PACKED:])
    return unpack_symmetric(*ordered(refs[0][...], refs[1][...]))


def received_link(refs):
    upper, lower = ordered(refs[0][...], refs[1][...])
    link = jnp.concatenate(
        [
            jnp.concatenate([upper[:HALF], upper[HALF : 2 * HALF]], axis=1),
            jnp.concatenate([lower[:HALF], lower[HALF : 2 * HALF]], axis=1),
        ],
        axis=0,
    )
    return link, unpack_symmetric(upper[2 * HALF :], lower[2 * HALF :])


def first_invert_kernel(diag, inv):
    inverse_into(diag[0], inv)


def first_merge_kernel(inv, diag, couple, gain_own, gain_other, ss, outer):
    start = chain_index() == 0
    above = jnp.where(start, 0.0, couple[0]).T
    below = couple[1]
    inverse = inv[...]
    gain_above = nn(above, inverse, HIGH)
    gain_below = nn(below, inverse, HIGH)
    own_above = -nt(gain_above, above, HIGH)
    own_below = diag[1] - nt(gain_below, below, HIGH)
    left = on_first_core()
    gain_own[...] = jnp.where(left, gain_above, gain_below)
    gain_other[...] = jnp.where(left, gain_below, gain_above)
    ss[...] = jnp.where(left, own_below, own_above)
    outer[...] = jnp.where(left, own_above, own_below)


def first_link_kernel(gain_own, gain_other, outer, couple, ps):
    order = outer.shape[0]
    left = on_first_core()
    gain_above = jnp.where(left, gain_own[...], gain_other[...])
    link = -nt(gain_above, couple[1], HIGH)
    ps[:order, :] = jnp.where(left, link, link.T)
    ps[order:, :] = outer[...]


def first_sources_kernel(source, inv, gain_own, gain_other, _, sources, partial):
    columns = partial.shape[1]
    held = source[0]
    left = on_first_core()
    sources[:, :columns] = jnp.where(left, 0.0, source[1]) - nn(gain_own[...], held, HIGH)
    sources[:, columns:] = jnp.where(left, source[1], 0.0) - nn(gain_other[...], held, HIGH)
    partial[...] = nn(inv[...], held, HIGH)


def first_factors_kernel(gain_own, gain_other, partial, _, factors, offset):
    order, columns = partial.shape
    rows = lax.broadcasted_iota(jnp.int32, (order, order), 0)
    identity = (rows == lax.broadcasted_iota(jnp.int32, (order, order), 1)).astype(f32)
    left = on_first_core()
    factors[0, :order, :] = gain_own[...].T
    factors[1, :order, :] = gain_other[...].T
    factors[0, order:, :] = jnp.where(left, 0.0, -identity)
    factors[1, order:, :] = jnp.where(left, -identity, 0.0)
    offset[:order, :] = partial[...]
    offset[order:, :] = jnp.zeros((order, columns), f32)


def invert_kernel(squarings, own_ss, _, *refs):
    inverse_into(own_ss[...] + received_separator(refs[:-1]), refs[-1], squarings)


def store_separator(stays, own, other, ss, outer, sends):
    separator = jnp.where(stays, other, own)
    ss[...] = separator
    outer[...] = jnp.where(stays, own, other)
    if sends:
        send_separator(separator, sends[0])


def store_link(stays, cross, outer, link, send):
    value = jnp.where(stays, cross, cross.T)
    link[...] = value
    send_link(value, outer[...], send)


def pair_kernel(level, inv, own_ps, other_ps, gain_own, gain_other, ss, outer, *sends):
    order = inv.shape[0]
    inverse = inv[...]
    link_own, link_other = own_ps[:order, :], other_ps[:order, :]
    own_gain = nn(link_own, inverse, HIGH)
    other_gain = nn(link_other, inverse, HIGH)
    gain_own[...] = own_gain
    gain_other[...] = other_gain
    own = own_ps[order:, :] - nt(own_gain, link_own, HIGH)
    other = other_ps[order:, :] - nt(other_gain, link_other, HIGH)
    store_separator(own_stays(level), own, other, ss, outer, sends)


def pair_link_kernel(level, gain_own, outer, other_ps, link, send):
    cross = -nt(gain_own[...], other_ps[: gain_own.shape[0], :], HIGH)
    store_link(own_stays(level), cross, outer, link, send)


def pass_kernel(_, arrived, passed):
    passed[...] = arrived[...]


def own_kernel(inv, link, outer, _, gain_own, reduced_own):
    link_own = link[...]
    gain_own[...] = nn(link_own, inv[...], HIGH)
    reduced_own[...] = outer[...] - nt(gain_own[...], link_own, HIGH)


def merge_kernel(level, inv, reduced_own, direct, swapped, gain_other, ss, outer, *sends):
    link_other, outer_other = received_link((direct, swapped))
    gain = nn(link_other, inv[...], HIGH)
    gain_other[...] = gain
    reduced_other = outer_other - nt(gain, link_other, HIGH)
    store_separator(own_stays(level), reduced_own[...], reduced_other, ss, outer, sends)


def link_kernel(level, gain_own, outer, direct, swapped, link, send):
    cross = -nt(gain_own[...], received_link((direct, swapped))[0], HIGH)
    store_link(own_stays(level), cross, outer, link, send)


def sources_step(level, gain_own, gain_other, own_f, other_f):
    columns = own_f.shape[1] // 2
    stays = own_stays(level)
    own, other = own_f[...], other_f[...]
    held = own[:, columns:] + other[:, columns:]
    after_own = own[:, :columns] - nn(gain_own[...], held, HIGH)
    after_other = other[:, :columns] - nn(gain_other[...], held, HIGH)
    return jnp.where(stays, after_own, after_other), jnp.where(stays, after_other, after_own), held


def sources_kernel(level, inv, gain_own, gain_other, own_f, other_f, _, sources, partial):
    columns = partial.shape[1]
    outer, inner, held = sources_step(level, gain_own, gain_other, own_f, other_f)
    sources[:, :columns] = outer
    sources[:, columns:] = inner
    partial[...] = nn(inv[...], held, HIGH)


def factors_step(level, gain_own, gain_other, partial, factors, offset):
    stays = own_stays(level)
    inner = split(factors[1])
    new_offset = offset[...] - three_pass(inner, split(partial))
    own_end = factors[0] - three_pass(inner, split(gain_own[...]), nt)
    other_end = -three_pass(inner, split(gain_other[...]), nt)
    return jnp.where(stays, own_end, other_end), jnp.where(stays, other_end, own_end), new_offset


def factors_kernel(level, gain_own, gain_other, partial, _, factors, offset, new_factors, new_offset):
    outer, inner, moved = factors_step(level, gain_own, gain_other, partial[...], factors, offset)
    new_factors[0] = outer
    new_factors[1] = inner
    new_offset[...] = moved


def end_kernel(level, ss, outer, gain_own, direct, swapped, end_inv, end_gain, new_ss, send_ss):
    order = ss.shape[0]
    rows = lax.broadcasted_iota(jnp.int32, (order, order), 0)
    identity = (rows == lax.broadcasted_iota(jnp.int32, (order, order), 1)).astype(f32)
    right = bit(chain_index(), LEVELS - 1) == 1
    inverse_into(jnp.where(right, outer[...], identity), end_inv, 6)
    cross = -nt(gain_own[...], received_link((direct, swapped))[0], HIGH)
    turned = jnp.where(own_stays(level), cross.T, cross)
    gain = nn(turned, end_inv[...], HIGH)
    end_gain[...] = gain
    separator = ss[...] - nt(gain, turned, HIGH)
    new_ss[...] = separator
    for place, first in ((0, True), (PACKED, False)):
        main, diagonal = pack_symmetric(separator, first)
        send_ss[place : place + HALF, :] = main
        send_ss[place + HALF : place + PACKED, :] = diagonal


def end_sources_kernel(level, gain_own, gain_other, own_f, other_f, end_gain, _, sources, outer, held):
    outer_f, inner_f, held_f = sources_step(level, gain_own, gain_other, own_f, other_f)
    sources[...] = inner_f - nn(end_gain[...], outer_f, HIGH)
    outer[...] = outer_f
    held[...] = held_f


def end_factors_kernel(
    level, inv, gain_own, gain_other, held, outer_f, end_inv, end_gain, _, factors, offset,
    new_factors, new_offset,
):
    partial = nn(inv[...], held[...], HIGH)
    end_partial = nn(end_inv[...], outer_f[...], HIGH)
    outer, inner, moved = factors_step(level, gain_own, gain_other, partial, factors, offset)
    outer = split(outer)
    new_offset[...] = moved - three_pass(outer, split(end_partial))
    new_factors[...] = inner - three_pass(outer, split(end_gain[...]), nt)


def back_kernel(inv, own_f, other_f, factors, offset, result):
    order = inv.shape[0]
    middle = nn(inv[...], own_f[...] + other_f[...], HIGH)
    both = offset[...] - three_pass(split(factors[...]), split(middle))
    result[0] = both[:order]
    result[1] = both[order:]


WEIGHTS = {"invert": 0.85, "own": 0.1, "merge": 0.1, "link": 0.1, "sources": 0.3, "factors": 0.1, "pass": 0.05, "end": 4.0, "tail": 0.1, "last": 0.1, "first": 2.0}


def call(kernel, name, operands, shapes):
    vmem = pl.BlockSpec(memory_space=pltpu.VMEM)
    flops = int(WEIGHTS[name.split("_")[0]] * 1e9)
    return pl.pallas_call(
        kernel,
        out_shape=[jax.ShapeDtypeStruct(shape, f32) for shape in shapes],
        in_specs=[vmem] * len(operands),
        out_specs=[vmem] * len(shapes),
        name=name,
        compiler_params=pltpu.CompilerParams(vmem_limit_bytes=40 << 20),
        cost_estimate=pl.CostEstimate(flops=flops, bytes_accessed=4096, transcendentals=0),
    )(*operands)


def local(diag_blocks, coupling, rhs):
    order, columns = rhs.shape[2:]
    square, tall = (order, order), (2 * order, order)
    small, medium = (PACKED, HALF), (2 * HALF + PACKED, HALF)
    flat, slim = (order, 2 * columns), (order, columns)
    double, long = (2, 2 * order, order), (2 * order, columns)
    (inv,) = call(first_invert_kernel, "first_invert", (diag_blocks[0],), (square,))
    gain_own, gain_other, ss, outer = call(
        first_merge_kernel, "first_merge", (inv, diag_blocks[0], coupling[0]), (square,) * 4
    )
    others_ss = (exchange(ss, 1),)
    (ps,) = call(
        first_link_kernel, "first_link", (gain_own, gain_other, outer, coupling[0]), (tall,)
    )
    other_ps = exchange(ps, 1)
    sources, partial = call(
        first_sources_kernel, "first_sources", (rhs[0], inv, gain_own, gain_other, ps), (flat, slim)
    )
    other_f = exchange(sources, 1)
    factors, offset = call(
        first_factors_kernel, "first_factors", (gain_own, gain_other, partial, ss), (double, long)
    )

    def swapped(direct, after, name):
        (passed,) = call(pass_kernel, name, (after, direct), (direct.shape,))
        return (direct, exchange(passed, 1))

    for level in range(1, LEVELS):
        last = level == LEVELS - 1
        send_ss_shape = () if last else (small,)
        (inv,) = call(
            functools.partial(invert_kernel, SQUARINGS[level]), f"invert_{level}",
            (ss, offset) + others_ss, (square,),
        )
        if level > 1:
            others_ps = swapped(direct_ps, inv, f"pass_ps_{level}")
            gain_own, reduced_own = call(
                own_kernel, f"own_{level}", (inv, link, outer, others_ps[0]), (square, square)
            )
            gain_other, ss, outer, *send_ss = call(
                functools.partial(merge_kernel, level), f"merge_{level}",
                (inv, reduced_own) + others_ps, (square, square, square) + send_ss_shape,
            )
            if not last:
                link, send_ps = call(
                    functools.partial(link_kernel, level), f"link_{level}",
                    (gain_own, outer) + others_ps, (square, medium),
                )
        else:
            gain_own, gain_other, ss, outer, *send_ss = call(
                functools.partial(pair_kernel, level), f"merge_{level}", (inv, ps, other_ps),
                (square,) * 4 + send_ss_shape,
            )
            link, send_ps = call(
                functools.partial(pair_link_kernel, level), f"link_{level}",
                (gain_own, outer, other_ps), (square, medium),
            )
        if last:
            end_inv, end_gain, ss, *send_ss = call(
                functools.partial(end_kernel, level), "end", (ss, outer, gain_own) + others_ps,
                (square, square, square, (2 * PACKED, HALF)),
            )
        direct_ss = exchange(send_ss[0], level + 1)
        if last:
            sources, outer_f, held = call(
                functools.partial(end_sources_kernel, level), "tail_sources",
                (gain_own, gain_other, sources, other_f, end_gain, send_ss[0]), (slim,) * 3,
            )
            other_f = exchange(sources, level + 1)
            factors, offset = call(
                functools.partial(end_factors_kernel, level), "tail_factors",
                (inv, gain_own, gain_other, held, outer_f, end_inv, end_gain, sources, factors, offset),
                (tall, long),
            )
            others_ss = (direct_ss,)
        else:
            direct_ps = exchange(send_ps, level + 1)
            sources, partial = call(
                functools.partial(sources_kernel, level), f"sources_{level}",
                (inv, gain_own, gain_other, sources, other_f, send_ps), (flat, slim),
            )
            other_f = exchange(sources, level + 1)
            factors, offset = call(
                functools.partial(factors_kernel, level), f"factors_{level}",
                (gain_own, gain_other, partial, send_ps, factors, offset), (double, long),
            )
            others_ss = swapped(direct_ss, offset, f"pass_ss_{level + 1}")
    (inv,) = call(
        functools.partial(invert_kernel, SQUARINGS[LEVELS]), "last_invert", (ss, offset) + others_ss,
        (square,),
    )
    (result,) = call(
        back_kernel, "tail_back", (inv, sources, other_f, factors, offset), ((2, order, columns),)
    )
    return result[None]


def solution(mesh):
    spec = P("seg", "run", None, None)
    return jax.shard_map(
        local, mesh=mesh, in_specs=(spec, spec, spec), out_specs=spec, check_vma=False
    )
```

```python
import functools

import jax
import jax.numpy as jnp
from jax import lax
from jax.experimental import pallas as pl
from jax.experimental.pallas import tpu as pltpu
from jax.sharding import PartitionSpec as P

HIGH = lax.Precision.HIGHEST
f32 = jnp.float32
bf16 = jnp.bfloat16
LEVELS = 7
TOLERANCE = 4e-3
SQUARINGS = (5, 4, 4, 3, 2, 2, 2, 2)
AXES = ("run", "seg")


def chain_coords(flat):
    run, seg = flat >> 3, flat & 7
    return seg >> 1, ((seg & 1) << 1) | (run >> 3), (run >> 1) & 3, run & 1


def flat_index(x, z, y, core):
    return ((((z & 1) << 3) | (y << 1) | core) << 3) | (x << 1) | (z >> 1)


def partner(level, flat):
    x, z, y, core = chain_coords(flat)
    if level == 1:
        core = core ^ 1
    elif level == 2:
        y = y ^ 1
    elif level == 3:
        y = 3 - y
    elif level == 4:
        z = z ^ 1
    elif level == 5:
        z = 3 - z
    elif level == 6:
        x = x ^ 1
    else:
        x = 3 - x
    return flat_index(x, z, y, core)


def exchange(value, level):
    return lax.ppermute(value, AXES, [(flat, partner(level, flat)) for flat in range(128)])


def chain_index():
    run, seg = lax.axis_index("run"), lax.axis_index("seg")
    return seg * 16 + run


def bit(value, place):
    return lax.rem(lax.div(value, 1 << place), 2)


def own_stays(level):
    chain = chain_index()
    if level == LEVELS:
        return bit(chain, LEVELS - 1) == 0
    return bit(chain, level - 1) == bit(chain, level)


def dot(left, right, contracted, precision):
    return lax.dot_general(
        left, right, (contracted, ((), ())), precision=precision, preferred_element_type=f32
    )


def nn(left, right, precision=None):
    half = left.shape[0] // 2
    parts = [dot(rows, right, ((1,), (0,)), precision) for rows in (left[:half], left[half:])]
    return jnp.concatenate(parts, axis=0)


def nt(left, right, precision=None):
    if precision is None:
        return dot(left, right, ((1,), (1,)), None)
    return nn(left, right.T, precision)


def split(value):
    upper = value.astype(bf16)
    return upper, (value - upper.astype(f32)).astype(bf16)


def three_pass(left, right, times=nn):
    lh, ll = left
    rh, rl = right
    return times(lh, rh) + (times(lh, rl) + times(ll, rh))


def inverse_into(matrix, out_ref, squarings=5):
    order = matrix.shape[0]
    rows = lax.broadcasted_iota(jnp.int32, (order, order), 0)
    identity = (rows == lax.broadcasted_iota(jnp.int32, (order, order), 1)).astype(f32)
    norm = jnp.max(jnp.sum(jnp.abs(matrix), axis=0, keepdims=True), axis=1, keepdims=True)
    scale = 1.75 / norm
    rest = identity - matrix * scale
    found = (identity + rest) * scale
    rest = rest.astype(bf16)
    rest = nn(rest, rest).astype(bf16)
    for step in range(1, squarings):
        found = found + nn(found.astype(bf16), rest)
        if step < squarings - 1:
            rest = nn(rest, rest).astype(bf16)
    upper = split(found)
    rest = identity - three_pass(split(matrix), upper)
    found = found + nn(upper[0], rest.astype(bf16))
    rest = identity - nn(matrix, found, HIGH)
    miss = jnp.sum(rest * rest)
    out_ref[...] = found + three_pass(split(found), split(rest))

    @pl.when(jnp.logical_not(miss < TOLERANCE * TOLERANCE))
    def _():
        near = jnp.logical_and(miss < 0.25, scale > 0.0)
        out_ref[...] = jnp.where(near, out_ref[...], identity * scale)

        def unfinished(state):
            step, miss_now = state
            return jnp.logical_and(step < 64, miss_now >= TOLERANCE * TOLERANCE)

        def improve(state):
            now = out_ref[...]
            gap = identity - nn(matrix, now, HIGH)
            out_ref[...] = now + nn(now, gap, HIGH)
            return state[0] + 1, jnp.sum(gap * gap)

        lax.while_loop(unfinished, improve, (jnp.int32(0), jnp.float32(jnp.inf)))


HALF = 128
PACKED = HALF + 8


def on_first_core():
    return lax.rem(lax.axis_index("run"), 2) == 0


def ordered(direct, swapped):
    first = on_first_core()
    return jnp.where(first, direct, swapped), jnp.where(first, swapped, direct)


def triangle():
    rows = lax.broadcasted_iota(jnp.int32, (HALF, HALF), 0)
    columns = lax.broadcasted_iota(jnp.int32, (HALF, HALF), 1)
    return rows, columns


def pack_symmetric(value, first):
    rows, columns = triangle()
    upper_left, lower_right = value[:HALF, :HALF], value[HALF:, HALF:]
    diagonal = jnp.sum(jnp.where(rows == columns, lower_right, 0.0), axis=0, keepdims=True)
    both = jnp.where(rows >= columns, upper_left, lower_right)
    lower_left = value[HALF:, :HALF]
    main = (lower_left if first else both) if isinstance(first, bool) else jnp.where(first, lower_left, both)
    return main, jnp.broadcast_to(diagonal, (8, HALF))


def unpack_symmetric(from_first, from_second):
    rows, columns = triangle()
    lower_left, diagonal = from_first[:HALF], from_first[HALF : HALF + 1]
    both = from_second[:HALF]
    turned = both.T
    upper_left = jnp.where(rows >= columns, both, turned)
    lower_right = jnp.where(rows < columns, both, turned)
    lower_right = jnp.where(rows == columns, diagonal, lower_right)
    return jnp.concatenate(
        [
            jnp.concatenate([upper_left, lower_left.T], axis=1),
            jnp.concatenate([lower_left, lower_right], axis=1),
        ],
        axis=0,
    )


def send_separator(value, send):
    main, diagonal = pack_symmetric(value, on_first_core())
    send[:HALF, :] = main
    send[HALF:, :] = diagonal


def send_link(link, outer, send):
    first = on_first_core()
    rows = jnp.where(first, link[:HALF], link[HALF:])
    send[:HALF, :] = rows[:, :HALF]
    send[HALF : 2 * HALF, :] = rows[:, HALF:]
    main, diagonal = pack_symmetric(outer, first)
    send[2 * HALF : 3 * HALF, :] = main
    send[3 * HALF :, :] = diagonal


def received_separator(refs):
    if len(refs) == 1:
        value = refs[0][...]
        return value if value.shape[1] > HALF else unpack_symmetric(value[:PACKED], value[PACKED:])
    return unpack_symmetric(*ordered(refs[0][...], refs[1][...]))


def received_link(refs):
    if len(refs) == 1:
        order = refs[0].shape[1]
        return refs[0][:order, :], refs[0][order:, :]
    upper, lower = ordered(refs[0][...], refs[1][...])
    link = jnp.concatenate(
        [
            jnp.concatenate([upper[:HALF], upper[HALF : 2 * HALF]], axis=1),
            jnp.concatenate([lower[:HALF], lower[HALF : 2 * HALF]], axis=1),
        ],
        axis=0,
    )
    return link, unpack_symmetric(upper[2 * HALF :], lower[2 * HALF :])


def first_invert_kernel(diag, inv):
    inverse_into(diag[0], inv)


def first_merge_kernel(inv, diag, couple, gain_own, gain_other, ss, ps):
    order = inv.shape[0]
    start = chain_index() == 0
    above = jnp.where(start, 0.0, couple[0]).T
    below = couple[1]
    inverse = inv[...]
    gain_above = nn(above, inverse, HIGH)
    gain_below = nn(below, inverse, HIGH)
    own_above = -nt(gain_above, above, HIGH)
    own_below = diag[1] - nt(gain_below, below, HIGH)
    link = -nt(gain_above, below, HIGH)
    left = on_first_core()
    gain_own[...] = jnp.where(left, gain_above, gain_below)
    gain_other[...] = jnp.where(left, gain_below, gain_above)
    ss[...] = jnp.where(left, own_below, own_above)
    ps[order:, :] = jnp.where(left, own_above, own_below)
    ps[:order, :] = jnp.where(left, link, link.T)


def first_sources_kernel(source, inv, gain_own, gain_other, _, sources, partial):
    columns = partial.shape[1]
    held = source[0]
    left = on_first_core()
    sources[:, :columns] = jnp.where(left, 0.0, source[1]) - nn(gain_own[...], held, HIGH)
    sources[:, columns:] = jnp.where(left, source[1], 0.0) - nn(gain_other[...], held, HIGH)
    partial[...] = nn(inv[...], held, HIGH)


def first_factors_kernel(gain_own, gain_other, partial, _, factors, offset):
    order, columns = partial.shape
    rows = lax.broadcasted_iota(jnp.int32, (order, order), 0)
    identity = (rows == lax.broadcasted_iota(jnp.int32, (order, order), 1)).astype(f32)
    left = on_first_core()
    factors[0, :order, :] = gain_own[...].T
    factors[1, :order, :] = gain_other[...].T
    factors[0, order:, :] = jnp.where(left, 0.0, -identity)
    factors[1, order:, :] = jnp.where(left, -identity, 0.0)
    offset[:order, :] = partial[...]
    offset[order:, :] = jnp.zeros((order, columns), f32)


def invert_kernel(squarings, own_ss, _, *refs):
    inverse_into(own_ss[...] + received_separator(refs[:-1]), refs[-1], squarings)


def store_element(stays, own, other, cross, ss, ps, sends):
    order = cross.shape[0]
    separator = jnp.where(stays, other, own)
    outer = jnp.where(stays, own, other)
    link = jnp.where(stays, cross, cross.T)
    ss[...] = separator
    ps[order:, :] = outer
    ps[:order, :] = link
    if sends:
        send_separator(separator, sends[0])
        send_link(link, outer, sends[1])


def pair_kernel(level, inv, own_ps, other_ps, gain_own, gain_other, ss, ps, *sends):
    order = inv.shape[0]
    stays = own_stays(level)
    inverse = inv[...]
    link_own, link_other = own_ps[:order, :], other_ps[:order, :]
    own_gain = nn(link_own, inverse, HIGH)
    other_gain = nn(link_other, inverse, HIGH)
    gain_own[...] = own_gain
    gain_other[...] = other_gain
    own = own_ps[order:, :] - nt(own_gain, link_own, HIGH)
    other = other_ps[order:, :] - nt(other_gain, link_other, HIGH)
    cross = -nt(own_gain, link_other, HIGH)
    store_element(stays, own, other, cross, ss, ps, sends)


def pass_kernel(_, arrived, passed):
    passed[...] = arrived[...]


def own_kernel(inv, own_ps, _, gain_own, reduced_own):
    order = inv.shape[0]
    link_own = own_ps[:order, :]
    gain_own[...] = nn(link_own, inv[...], HIGH)
    reduced_own[...] = own_ps[order:, :] - nt(gain_own[...], link_own, HIGH)


def merge_kernel(level, count, inv, gain_own, reduced_own, *refs):
    others, (gain_other, ss, ps, *sends) = refs[:count], refs[count:]
    order = inv.shape[0]
    stays = own_stays(level)
    link_other, outer_other = received_link(others)
    gain = nn(link_other, inv[...], HIGH)
    gain_other[...] = gain
    cross = -nt(gain_own[...], link_other, HIGH)
    reduced_other = outer_other - nt(gain, link_other, HIGH)
    store_element(stays, reduced_own[...], reduced_other, cross, ss, ps, sends)


def sources_step(level, inv, gain_own, gain_other, own_f, other_f):
    columns = own_f.shape[1] // 2
    stays = own_stays(level)
    own, other = own_f[...], other_f[...]
    held = own[:, columns:] + other[:, columns:]
    after_own = own[:, :columns] - nn(gain_own[...], held, HIGH)
    after_other = other[:, :columns] - nn(gain_other[...], held, HIGH)
    partial = nn(inv[...], held, HIGH)
    return jnp.where(stays, after_own, after_other), jnp.where(stays, after_other, after_own), partial


def sources_kernel(level, inv, gain_own, gain_other, own_f, other_f, _, sources, partial):
    columns = partial.shape[1]
    outer, inner, found = sources_step(level, inv, gain_own, gain_other, own_f, other_f)
    sources[:, :columns] = outer
    sources[:, columns:] = inner
    partial[...] = found


def factors_step(level, gain_own, gain_other, partial, factors, offset):
    stays = own_stays(level)
    inner = split(factors[1])
    new_offset = offset[...] - three_pass(inner, split(partial[...]))
    own_end = factors[0] - three_pass(inner, split(gain_own[...]), nt)
    other_end = -three_pass(inner, split(gain_other[...]), nt)
    return jnp.where(stays, own_end, other_end), jnp.where(stays, other_end, own_end), new_offset


def factors_kernel(level, gain_own, gain_other, partial, _, factors, offset, new_factors, new_offset):
    outer, inner, moved = factors_step(level, gain_own, gain_other, partial, factors, offset)
    new_factors[0] = outer
    new_factors[1] = inner
    new_offset[...] = moved


def end_kernel(ss, ps, end_inv, end_gain, new_ss, send_ss):
    order = ss.shape[0]
    rows = lax.broadcasted_iota(jnp.int32, (order, order), 0)
    identity = (rows == lax.broadcasted_iota(jnp.int32, (order, order), 1)).astype(f32)
    right = bit(chain_index(), LEVELS - 1) == 1
    inverse_into(jnp.where(right, ps[order:, :], identity), end_inv, 6)
    turned = ps[:order, :].T
    gain = nn(turned, end_inv[...], HIGH)
    end_gain[...] = gain
    separator = ss[...] - nt(gain, turned, HIGH)
    new_ss[...] = separator
    for place, first in ((0, True), (PACKED, False)):
        main, diagonal = pack_symmetric(separator, first)
        send_ss[place : place + HALF, :] = main
        send_ss[place + HALF : place + PACKED, :] = diagonal


def end_sources_kernel(
    level, inv, gain_own, gain_other, own_f, other_f, end_inv, end_gain, _, sources, partial, end_partial
):
    outer, inner, found = sources_step(level, inv, gain_own, gain_other, own_f, other_f)
    sources[...] = inner - nn(end_gain[...], outer, HIGH)
    partial[...] = found
    end_partial[...] = nn(end_inv[...], outer, HIGH)


def end_factors_kernel(
    level, gain_own, gain_other, partial, _, factors, offset, end_gain, end_partial,
    new_factors, new_offset,
):
    outer, inner, moved = factors_step(level, gain_own, gain_other, partial, factors, offset)
    outer = split(outer)
    new_offset[...] = moved - three_pass(outer, split(end_partial[...]))
    new_factors[...] = inner - three_pass(outer, split(end_gain[...]), nt)


def back_kernel(inv, own_f, other_f, factors, offset, result):
    order = inv.shape[0]
    middle = nn(inv[...], own_f[...] + other_f[...], HIGH)
    both = offset[...] - three_pass(split(factors[...]), split(middle))
    result[0] = both[:order]
    result[1] = both[order:]


WEIGHTS = {"invert": 0.85, "own": 0.1, "merge": 0.1, "sources": 0.3, "factors": 0.1, "pass": 0.05, "end": 4.0, "tail": 0.1, "last": 0.1, "first": 2.0}


def call(kernel, name, operands, shapes):
    vmem = pl.BlockSpec(memory_space=pltpu.VMEM)
    flops = int(WEIGHTS[name.split("_")[0]] * 1e9)
    return pl.pallas_call(
        kernel,
        out_shape=[jax.ShapeDtypeStruct(shape, f32) for shape in shapes],
        in_specs=[vmem] * len(operands),
        out_specs=[vmem] * len(shapes),
        name=name,
        compiler_params=pltpu.CompilerParams(vmem_limit_bytes=40 << 20),
        cost_estimate=pl.CostEstimate(flops=flops, bytes_accessed=4096, transcendentals=0),
    )(*operands)


def local(diag_blocks, coupling, rhs):
    order, columns = rhs.shape[2:]
    square, tall = (order, order), (2 * order, order)
    small, medium = (PACKED, HALF), (2 * HALF + PACKED, HALF)
    flat, slim = (order, 2 * columns), (order, columns)
    double, long = (2, 2 * order, order), (2 * order, columns)
    (inv,) = call(first_invert_kernel, "first_invert", (diag_blocks[0],), (square,))
    gain_own, gain_other, ss, ps = call(
        first_merge_kernel, "first_merge", (inv, diag_blocks[0], coupling[0]),
        (square, square, square, tall)
    )
    others_ss = (exchange(ss, 1),)
    others_ps = (exchange(ps, 1),)
    sources, partial = call(
        first_sources_kernel, "first_sources", (rhs[0], inv, gain_own, gain_other, ss),
        (flat, slim)
    )
    other_f = exchange(sources, 1)
    factors, offset = call(
        first_factors_kernel, "first_factors", (gain_own, gain_other, partial, ss),
        (double, long)
    )

    def swapped(direct, after, name):
        (passed,) = call(pass_kernel, name, (after, direct), (direct.shape,))
        return (direct, exchange(passed, 1))

    for level in range(1, LEVELS):
        last = level == LEVELS - 1
        (inv,) = call(
            functools.partial(invert_kernel, SQUARINGS[level]), f"invert_{level}",
            (ss, offset) + others_ss, (square,)
        )
        if level > 1:
            others_ps = swapped(direct_ps, inv, f"pass_ps_{level}")
            gain_own, reduced_own = call(
                own_kernel, f"own_{level}", (inv, ps, others_ps[0]), (square, square)
            )
            gain_other, ss, ps, *sends = call(
                functools.partial(merge_kernel, level, len(others_ps)), f"merge_{level}",
                (inv, gain_own, reduced_own) + others_ps,
                (square, square, tall) + (() if last else (small, medium)),
            )
        else:
            gain_own, gain_other, ss, ps, *sends = call(
                functools.partial(pair_kernel, level), f"merge_{level}", (inv, ps) + others_ps,
                (square, square, square, tall, small, medium),
            )
        if last:
            end_inv, end_gain, ss, send_ss = call(
                end_kernel, "end", (ss, ps), (square, square, square, (2 * PACKED, HALF))
            )
        else:
            send_ss, send_ps = sends
        direct_ss = exchange(send_ss, level + 1)
        held = (inv, gain_own, gain_other, sources, other_f)
        if last:
            sources, partial, end_partial = call(
                functools.partial(end_sources_kernel, level), "tail_sources",
                held + (end_inv, end_gain, send_ss), (slim, slim, slim)
            )
        else:
            direct_ps = exchange(send_ps, level + 1)
            sources, partial = call(
                functools.partial(sources_kernel, level), f"sources_{level}",
                held + (send_ss,), (flat, slim)
            )
        other_f = exchange(sources, level + 1)
        before = (gain_own, gain_other, partial, send_ss, factors, offset)
        if last:
            factors, offset = call(
                functools.partial(end_factors_kernel, level), "tail_factors",
                before + (end_gain, end_partial), (tall, long)
            )
        else:
            factors, offset = call(
                functools.partial(factors_kernel, level), f"factors_{level}", before,
                (double, long)
            )
        others_ss = (direct_ss,) if last else swapped(direct_ss, offset, f"pass_ss_{level + 1}")
    (inv,) = call(
        functools.partial(invert_kernel, SQUARINGS[LEVELS]), "last_invert", (ss, offset) + others_ss,
        (square,)
    )
    (result,) = call(
        back_kernel, "tail_back", (inv, sources, other_f, factors, offset), ((2, order, columns),)
    )
    return result[None]


def solution(mesh):
    spec = P("seg", "run", None, None)
    return jax.shard_map(
        local, mesh=mesh, in_specs=(spec, spec, spec), out_specs=spec, check_vma=False
    )
```

```python
import functools

import jax
import jax.numpy as jnp
from jax import lax
from jax.experimental import pallas as pl
from jax.experimental.pallas import tpu as pltpu
from jax.sharding import PartitionSpec as P

HIGH = lax.Precision.HIGHEST
f32 = jnp.float32
bf16 = jnp.bfloat16
LEVELS = 7
TOLERANCE = 4e-3
SQUARINGS = (5, 4, 4, 3, 2, 2, 2, 2)
AXES = ("run", "seg")


def chain_coords(flat):
    run, seg = flat >> 3, flat & 7
    return seg >> 1, ((seg & 1) << 1) | (run >> 3), (run >> 1) & 3, run & 1


def flat_index(x, z, y, core):
    return ((((z & 1) << 3) | (y << 1) | core) << 3) | (x << 1) | (z >> 1)


def partner(level, flat):
    x, z, y, core = chain_coords(flat)
    if level == 1:
        core = core ^ 1
    elif level == 2:
        y = y ^ 1
    elif level == 3:
        y = 3 - y
    elif level == 4:
        z = z ^ 1
    elif level == 5:
        z = 3 - z
    elif level == 6:
        x = x ^ 1
    else:
        x = 3 - x
    return flat_index(x, z, y, core)


def exchange(value, level):
    return lax.ppermute(value, AXES, [(flat, partner(level, flat)) for flat in range(128)])


def chain_index():
    run, seg = lax.axis_index("run"), lax.axis_index("seg")
    return seg * 16 + run


def bit(value, place):
    return lax.rem(lax.div(value, 1 << place), 2)


def own_stays(level):
    chain = chain_index()
    if level == LEVELS:
        return bit(chain, LEVELS - 1) == 0
    return bit(chain, level - 1) == bit(chain, level)


def nn(left, right, precision=None):
    return lax.dot_general(
        left, right, (((1,), (0,)), ((), ())), precision=precision, preferred_element_type=f32
    )


def nt(left, right, precision=None):
    return lax.dot_general(
        left, right, (((1,), (1,)), ((), ())), precision=precision, preferred_element_type=f32
    )


def halves(left, right, precision=None):
    half = left.shape[0] // 2
    return jnp.concatenate(
        [nn(left[:half], right, precision), nn(left[half:], right, precision)], axis=0
    )


def split(value):
    upper = value.astype(bf16)
    return upper, (value - upper.astype(f32)).astype(bf16)


def three_pass(left, right, dot=nn):
    lh, ll = left
    rh, rl = right
    return dot(lh, rh) + (dot(lh, rl) + dot(ll, rh))


def inverse_into(matrix, out_ref, squarings=5):
    order = matrix.shape[0]
    rows = lax.broadcasted_iota(jnp.int32, (order, order), 0)
    identity = (rows == lax.broadcasted_iota(jnp.int32, (order, order), 1)).astype(f32)
    norm = jnp.max(jnp.sum(jnp.abs(matrix), axis=0, keepdims=True), axis=1, keepdims=True)
    scale = 1.75 / norm
    rest = identity - matrix * scale
    found = (identity + rest) * scale
    rest = rest.astype(bf16)
    rest = halves(rest, rest).astype(bf16)
    for step in range(1, squarings):
        found = found + halves(found.astype(bf16), rest)
        if step < squarings - 1:
            rest = halves(rest, rest).astype(bf16)
    upper = split(found)
    rest = identity - three_pass(split(matrix), upper, halves)
    found = found + halves(upper[0], rest.astype(bf16))
    rest = identity - halves(matrix, found, HIGH)
    miss = jnp.sum(rest * rest)
    out_ref[...] = found + three_pass(split(found), split(rest), halves)

    @pl.when(jnp.logical_not(miss < TOLERANCE * TOLERANCE))
    def _():
        near = jnp.logical_and(miss < 0.25, scale > 0.0)
        out_ref[...] = jnp.where(near, out_ref[...], identity * scale)

        def unfinished(state):
            step, miss_now = state
            return jnp.logical_and(step < 64, miss_now >= TOLERANCE * TOLERANCE)

        def improve(state):
            now = out_ref[...]
            gap = identity - halves(matrix, now, HIGH)
            out_ref[...] = now + halves(now, gap, HIGH)
            return state[0] + 1, jnp.sum(gap * gap)

        lax.while_loop(unfinished, improve, (jnp.int32(0), jnp.float32(jnp.inf)))


HALF = 128
PACKED = HALF + 8


def on_first_core():
    return lax.rem(lax.axis_index("run"), 2) == 0


def ordered(direct, swapped):
    first = on_first_core()
    return jnp.where(first, direct, swapped), jnp.where(first, swapped, direct)


def triangle():
    rows = lax.broadcasted_iota(jnp.int32, (HALF, HALF), 0)
    columns = lax.broadcasted_iota(jnp.int32, (HALF, HALF), 1)
    return rows, columns


def pack_symmetric(value, first):
    rows, columns = triangle()
    upper_left, lower_right = value[:HALF, :HALF], value[HALF:, HALF:]
    diagonal = jnp.sum(jnp.where(rows == columns, lower_right, 0.0), axis=0, keepdims=True)
    both = jnp.where(rows >= columns, upper_left, lower_right)
    lower_left = value[HALF:, :HALF]
    main = (lower_left if first else both) if isinstance(first, bool) else jnp.where(first, lower_left, both)
    return main, jnp.broadcast_to(diagonal, (8, HALF))


def unpack_symmetric(from_first, from_second):
    rows, columns = triangle()
    lower_left, diagonal = from_first[:HALF], from_first[HALF : HALF + 1]
    both = from_second[:HALF]
    turned = both.T
    upper_left = jnp.where(rows >= columns, both, turned)
    lower_right = jnp.where(rows < columns, both, turned)
    lower_right = jnp.where(rows == columns, diagonal, lower_right)
    return jnp.concatenate(
        [
            jnp.concatenate([upper_left, lower_left.T], axis=1),
            jnp.concatenate([lower_left, lower_right], axis=1),
        ],
        axis=0,
    )


def send_separator(value, send):
    main, diagonal = pack_symmetric(value, on_first_core())
    send[:HALF, :] = main
    send[HALF:, :] = diagonal


def send_link(link, outer, send):
    first = on_first_core()
    rows = jnp.where(first, link[:HALF], link[HALF:])
    send[:HALF, :] = rows[:, :HALF]
    send[HALF : 2 * HALF, :] = rows[:, HALF:]
    main, diagonal = pack_symmetric(outer, first)
    send[2 * HALF : 3 * HALF, :] = main
    send[3 * HALF :, :] = diagonal


def received_separator(refs):
    if len(refs) == 1:
        value = refs[0][...]
        return value if value.shape[1] > HALF else unpack_symmetric(value[:PACKED], value[PACKED:])
    return unpack_symmetric(*ordered(refs[0][...], refs[1][...]))


def received_link(refs):
    if len(refs) == 1:
        order = refs[0].shape[1]
        return refs[0][:order, :], refs[0][order:, :]
    upper, lower = ordered(refs[0][...], refs[1][...])
    link = jnp.concatenate(
        [
            jnp.concatenate([upper[:HALF], upper[HALF : 2 * HALF]], axis=1),
            jnp.concatenate([lower[:HALF], lower[HALF : 2 * HALF]], axis=1),
        ],
        axis=0,
    )
    return link, unpack_symmetric(upper[2 * HALF :], lower[2 * HALF :])


def first_invert_kernel(diag, inv):
    inverse_into(diag[0], inv)


def first_merge_kernel(inv, diag, couple, gain_own, gain_other, ss, ps):
    order = inv.shape[0]
    start = chain_index() == 0
    above = jnp.where(start, 0.0, couple[0]).T
    below = couple[1]
    inverse = inv[...]
    gain_above = nn(above, inverse, HIGH)
    gain_below = nn(below, inverse, HIGH)
    own_above = -nt(gain_above, above, HIGH)
    own_below = diag[1] - nt(gain_below, below, HIGH)
    link = -nt(gain_above, below, HIGH)
    left = on_first_core()
    gain_own[...] = jnp.where(left, gain_above, gain_below)
    gain_other[...] = jnp.where(left, gain_below, gain_above)
    ss[...] = jnp.where(left, own_below, own_above)
    ps[order:, :] = jnp.where(left, own_above, own_below)
    ps[:order, :] = jnp.where(left, link, link.T)


def first_sources_kernel(source, inv, gain_own, gain_other, _, sources, partial):
    columns = partial.shape[1]
    held = source[0]
    left = on_first_core()
    sources[:, :columns] = jnp.where(left, 0.0, source[1]) - nn(gain_own[...], held, HIGH)
    sources[:, columns:] = jnp.where(left, source[1], 0.0) - nn(gain_other[...], held, HIGH)
    partial[...] = nn(inv[...], held, HIGH)


def first_factors_kernel(gain_own, gain_other, partial, _, factors, offset):
    order, columns = partial.shape
    rows = lax.broadcasted_iota(jnp.int32, (order, order), 0)
    identity = (rows == lax.broadcasted_iota(jnp.int32, (order, order), 1)).astype(f32)
    left = on_first_core()
    factors[0, :order, :] = gain_own[...].T
    factors[1, :order, :] = gain_other[...].T
    factors[0, order:, :] = jnp.where(left, 0.0, -identity)
    factors[1, order:, :] = jnp.where(left, -identity, 0.0)
    offset[:order, :] = partial[...]
    offset[order:, :] = jnp.zeros((order, columns), f32)


def invert_kernel(squarings, own_ss, _, *refs):
    inverse_into(own_ss[...] + received_separator(refs[:-1]), refs[-1], squarings)


def store_element(stays, own, other, cross, ss, ps, sends):
    order = cross.shape[0]
    separator = jnp.where(stays, other, own)
    outer = jnp.where(stays, own, other)
    link = jnp.where(stays, cross, cross.T)
    ss[...] = separator
    ps[order:, :] = outer
    ps[:order, :] = link
    if sends:
        send_separator(separator, sends[0])
        send_link(link, outer, sends[1])


def pair_kernel(level, inv, own_ps, other_ps, gain_own, gain_other, ss, ps, *sends):
    order = inv.shape[0]
    stays = own_stays(level)
    inverse = inv[...]
    link_own, link_other = own_ps[:order, :], other_ps[:order, :]
    own_gain = nn(link_own, inverse, HIGH)
    other_gain = nn(link_other, inverse, HIGH)
    gain_own[...] = own_gain
    gain_other[...] = other_gain
    own = own_ps[order:, :] - nt(own_gain, link_own, HIGH)
    other = other_ps[order:, :] - nt(other_gain, link_other, HIGH)
    cross = -nt(own_gain, link_other, HIGH)
    store_element(stays, own, other, cross, ss, ps, sends)


def pass_kernel(_, arrived, passed):
    passed[...] = arrived[...]


def own_kernel(inv, own_ps, _, gain_own, reduced_own):
    order = inv.shape[0]
    link_own = own_ps[:order, :]
    gain_own[...] = nn(link_own, inv[...], HIGH)
    reduced_own[...] = own_ps[order:, :] - nt(gain_own[...], link_own, HIGH)


def merge_kernel(level, count, inv, gain_own, reduced_own, *refs):
    others, (gain_other, ss, ps, *sends) = refs[:count], refs[count:]
    order = inv.shape[0]
    stays = own_stays(level)
    link_other, outer_other = received_link(others)
    gain = nn(link_other, inv[...], HIGH)
    gain_other[...] = gain
    cross = -nt(gain_own[...], link_other, HIGH)
    reduced_other = outer_other - nt(gain, link_other, HIGH)
    store_element(stays, reduced_own[...], reduced_other, cross, ss, ps, sends)


def sources_step(level, inv, gain_own, gain_other, own_f, other_f):
    columns = own_f.shape[1] // 2
    stays = own_stays(level)
    own, other = own_f[...], other_f[...]
    held = own[:, columns:] + other[:, columns:]
    after_own = own[:, :columns] - halves(gain_own[...], held, HIGH)
    after_other = other[:, :columns] - halves(gain_other[...], held, HIGH)
    partial = halves(inv[...], held, HIGH)
    return jnp.where(stays, after_own, after_other), jnp.where(stays, after_other, after_own), partial


def sources_kernel(level, inv, gain_own, gain_other, own_f, other_f, _, sources, partial):
    columns = partial.shape[1]
    outer, inner, found = sources_step(level, inv, gain_own, gain_other, own_f, other_f)
    sources[:, :columns] = outer
    sources[:, columns:] = inner
    partial[...] = found


def factors_step(level, gain_own, gain_other, partial, factors, offset):
    stays = own_stays(level)
    inner = split(factors[1])
    new_offset = offset[...] - three_pass(inner, split(partial[...]))
    own_end = factors[0] - three_pass(inner, split(gain_own[...]), nt)
    other_end = -three_pass(inner, split(gain_other[...]), nt)
    return jnp.where(stays, own_end, other_end), jnp.where(stays, other_end, own_end), new_offset


def factors_kernel(level, gain_own, gain_other, partial, _, factors, offset, new_factors, new_offset):
    outer, inner, moved = factors_step(level, gain_own, gain_other, partial, factors, offset)
    new_factors[0] = outer
    new_factors[1] = inner
    new_offset[...] = moved


def end_kernel(ss, ps, end_inv, end_gain, new_ss, send_ss):
    order = ss.shape[0]
    rows = lax.broadcasted_iota(jnp.int32, (order, order), 0)
    identity = (rows == lax.broadcasted_iota(jnp.int32, (order, order), 1)).astype(f32)
    right = bit(chain_index(), LEVELS - 1) == 1
    inverse_into(jnp.where(right, ps[order:, :], identity), end_inv, 6)
    turned = ps[:order, :].T
    gain = halves(turned, end_inv[...], HIGH)
    end_gain[...] = gain
    separator = ss[...] - halves(gain, ps[:order, :], HIGH)
    new_ss[...] = separator
    for place, first in ((0, True), (PACKED, False)):
        main, diagonal = pack_symmetric(separator, first)
        send_ss[place : place + HALF, :] = main
        send_ss[place + HALF : place + PACKED, :] = diagonal


def end_sources_kernel(
    level, inv, gain_own, gain_other, own_f, other_f, end_inv, end_gain, _, sources, partial, end_partial
):
    outer, inner, found = sources_step(level, inv, gain_own, gain_other, own_f, other_f)
    sources[...] = inner - halves(end_gain[...], outer, HIGH)
    partial[...] = found
    end_partial[...] = halves(end_inv[...], outer, HIGH)


def end_factors_kernel(
    level, gain_own, gain_other, partial, _, factors, offset, end_gain, end_partial,
    new_factors, new_offset,
):
    outer, inner, moved = factors_step(level, gain_own, gain_other, partial, factors, offset)
    outer = split(outer)
    new_offset[...] = moved - three_pass(outer, split(end_partial[...]))
    new_factors[...] = inner - three_pass(outer, split(end_gain[...]), nt)


def back_kernel(inv, own_f, other_f, factors, offset, result):
    order = inv.shape[0]
    middle = halves(inv[...], own_f[...] + other_f[...], HIGH)
    both = offset[...] - three_pass(split(factors[...]), split(middle), halves)
    result[0] = both[:order]
    result[1] = both[order:]


WEIGHTS = {"invert": 0.85, "own": 0.1, "merge": 0.1, "sources": 0.3, "factors": 0.1, "pass": 0.05, "end": 4.0, "tail": 0.1, "last": 0.1, "first": 2.0}


def call(kernel, name, operands, shapes):
    vmem = pl.BlockSpec(memory_space=pltpu.VMEM)
    flops = int(WEIGHTS[name.split("_")[0]] * 1e9)
    return pl.pallas_call(
        kernel,
        out_shape=[jax.ShapeDtypeStruct(shape, f32) for shape in shapes],
        in_specs=[vmem] * len(operands),
        out_specs=[vmem] * len(shapes),
        name=name,
        compiler_params=pltpu.CompilerParams(vmem_limit_bytes=40 << 20),
        cost_estimate=pl.CostEstimate(flops=flops, bytes_accessed=4096, transcendentals=0),
    )(*operands)


def local(diag_blocks, coupling, rhs):
    order, columns = rhs.shape[2:]
    square, tall = (order, order), (2 * order, order)
    small, medium = (PACKED, HALF), (2 * HALF + PACKED, HALF)
    flat, slim = (order, 2 * columns), (order, columns)
    double, long = (2, 2 * order, order), (2 * order, columns)
    (inv,) = call(first_invert_kernel, "first_invert", (diag_blocks[0],), (square,))
    gain_own, gain_other, ss, ps = call(
        first_merge_kernel, "first_merge", (inv, diag_blocks[0], coupling[0]),
        (square, square, square, tall)
    )
    others_ss = (exchange(ss, 1),)
    others_ps = (exchange(ps, 1),)
    sources, partial = call(
        first_sources_kernel, "first_sources", (rhs[0], inv, gain_own, gain_other, ss),
        (flat, slim)
    )
    other_f = exchange(sources, 1)
    factors, offset = call(
        first_factors_kernel, "first_factors", (gain_own, gain_other, partial, ss),
        (double, long)
    )

    def swapped(direct, after, name):
        (passed,) = call(pass_kernel, name, (after, direct), (direct.shape,))
        return (direct, exchange(passed, 1))

    for level in range(1, LEVELS):
        last = level == LEVELS - 1
        (inv,) = call(
            functools.partial(invert_kernel, SQUARINGS[level]), f"invert_{level}",
            (ss, offset) + others_ss, (square,)
        )
        if level > 1:
            others_ps = swapped(direct_ps, inv, f"pass_ps_{level}")
            gain_own, reduced_own = call(
                own_kernel, f"own_{level}", (inv, ps, others_ps[0]), (square, square)
            )
            gain_other, ss, ps, *sends = call(
                functools.partial(merge_kernel, level, len(others_ps)), f"merge_{level}",
                (inv, gain_own, reduced_own) + others_ps,
                (square, square, tall) + (() if last else (small, medium)),
            )
        else:
            gain_own, gain_other, ss, ps, *sends = call(
                functools.partial(pair_kernel, level), f"merge_{level}", (inv, ps) + others_ps,
                (square, square, square, tall, small, medium),
            )
        if last:
            end_inv, end_gain, ss, send_ss = call(
                end_kernel, "end", (ss, ps), (square, square, square, (2 * PACKED, HALF))
            )
        else:
            send_ss, send_ps = sends
        direct_ss = exchange(send_ss, level + 1)
        held = (inv, gain_own, gain_other, sources, other_f)
        if last:
            sources, partial, end_partial = call(
                functools.partial(end_sources_kernel, level), "tail_sources",
                held + (end_inv, end_gain, send_ss), (slim, slim, slim)
            )
        else:
            direct_ps = exchange(send_ps, level + 1)
            sources, partial = call(
                functools.partial(sources_kernel, level), f"sources_{level}",
                held + (send_ss,), (flat, slim)
            )
        other_f = exchange(sources, level + 1)
        before = (gain_own, gain_other, partial, send_ss, factors, offset)
        if last:
            factors, offset = call(
                functools.partial(end_factors_kernel, level), "tail_factors",
                before + (end_gain, end_partial), (tall, long)
            )
        else:
            factors, offset = call(
                functools.partial(factors_kernel, level), f"factors_{level}", before,
                (double, long)
            )
        others_ss = (direct_ss,) if last else swapped(direct_ss, offset, f"pass_ss_{level + 1}")
    (inv,) = call(
        functools.partial(invert_kernel, SQUARINGS[LEVELS]), "last_invert", (ss, offset) + others_ss,
        (square,)
    )
    (result,) = call(
        back_kernel, "tail_back", (inv, sources, other_f, factors, offset), ((2, order, columns),)
    )
    return result[None]


def solution(mesh):
    spec = P("seg", "run", None, None)
    return jax.shard_map(
        local, mesh=mesh, in_specs=(spec, spec, spec), out_specs=spec, check_vma=False
    )
```

```python
import functools

import jax
import jax.numpy as jnp
from jax import lax
from jax.experimental import pallas as pl
from jax.experimental.pallas import tpu as pltpu
from jax.sharding import PartitionSpec as P

HIGH = lax.Precision.HIGHEST
f32 = jnp.float32
bf16 = jnp.bfloat16
LEVELS = 7
TOLERANCE = 4e-3
SQUARINGS = (5, 4, 4, 3, 2, 2, 2, 2)
AXES = ("run", "seg")


def chain_coords(flat):
    run, seg = flat >> 3, flat & 7
    return seg >> 1, ((seg & 1) << 1) | (run >> 3), (run >> 1) & 3, run & 1


def flat_index(x, z, y, core):
    return ((((z & 1) << 3) | (y << 1) | core) << 3) | (x << 1) | (z >> 1)


def partner(level, flat):
    x, z, y, core = chain_coords(flat)
    if level == 1:
        core = core ^ 1
    elif level == 2:
        y = y ^ 1
    elif level == 3:
        y = 3 - y
    elif level == 4:
        z = z ^ 1
    elif level == 5:
        z = 3 - z
    elif level == 6:
        x = x ^ 1
    else:
        x = 3 - x
    return flat_index(x, z, y, core)


def exchange(value, level):
    return lax.ppermute(value, AXES, [(flat, partner(level, flat)) for flat in range(128)])


def chain_index():
    run, seg = lax.axis_index("run"), lax.axis_index("seg")
    return seg * 16 + run


def bit(value, place):
    return lax.rem(lax.div(value, 1 << place), 2)


def own_stays(level):
    chain = chain_index()
    if level == LEVELS:
        return bit(chain, LEVELS - 1) == 0
    return bit(chain, level - 1) == bit(chain, level)


def nn(left, right, precision=None):
    return lax.dot_general(
        left, right, (((1,), (0,)), ((), ())), precision=precision, preferred_element_type=f32
    )


def nt(left, right, precision=None):
    return lax.dot_general(
        left, right, (((1,), (1,)), ((), ())), precision=precision, preferred_element_type=f32
    )


def halves(left, right, precision=None):
    half = left.shape[0] // 2
    return jnp.concatenate(
        [nn(left[:half], right, precision), nn(left[half:], right, precision)], axis=0
    )


def split(value):
    upper = value.astype(bf16)
    return upper, (value - upper.astype(f32)).astype(bf16)


def three_pass(left, right, dot=nn):
    lh, ll = left
    rh, rl = right
    return dot(lh, rh) + (dot(lh, rl) + dot(ll, rh))


def inverse_into(matrix, out_ref, squarings=5):
    order = matrix.shape[0]
    rows = lax.broadcasted_iota(jnp.int32, (order, order), 0)
    identity = (rows == lax.broadcasted_iota(jnp.int32, (order, order), 1)).astype(f32)
    norm = jnp.max(jnp.sum(jnp.abs(matrix), axis=0, keepdims=True), axis=1, keepdims=True)
    scale = 1.75 / norm
    rest = identity - matrix * scale
    found = (identity + rest) * scale
    rest = rest.astype(bf16)
    rest = halves(rest, rest).astype(bf16)
    for step in range(1, squarings):
        found = found + halves(found.astype(bf16), rest)
        if step < squarings - 1:
            rest = halves(rest, rest).astype(bf16)
    upper = split(found)
    rest = identity - three_pass(split(matrix), upper, halves)
    found = found + halves(upper[0], rest.astype(bf16))
    rest = identity - halves(matrix, found, HIGH)
    miss = jnp.sum(rest * rest)
    out_ref[...] = found + three_pass(split(found), split(rest), halves)

    @pl.when(jnp.logical_not(miss < TOLERANCE * TOLERANCE))
    def _():
        near = jnp.logical_and(miss < 0.25, scale > 0.0)
        out_ref[...] = jnp.where(near, out_ref[...], identity * scale)

        def unfinished(state):
            step, miss_now = state
            return jnp.logical_and(step < 64, miss_now >= TOLERANCE * TOLERANCE)

        def improve(state):
            now = out_ref[...]
            gap = identity - halves(matrix, now, HIGH)
            out_ref[...] = now + halves(now, gap, HIGH)
            return state[0] + 1, jnp.sum(gap * gap)

        lax.while_loop(unfinished, improve, (jnp.int32(0), jnp.float32(jnp.inf)))


HALF = 128
PACKED = HALF + 8


def on_first_core():
    return lax.rem(lax.axis_index("run"), 2) == 0


def ordered(direct, swapped):
    first = on_first_core()
    return jnp.where(first, direct, swapped), jnp.where(first, swapped, direct)


def triangle():
    rows = lax.broadcasted_iota(jnp.int32, (HALF, HALF), 0)
    columns = lax.broadcasted_iota(jnp.int32, (HALF, HALF), 1)
    return rows, columns


def pack_symmetric(value, first):
    rows, columns = triangle()
    upper_left, lower_right = value[:HALF, :HALF], value[HALF:, HALF:]
    diagonal = jnp.sum(jnp.where(rows == columns, lower_right, 0.0), axis=0, keepdims=True)
    both = jnp.where(rows >= columns, upper_left, lower_right)
    lower_left = value[HALF:, :HALF]
    main = (lower_left if first else both) if isinstance(first, bool) else jnp.where(first, lower_left, both)
    return main, jnp.broadcast_to(diagonal, (8, HALF))


def unpack_symmetric(from_first, from_second):
    rows, columns = triangle()
    lower_left, diagonal = from_first[:HALF], from_first[HALF : HALF + 1]
    both = from_second[:HALF]
    turned = both.T
    upper_left = jnp.where(rows >= columns, both, turned)
    lower_right = jnp.where(rows < columns, both, turned)
    lower_right = jnp.where(rows == columns, diagonal, lower_right)
    return jnp.concatenate(
        [
            jnp.concatenate([upper_left, lower_left.T], axis=1),
            jnp.concatenate([lower_left, lower_right], axis=1),
        ],
        axis=0,
    )


def send_separator(value, send):
    main, diagonal = pack_symmetric(value, on_first_core())
    send[:HALF, :] = main
    send[HALF:, :] = diagonal


def send_link(link, outer, send):
    first = on_first_core()
    rows = jnp.where(first, link[:HALF], link[HALF:])
    send[:HALF, :] = rows[:, :HALF]
    send[HALF : 2 * HALF, :] = rows[:, HALF:]
    main, diagonal = pack_symmetric(outer, first)
    send[2 * HALF : 3 * HALF, :] = main
    send[3 * HALF :, :] = diagonal


def received_separator(refs):
    if len(refs) == 1:
        value = refs[0][...]
        return value if value.shape[1] > HALF else unpack_symmetric(value[:PACKED], value[PACKED:])
    return unpack_symmetric(*ordered(refs[0][...], refs[1][...]))


def received_link(refs):
    if len(refs) == 1:
        order = refs[0].shape[1]
        return refs[0][:order, :], refs[0][order:, :]
    upper, lower = ordered(refs[0][...], refs[1][...])
    link = jnp.concatenate(
        [
            jnp.concatenate([upper[:HALF], upper[HALF : 2 * HALF]], axis=1),
            jnp.concatenate([lower[:HALF], lower[HALF : 2 * HALF]], axis=1),
        ],
        axis=0,
    )
    return link, unpack_symmetric(upper[2 * HALF :], lower[2 * HALF :])


def first_invert_kernel(diag, inv):
    inverse_into(diag[0], inv)


def first_merge_kernel(inv, diag, couple, gain_own, gain_other, ss, ps):
    order = inv.shape[0]
    start = chain_index() == 0
    above = jnp.where(start, 0.0, couple[0]).T
    below = couple[1]
    inverse = inv[...]
    gain_above = nn(above, inverse, HIGH)
    gain_below = nn(below, inverse, HIGH)
    own_above = -nt(gain_above, above, HIGH)
    own_below = diag[1] - nt(gain_below, below, HIGH)
    link = -nt(gain_above, below, HIGH)
    left = on_first_core()
    gain_own[...] = jnp.where(left, gain_above, gain_below)
    gain_other[...] = jnp.where(left, gain_below, gain_above)
    ss[...] = jnp.where(left, own_below, own_above)
    ps[order:, :] = jnp.where(left, own_above, own_below)
    ps[:order, :] = jnp.where(left, link, link.T)


def first_sources_kernel(source, inv, gain_own, gain_other, _, sources, partial):
    columns = partial.shape[1]
    held = source[0]
    left = on_first_core()
    sources[:, :columns] = jnp.where(left, 0.0, source[1]) - nn(gain_own[...], held, HIGH)
    sources[:, columns:] = jnp.where(left, source[1], 0.0) - nn(gain_other[...], held, HIGH)
    partial[...] = nn(inv[...], held, HIGH)


def first_factors_kernel(gain_own, gain_other, partial, _, factors, offset):
    order, columns = partial.shape
    rows = lax.broadcasted_iota(jnp.int32, (order, order), 0)
    identity = (rows == lax.broadcasted_iota(jnp.int32, (order, order), 1)).astype(f32)
    left = on_first_core()
    factors[0, :order, :] = gain_own[...].T
    factors[1, :order, :] = gain_other[...].T
    factors[0, order:, :] = jnp.where(left, 0.0, -identity)
    factors[1, order:, :] = jnp.where(left, -identity, 0.0)
    offset[:order, :] = partial[...]
    offset[order:, :] = jnp.zeros((order, columns), f32)


def invert_kernel(squarings, own_ss, _, *refs):
    inverse_into(own_ss[...] + received_separator(refs[:-1]), refs[-1], squarings)


def store_element(stays, own, other, cross, ss, ps, sends):
    order = cross.shape[0]
    separator = jnp.where(stays, other, own)
    outer = jnp.where(stays, own, other)
    link = jnp.where(stays, cross, cross.T)
    ss[...] = separator
    ps[order:, :] = outer
    ps[:order, :] = link
    if sends:
        send_separator(separator, sends[0])
        send_link(link, outer, sends[1])


def pair_kernel(level, inv, own_ps, other_ps, gain_own, gain_other, ss, ps, *sends):
    order = inv.shape[0]
    stays = own_stays(level)
    inverse = inv[...]
    link_own, link_other = own_ps[:order, :], other_ps[:order, :]
    own_gain = nn(link_own, inverse, HIGH)
    other_gain = nn(link_other, inverse, HIGH)
    gain_own[...] = own_gain
    gain_other[...] = other_gain
    own = own_ps[order:, :] - nt(own_gain, link_own, HIGH)
    other = other_ps[order:, :] - nt(other_gain, link_other, HIGH)
    cross = -nt(own_gain, link_other, HIGH)
    store_element(stays, own, other, cross, ss, ps, sends)


def pass_kernel(_, arrived, passed):
    passed[...] = arrived[...]


def own_kernel(inv, own_ps, _, gain_own, reduced_own):
    order = inv.shape[0]
    link_own = own_ps[:order, :]
    gain_own[...] = nn(link_own, inv[...], HIGH)
    reduced_own[...] = own_ps[order:, :] - nt(gain_own[...], link_own, HIGH)


def merge_kernel(level, count, inv, gain_own, reduced_own, *refs):
    others, (gain_other, ss, ps, *sends) = refs[:count], refs[count:]
    order = inv.shape[0]
    stays = own_stays(level)
    link_other, outer_other = received_link(others)
    gain = nn(link_other, inv[...], HIGH)
    gain_other[...] = gain
    cross = -nt(gain_own[...], link_other, HIGH)
    reduced_other = outer_other - nt(gain, link_other, HIGH)
    store_element(stays, reduced_own[...], reduced_other, cross, ss, ps, sends)


def sources_step(level, inv, gain_own, gain_other, own_f, other_f):
    columns = own_f.shape[1] // 2
    stays = own_stays(level)
    own, other = own_f[...], other_f[...]
    held = own[:, columns:] + other[:, columns:]
    after_own = own[:, :columns] - halves(gain_own[...], held, HIGH)
    after_other = other[:, :columns] - halves(gain_other[...], held, HIGH)
    partial = halves(inv[...], held, HIGH)
    return jnp.where(stays, after_own, after_other), jnp.where(stays, after_other, after_own), partial


def sources_kernel(level, inv, gain_own, gain_other, own_f, other_f, _, sources, partial):
    columns = partial.shape[1]
    outer, inner, found = sources_step(level, inv, gain_own, gain_other, own_f, other_f)
    sources[:, :columns] = outer
    sources[:, columns:] = inner
    partial[...] = found


def factors_step(level, gain_own, gain_other, partial, factors, offset):
    stays = own_stays(level)
    inner = split(factors[1])
    new_offset = offset[...] - three_pass(inner, split(partial[...]))
    own_end = factors[0] - three_pass(inner, split(gain_own[...]), nt)
    other_end = -three_pass(inner, split(gain_other[...]), nt)
    return jnp.where(stays, own_end, other_end), jnp.where(stays, other_end, own_end), new_offset


def factors_kernel(level, gain_own, gain_other, partial, _, factors, offset, new_factors, new_offset):
    outer, inner, moved = factors_step(level, gain_own, gain_other, partial, factors, offset)
    new_factors[0] = outer
    new_factors[1] = inner
    new_offset[...] = moved


def end_kernel(ss, ps, end_inv, end_gain, new_ss, send_ss):
    order = ss.shape[0]
    rows = lax.broadcasted_iota(jnp.int32, (order, order), 0)
    identity = (rows == lax.broadcasted_iota(jnp.int32, (order, order), 1)).astype(f32)
    right = bit(chain_index(), LEVELS - 1) == 1
    inverse_into(jnp.where(right, ps[order:, :], identity), end_inv, 6)
    turned = ps[:order, :].T
    gain = halves(turned, end_inv[...], HIGH)
    end_gain[...] = gain
    separator = ss[...] - halves(gain, ps[:order, :], HIGH)
    new_ss[...] = separator
    for place, first in ((0, True), (PACKED, False)):
        main, diagonal = pack_symmetric(separator, first)
        send_ss[place : place + HALF, :] = main
        send_ss[place + HALF : place + PACKED, :] = diagonal


def end_sources_kernel(
    level, inv, gain_own, gain_other, own_f, other_f, end_inv, end_gain, _, sources, partial, end_partial
):
    outer, inner, found = sources_step(level, inv, gain_own, gain_other, own_f, other_f)
    sources[...] = inner - halves(end_gain[...], outer, HIGH)
    partial[...] = found
    end_partial[...] = halves(end_inv[...], outer, HIGH)


def end_factors_kernel(
    level, gain_own, gain_other, partial, _, factors, offset, end_gain, end_partial,
    new_factors, new_offset,
):
    outer, inner, moved = factors_step(level, gain_own, gain_other, partial, factors, offset)
    outer = split(outer)
    new_offset[...] = moved - three_pass(outer, split(end_partial[...]))
    new_factors[...] = inner - three_pass(outer, split(end_gain[...]), nt)


def back_kernel(inv, own_f, other_f, factors, offset, result):
    order = inv.shape[0]
    middle = halves(inv[...], own_f[...] + other_f[...], HIGH)
    both = offset[...] - three_pass(split(factors[...]), split(middle), halves)
    result[0] = both[:order]
    result[1] = both[order:]


WEIGHTS = {"invert": 0.85, "own": 0.1, "merge": 0.1, "sources": 0.3, "factors": 0.1, "pass": 0.05, "end": 0.1, "begin": 4.0, "tail": 0.1, "last": 0.1, "first": 2.0}


def call(kernel, name, operands, shapes):
    vmem = pl.BlockSpec(memory_space=pltpu.VMEM)
    flops = int(WEIGHTS[name.split("_")[0]] * 1e9)
    return pl.pallas_call(
        kernel,
        out_shape=[jax.ShapeDtypeStruct(shape, f32) for shape in shapes],
        in_specs=[vmem] * len(operands),
        out_specs=[vmem] * len(shapes),
        name=name,
        compiler_params=pltpu.CompilerParams(vmem_limit_bytes=40 << 20),
        cost_estimate=pl.CostEstimate(flops=flops, bytes_accessed=4096, transcendentals=0),
    )(*operands)


def local(diag_blocks, coupling, rhs):
    order, columns = rhs.shape[2:]
    square, tall = (order, order), (2 * order, order)
    small, medium = (PACKED, HALF), (2 * HALF + PACKED, HALF)
    flat, slim = (order, 2 * columns), (order, columns)
    double, long = (2, 2 * order, order), (2 * order, columns)
    (inv,) = call(first_invert_kernel, "first_invert", (diag_blocks[0],), (square,))
    gain_own, gain_other, ss, ps = call(
        first_merge_kernel, "first_merge", (inv, diag_blocks[0], coupling[0]),
        (square, square, square, tall)
    )
    others_ss = (exchange(ss, 1),)
    others_ps = (exchange(ps, 1),)
    sources, partial = call(
        first_sources_kernel, "first_sources", (rhs[0], inv, gain_own, gain_other, ss),
        (flat, slim)
    )
    other_f = exchange(sources, 1)
    factors, offset = call(
        first_factors_kernel, "first_factors", (gain_own, gain_other, partial, ss),
        (double, long)
    )

    def swapped(direct, after, name):
        (passed,) = call(pass_kernel, name, (after, direct), (direct.shape,))
        return (direct, exchange(passed, 1))

    for level in range(1, LEVELS):
        last = level == LEVELS - 1
        (inv,) = call(
            functools.partial(invert_kernel, SQUARINGS[level]), "begin" if level == 1 else f"invert_{level}",
            (ss, offset) + others_ss, (square,)
        )
        if level > 1:
            others_ps = swapped(direct_ps, inv, f"pass_ps_{level}")
            gain_own, reduced_own = call(
                own_kernel, f"own_{level}", (inv, ps, others_ps[0]), (square, square)
            )
            gain_other, ss, ps, *sends = call(
                functools.partial(merge_kernel, level, len(others_ps)), f"merge_{level}",
                (inv, gain_own, reduced_own) + others_ps,
                (square, square, tall) + (() if last else (small, medium)),
            )
        else:
            gain_own, gain_other, ss, ps, *sends = call(
                functools.partial(pair_kernel, level), f"merge_{level}", (inv, ps) + others_ps,
                (square, square, square, tall, small, medium),
            )
        if last:
            end_inv, end_gain, ss, send_ss = call(
                end_kernel, "end", (ss, ps), (square, square, square, (2 * PACKED, HALF))
            )
        else:
            send_ss, send_ps = sends
        direct_ss = exchange(send_ss, level + 1)
        held = (inv, gain_own, gain_other, sources, other_f)
        if last:
            sources, partial, end_partial = call(
                functools.partial(end_sources_kernel, level), "tail_sources",
                held + (end_inv, end_gain, send_ss), (slim, slim, slim)
            )
        else:
            direct_ps = exchange(send_ps, level + 1)
            sources, partial = call(
                functools.partial(sources_kernel, level), f"sources_{level}",
                held + (send_ss,), (flat, slim)
            )
        other_f = exchange(sources, level + 1)
        before = (gain_own, gain_other, partial, send_ss, factors, offset)
        if last:
            factors, offset = call(
                functools.partial(end_factors_kernel, level), "tail_factors",
                before + (end_gain, end_partial), (tall, long)
            )
        else:
            factors, offset = call(
                functools.partial(factors_kernel, level), f"factors_{level}", before,
                (double, long)
            )
        others_ss = (direct_ss,) if last else swapped(direct_ss, offset, f"pass_ss_{level + 1}")
    (inv,) = call(
        functools.partial(invert_kernel, SQUARINGS[LEVELS]), "last_invert", (ss, offset) + others_ss,
        (square,)
    )
    (result,) = call(
        back_kernel, "tail_back", (inv, sources, other_f, factors, offset), ((2, order, columns),)
    )
    return result[None]


def solution(mesh):
    spec = P("seg", "run", None, None)
    return jax.shard_map(
        local, mesh=mesh, in_specs=(spec, spec, spec), out_specs=spec, check_vma=False
    )
```

```python
import functools

import jax
import jax.numpy as jnp
from jax import lax
from jax.experimental import pallas as pl
from jax.experimental.pallas import tpu as pltpu
from jax.sharding import PartitionSpec as P

HIGH = lax.Precision.HIGHEST
f32 = jnp.float32
bf16 = jnp.bfloat16
LEVELS = 7
TOLERANCE = 4e-3
SQUARINGS = (5, 4, 4, 3, 2, 2, 2, 2)
AXES = ("run", "seg")


def chain_coords(flat):
    run, seg = flat >> 3, flat & 7
    return seg >> 1, ((seg & 1) << 1) | (run >> 3), (run >> 1) & 3, run & 1


def flat_index(x, z, y, core):
    return ((((z & 1) << 3) | (y << 1) | core) << 3) | (x << 1) | (z >> 1)


def partner(level, flat):
    x, z, y, core = chain_coords(flat)
    if level == 1:
        core = core ^ 1
    elif level == 2:
        y = y ^ 1
    elif level == 3:
        y = 3 - y
    elif level == 4:
        z = z ^ 1
    elif level == 5:
        z = 3 - z
    elif level == 6:
        x = x ^ 1
    else:
        x = 3 - x
    return flat_index(x, z, y, core)


def exchange(value, level):
    return lax.ppermute(value, AXES, [(flat, partner(level, flat)) for flat in range(128)])


def chain_index():
    run, seg = lax.axis_index("run"), lax.axis_index("seg")
    return seg * 16 + run


def bit(value, place):
    return lax.rem(lax.div(value, 1 << place), 2)


def own_stays(level):
    chain = chain_index()
    if level == LEVELS:
        return bit(chain, LEVELS - 1) == 0
    return bit(chain, level - 1) == bit(chain, level)


def nn(left, right, precision=None):
    return lax.dot_general(
        left, right, (((1,), (0,)), ((), ())), precision=precision, preferred_element_type=f32
    )


def nt(left, right, precision=None):
    return lax.dot_general(
        left, right, (((1,), (1,)), ((), ())), precision=precision, preferred_element_type=f32
    )


def halves(left, right, precision=None):
    half = left.shape[0] // 2
    return jnp.concatenate(
        [nn(left[:half], right, precision), nn(left[half:], right, precision)], axis=0
    )


def split(value):
    upper = value.astype(bf16)
    return upper, (value - upper.astype(f32)).astype(bf16)


def three_pass(left, right, dot=nn):
    lh, ll = left
    rh, rl = right
    return dot(lh, rh) + (dot(lh, rl) + dot(ll, rh))


def inverse_into(matrix, out_ref, squarings=5):
    order = matrix.shape[0]
    rows = lax.broadcasted_iota(jnp.int32, (order, order), 0)
    identity = (rows == lax.broadcasted_iota(jnp.int32, (order, order), 1)).astype(f32)
    norm = jnp.max(jnp.sum(jnp.abs(matrix), axis=0, keepdims=True), axis=1, keepdims=True)
    scale = 1.75 / norm
    rest = identity - matrix * scale
    found = (identity + rest) * scale
    rest = rest.astype(bf16)
    rest = halves(rest, rest).astype(bf16)
    for step in range(1, squarings):
        found = found + halves(found.astype(bf16), rest)
        if step < squarings - 1:
            rest = halves(rest, rest).astype(bf16)
    upper = split(found)
    rest = identity - three_pass(split(matrix), upper, halves)
    found = found + halves(upper[0], rest.astype(bf16))
    rest = identity - halves(matrix, found, HIGH)
    miss = jnp.sum(rest * rest)
    out_ref[...] = found + three_pass(split(found), split(rest), halves)

    @pl.when(jnp.logical_not(miss < TOLERANCE * TOLERANCE))
    def _():
        near = jnp.logical_and(miss < 0.25, scale > 0.0)
        out_ref[...] = jnp.where(near, out_ref[...], identity * scale)

        def unfinished(state):
            step, miss_now = state
            return jnp.logical_and(step < 64, miss_now >= TOLERANCE * TOLERANCE)

        def improve(state):
            now = out_ref[...]
            gap = identity - halves(matrix, now, HIGH)
            out_ref[...] = now + halves(now, gap, HIGH)
            return state[0] + 1, jnp.sum(gap * gap)

        lax.while_loop(unfinished, improve, (jnp.int32(0), jnp.float32(jnp.inf)))


HALF = 128
PACKED = HALF + 8


def on_first_core():
    return lax.rem(lax.axis_index("run"), 2) == 0


def ordered(direct, swapped):
    first = on_first_core()
    return jnp.where(first, direct, swapped), jnp.where(first, swapped, direct)


def triangle():
    rows = lax.broadcasted_iota(jnp.int32, (HALF, HALF), 0)
    columns = lax.broadcasted_iota(jnp.int32, (HALF, HALF), 1)
    return rows, columns


def pack_symmetric(value, first):
    rows, columns = triangle()
    upper_left, lower_right = value[:HALF, :HALF], value[HALF:, HALF:]
    diagonal = jnp.sum(jnp.where(rows == columns, lower_right, 0.0), axis=0, keepdims=True)
    both = jnp.where(rows >= columns, upper_left, lower_right)
    lower_left = value[HALF:, :HALF]
    main = (lower_left if first else both) if isinstance(first, bool) else jnp.where(first, lower_left, both)
    return main, jnp.broadcast_to(diagonal, (8, HALF))


def unpack_symmetric(from_first, from_second):
    rows, columns = triangle()
    lower_left, diagonal = from_first[:HALF], from_first[HALF : HALF + 1]
    both = from_second[:HALF]
    turned = both.T
    upper_left = jnp.where(rows >= columns, both, turned)
    lower_right = jnp.where(rows < columns, both, turned)
    lower_right = jnp.where(rows == columns, diagonal, lower_right)
    return jnp.concatenate(
        [
            jnp.concatenate([upper_left, lower_left.T], axis=1),
            jnp.concatenate([lower_left, lower_right], axis=1),
        ],
        axis=0,
    )


def send_separator(value, send):
    main, diagonal = pack_symmetric(value, on_first_core())
    send[:HALF, :] = main
    send[HALF:, :] = diagonal


def send_link(link, outer, send):
    first = on_first_core()
    rows = jnp.where(first, link[:HALF], link[HALF:])
    send[:HALF, :] = rows[:, :HALF]
    send[HALF : 2 * HALF, :] = rows[:, HALF:]
    main, diagonal = pack_symmetric(outer, first)
    send[2 * HALF : 3 * HALF, :] = main
    send[3 * HALF :, :] = diagonal


def received_separator(refs):
    if len(refs) == 1:
        value = refs[0][...]
        return value if value.shape[1] > HALF else unpack_symmetric(value[:PACKED], value[PACKED:])
    return unpack_symmetric(*ordered(refs[0][...], refs[1][...]))


def received_link(refs):
    if len(refs) == 1:
        order = refs[0].shape[1]
        return refs[0][:order, :], refs[0][order:, :]
    upper, lower = ordered(refs[0][...], refs[1][...])
    link = jnp.concatenate(
        [
            jnp.concatenate([upper[:HALF], upper[HALF : 2 * HALF]], axis=1),
            jnp.concatenate([lower[:HALF], lower[HALF : 2 * HALF]], axis=1),
        ],
        axis=0,
    )
    return link, unpack_symmetric(upper[2 * HALF :], lower[2 * HALF :])


def first_invert_kernel(diag, inv):
    inverse_into(diag[0], inv)


def first_merge_kernel(inv, diag, couple, gain_own, gain_other, ss, ps):
    order = inv.shape[0]
    start = chain_index() == 0
    above = jnp.where(start, 0.0, couple[0]).T
    below = couple[1]
    inverse = inv[...]
    gain_above = nn(above, inverse, HIGH)
    gain_below = nn(below, inverse, HIGH)
    own_above = -nt(gain_above, above, HIGH)
    own_below = diag[1] - nt(gain_below, below, HIGH)
    link = -nt(gain_above, below, HIGH)
    left = on_first_core()
    gain_own[...] = jnp.where(left, gain_above, gain_below)
    gain_other[...] = jnp.where(left, gain_below, gain_above)
    ss[...] = jnp.where(left, own_below, own_above)
    ps[order:, :] = jnp.where(left, own_above, own_below)
    ps[:order, :] = jnp.where(left, link, link.T)


def first_sources_kernel(source, inv, gain_own, gain_other, _, sources, partial):
    columns = partial.shape[1]
    held = source[0]
    left = on_first_core()
    sources[:, :columns] = jnp.where(left, 0.0, source[1]) - nn(gain_own[...], held, HIGH)
    sources[:, columns:] = jnp.where(left, source[1], 0.0) - nn(gain_other[...], held, HIGH)
    partial[...] = nn(inv[...], held, HIGH)


def first_factors_kernel(gain_own, gain_other, partial, _, factors, offset):
    order, columns = partial.shape
    rows = lax.broadcasted_iota(jnp.int32, (order, order), 0)
    identity = (rows == lax.broadcasted_iota(jnp.int32, (order, order), 1)).astype(f32)
    left = on_first_core()
    factors[0, :order, :] = gain_own[...].T
    factors[1, :order, :] = gain_other[...].T
    factors[0, order:, :] = jnp.where(left, 0.0, -identity)
    factors[1, order:, :] = jnp.where(left, -identity, 0.0)
    offset[:order, :] = partial[...]
    offset[order:, :] = jnp.zeros((order, columns), f32)


def invert_kernel(squarings, own_ss, _, *refs):
    inverse_into(own_ss[...] + received_separator(refs[:-1]), refs[-1], squarings)


def store_element(stays, own, other, cross, ss, ps, sends):
    order = cross.shape[0]
    separator = jnp.where(stays, other, own)
    outer = jnp.where(stays, own, other)
    link = jnp.where(stays, cross, cross.T)
    ss[...] = separator
    ps[order:, :] = outer
    ps[:order, :] = link
    if sends:
        send_separator(separator, sends[0])
        send_link(link, outer, sends[1])


def pair_kernel(level, inv, own_ps, other_ps, gain_own, gain_other, ss, ps, *sends):
    order = inv.shape[0]
    stays = own_stays(level)
    inverse = inv[...]
    link_own, link_other = own_ps[:order, :], other_ps[:order, :]
    own_gain = nn(link_own, inverse, HIGH)
    other_gain = nn(link_other, inverse, HIGH)
    gain_own[...] = own_gain
    gain_other[...] = other_gain
    own = own_ps[order:, :] - nt(own_gain, link_own, HIGH)
    other = other_ps[order:, :] - nt(other_gain, link_other, HIGH)
    cross = -nt(own_gain, link_other, HIGH)
    store_element(stays, own, other, cross, ss, ps, sends)


def pass_kernel(_, arrived, passed):
    passed[...] = arrived[...]


def own_kernel(inv, own_ps, _, gain_own, reduced_own):
    order = inv.shape[0]
    link_own = own_ps[:order, :]
    gain_own[...] = nn(link_own, inv[...], HIGH)
    reduced_own[...] = own_ps[order:, :] - nt(gain_own[...], link_own, HIGH)


def merge_kernel(level, count, inv, gain_own, reduced_own, *refs):
    others, (gain_other, ss, ps, *sends) = refs[:count], refs[count:]
    order = inv.shape[0]
    stays = own_stays(level)
    link_other, outer_other = received_link(others)
    gain = nn(link_other, inv[...], HIGH)
    gain_other[...] = gain
    cross = -nt(gain_own[...], link_other, HIGH)
    reduced_other = outer_other - nt(gain, link_other, HIGH)
    store_element(stays, reduced_own[...], reduced_other, cross, ss, ps, sends)


def sources_step(level, inv, gain_own, gain_other, own_f, other_f):
    columns = own_f.shape[1] // 2
    stays = own_stays(level)
    own, other = own_f[...], other_f[...]
    held = own[:, columns:] + other[:, columns:]
    after_own = own[:, :columns] - halves(gain_own[...], held, HIGH)
    after_other = other[:, :columns] - halves(gain_other[...], held, HIGH)
    partial = halves(inv[...], held, HIGH)
    return jnp.where(stays, after_own, after_other), jnp.where(stays, after_other, after_own), partial


def sources_kernel(level, inv, gain_own, gain_other, own_f, other_f, _, sources, partial):
    columns = partial.shape[1]
    outer, inner, found = sources_step(level, inv, gain_own, gain_other, own_f, other_f)
    sources[:, :columns] = outer
    sources[:, columns:] = inner
    partial[...] = found


def factors_step(level, gain_own, gain_other, partial, factors, offset):
    stays = own_stays(level)
    inner = split(factors[1])
    new_offset = offset[...] - three_pass(inner, split(partial[...]))
    own_end = factors[0] - three_pass(inner, split(gain_own[...]), nt)
    other_end = -three_pass(inner, split(gain_other[...]), nt)
    return jnp.where(stays, own_end, other_end), jnp.where(stays, other_end, own_end), new_offset


def factors_kernel(level, gain_own, gain_other, partial, _, factors, offset, new_factors, new_offset):
    outer, inner, moved = factors_step(level, gain_own, gain_other, partial, factors, offset)
    new_factors[0] = outer
    new_factors[1] = inner
    new_offset[...] = moved


def end_kernel(ss, ps, end_inv, end_gain, new_ss, send_ss):
    order = ss.shape[0]
    rows = lax.broadcasted_iota(jnp.int32, (order, order), 0)
    identity = (rows == lax.broadcasted_iota(jnp.int32, (order, order), 1)).astype(f32)
    right = bit(chain_index(), LEVELS - 1) == 1
    inverse_into(jnp.where(right, ps[order:, :], identity), end_inv, 6)
    turned = ps[:order, :].T
    gain = halves(turned, end_inv[...], HIGH)
    end_gain[...] = gain
    separator = ss[...] - halves(gain, ps[:order, :], HIGH)
    new_ss[...] = separator
    send_separator(separator, send_ss)


def end_sources_kernel(
    level, inv, gain_own, gain_other, own_f, other_f, end_inv, end_gain, _, sources, partial, end_partial
):
    outer, inner, found = sources_step(level, inv, gain_own, gain_other, own_f, other_f)
    sources[...] = inner - halves(end_gain[...], outer, HIGH)
    partial[...] = found
    end_partial[...] = halves(end_inv[...], outer, HIGH)


def end_factors_kernel(
    level, gain_own, gain_other, partial, _, factors, offset, end_gain, end_partial,
    new_factors, new_offset,
):
    outer, inner, moved = factors_step(level, gain_own, gain_other, partial, factors, offset)
    outer = split(outer)
    new_offset[...] = moved - three_pass(outer, split(end_partial[...]))
    new_factors[...] = inner - three_pass(outer, split(end_gain[...]), nt)


def back_kernel(inv, own_f, other_f, factors, offset, result):
    order = inv.shape[0]
    middle = halves(inv[...], own_f[...] + other_f[...], HIGH)
    both = offset[...] - three_pass(split(factors[...]), split(middle), halves)
    result[0] = both[:order]
    result[1] = both[order:]


WEIGHTS = {"invert": 0.85, "own": 0.1, "merge": 0.1, "sources": 0.3, "factors": 0.1, "pass": 0.05, "end": 0.1, "begin": 4.0, "tail": 0.1, "last": 0.1, "first": 2.0}


def call(kernel, name, operands, shapes):
    vmem = pl.BlockSpec(memory_space=pltpu.VMEM)
    flops = int(WEIGHTS[name.split("_")[0]] * 1e9)
    return pl.pallas_call(
        kernel,
        out_shape=[jax.ShapeDtypeStruct(shape, f32) for shape in shapes],
        in_specs=[vmem] * len(operands),
        out_specs=[vmem] * len(shapes),
        name=name,
        compiler_params=pltpu.CompilerParams(vmem_limit_bytes=40 << 20),
        cost_estimate=pl.CostEstimate(flops=flops, bytes_accessed=4096, transcendentals=0),
    )(*operands)


def local(diag_blocks, coupling, rhs):
    order, columns = rhs.shape[2:]
    square, tall = (order, order), (2 * order, order)
    small, medium = (PACKED, HALF), (2 * HALF + PACKED, HALF)
    flat, slim = (order, 2 * columns), (order, columns)
    double, long = (2, 2 * order, order), (2 * order, columns)
    (inv,) = call(first_invert_kernel, "first_invert", (diag_blocks[0],), (square,))
    gain_own, gain_other, ss, ps = call(
        first_merge_kernel, "first_merge", (inv, diag_blocks[0], coupling[0]),
        (square, square, square, tall)
    )
    others_ss = (exchange(ss, 1),)
    others_ps = (exchange(ps, 1),)
    sources, partial = call(
        first_sources_kernel, "first_sources", (rhs[0], inv, gain_own, gain_other, ss),
        (flat, slim)
    )
    other_f = exchange(sources, 1)
    factors, offset = call(
        first_factors_kernel, "first_factors", (gain_own, gain_other, partial, ss),
        (double, long)
    )

    def swapped(direct, after, name):
        (passed,) = call(pass_kernel, name, (after, direct), (direct.shape,))
        return (direct, exchange(passed, 1))

    for level in range(1, LEVELS):
        last = level == LEVELS - 1
        (inv,) = call(
            functools.partial(invert_kernel, SQUARINGS[level]), "begin" if level == 1 else f"invert_{level}",
            (ss, offset) + others_ss, (square,)
        )
        if level > 1:
            others_ps = swapped(direct_ps, inv, f"pass_ps_{level}")
            gain_own, reduced_own = call(
                own_kernel, f"own_{level}", (inv, ps, others_ps[0]), (square, square)
            )
            gain_other, ss, ps, *sends = call(
                functools.partial(merge_kernel, level, len(others_ps)), f"merge_{level}",
                (inv, gain_own, reduced_own) + others_ps,
                (square, square, tall) + (() if last else (small, medium)),
            )
        else:
            gain_own, gain_other, ss, ps, *sends = call(
                functools.partial(pair_kernel, level), f"merge_{level}", (inv, ps) + others_ps,
                (square, square, square, tall, small, medium),
            )
        if last:
            end_inv, end_gain, ss, send_ss = call(
                end_kernel, "end", (ss, ps), (square, square, square, small)
            )
        else:
            send_ss, send_ps = sends
        direct_ss = exchange(send_ss, level + 1)
        held = (inv, gain_own, gain_other, sources, other_f)
        if last:
            sources, partial, end_partial = call(
                functools.partial(end_sources_kernel, level), "tail_sources",
                held + (end_inv, end_gain, send_ss), (slim, slim, slim)
            )
        else:
            direct_ps = exchange(send_ps, level + 1)
            sources, partial = call(
                functools.partial(sources_kernel, level), f"sources_{level}",
                held + (send_ss,), (flat, slim)
            )
        other_f = exchange(sources, level + 1)
        before = (gain_own, gain_other, partial, direct_ss if last else send_ss, factors, offset)
        if last:
            factors, offset = call(
                functools.partial(end_factors_kernel, level), "tail_factors",
                before + (end_gain, end_partial), (tall, long)
            )
        else:
            factors, offset = call(
                functools.partial(factors_kernel, level), f"factors_{level}", before,
                (double, long)
            )
        others_ss = swapped(direct_ss, sources if last else offset, f"pass_ss_{level + 1}")
    (inv,) = call(
        functools.partial(invert_kernel, SQUARINGS[LEVELS]), "last_invert", (ss, offset) + others_ss,
        (square,)
    )
    (result,) = call(
        back_kernel, "tail_back", (inv, sources, other_f, factors, offset), ((2, order, columns),)
    )
    return result[None]


def solution(mesh):
    spec = P("seg", "run", None, None)
    return jax.shard_map(
        local, mesh=mesh, in_specs=(spec, spec, spec), out_specs=spec, check_vma=False
    )
```

```python
import functools

import jax
import jax.numpy as jnp
from jax import lax
from jax.experimental import pallas as pl
from jax.experimental.pallas import tpu as pltpu
from jax.sharding import PartitionSpec as P

HIGH = lax.Precision.HIGHEST
f32 = jnp.float32
bf16 = jnp.bfloat16
LEVELS = 7
TOLERANCE = 4e-3
SQUARINGS = (5, 4, 4, 3, 2, 2, 2, 2)
AXES = ("run", "seg")


def chain_coords(flat):
    run, seg = flat >> 3, flat & 7
    return seg >> 1, ((seg & 1) << 1) | (run >> 3), (run >> 1) & 3, run & 1


def flat_index(x, z, y, core):
    return ((((z & 1) << 3) | (y << 1) | core) << 3) | (x << 1) | (z >> 1)


def partner(level, flat):
    x, z, y, core = chain_coords(flat)
    if level == 1:
        core = core ^ 1
    elif level == 2:
        y = y ^ 1
    elif level == 3:
        y = 3 - y
    elif level == 4:
        z = z ^ 1
    elif level == 5:
        z = 3 - z
    elif level == 6:
        x = x ^ 1
    else:
        x = 3 - x
    return flat_index(x, z, y, core)


def exchange(value, level):
    return lax.ppermute(value, AXES, [(flat, partner(level, flat)) for flat in range(128)])


def chain_index():
    run, seg = lax.axis_index("run"), lax.axis_index("seg")
    return seg * 16 + run


def bit(value, place):
    return lax.rem(lax.div(value, 1 << place), 2)


def own_stays(level):
    chain = chain_index()
    if level == LEVELS:
        return bit(chain, LEVELS - 1) == 0
    return bit(chain, level - 1) == bit(chain, level)


def nn(left, right, precision=None):
    return lax.dot_general(
        left, right, (((1,), (0,)), ((), ())), precision=precision, preferred_element_type=f32
    )


def nt(left, right, precision=None):
    return lax.dot_general(
        left, right, (((1,), (1,)), ((), ())), precision=precision, preferred_element_type=f32
    )


def halves(left, right, precision=None):
    half = left.shape[0] // 2
    return jnp.concatenate(
        [nn(left[:half], right, precision), nn(left[half:], right, precision)], axis=0
    )


def split(value):
    upper = value.astype(bf16)
    return upper, (value - upper.astype(f32)).astype(bf16)


def three_pass(left, right, dot=nn):
    lh, ll = left
    rh, rl = right
    return dot(lh, rh) + (dot(lh, rl) + dot(ll, rh))


def inverse_into(matrix, out_ref, squarings=5):
    order = matrix.shape[0]
    rows = lax.broadcasted_iota(jnp.int32, (order, order), 0)
    identity = (rows == lax.broadcasted_iota(jnp.int32, (order, order), 1)).astype(f32)
    norm = jnp.max(jnp.sum(jnp.abs(matrix), axis=0, keepdims=True), axis=1, keepdims=True)
    scale = 1.75 / norm
    rest = identity - matrix * scale
    found = (identity + rest) * scale
    rest = rest.astype(bf16)
    rest = halves(rest, rest).astype(bf16)
    for step in range(1, squarings):
        found = found + halves(found.astype(bf16), rest)
        if step < squarings - 1:
            rest = halves(rest, rest).astype(bf16)
    upper = split(found)
    rest = identity - three_pass(split(matrix), upper, halves)
    found = found + halves(upper[0], rest.astype(bf16))
    rest = identity - halves(matrix, found, HIGH)
    miss = jnp.sum(rest * rest)
    out_ref[...] = found + three_pass(split(found), split(rest), halves)

    @pl.when(jnp.logical_not(miss < TOLERANCE * TOLERANCE))
    def _():
        near = jnp.logical_and(miss < 0.25, scale > 0.0)
        out_ref[...] = jnp.where(near, out_ref[...], identity * scale)

        def unfinished(state):
            step, miss_now = state
            return jnp.logical_and(step < 64, miss_now >= TOLERANCE * TOLERANCE)

        def improve(state):
            now = out_ref[...]
            gap = identity - halves(matrix, now, HIGH)
            out_ref[...] = now + halves(now, gap, HIGH)
            return state[0] + 1, jnp.sum(gap * gap)

        lax.while_loop(unfinished, improve, (jnp.int32(0), jnp.float32(jnp.inf)))


HALF = 128
PACKED = HALF + 8


def on_first_core():
    return lax.rem(lax.axis_index("run"), 2) == 0


def ordered(direct, swapped):
    first = on_first_core()
    return jnp.where(first, direct, swapped), jnp.where(first, swapped, direct)


def triangle():
    rows = lax.broadcasted_iota(jnp.int32, (HALF, HALF), 0)
    columns = lax.broadcasted_iota(jnp.int32, (HALF, HALF), 1)
    return rows, columns


def pack_symmetric(value, first):
    rows, columns = triangle()
    upper_left, lower_right = value[:HALF, :HALF], value[HALF:, HALF:]
    diagonal = jnp.sum(jnp.where(rows == columns, lower_right, 0.0), axis=0, keepdims=True)
    both = jnp.where(rows >= columns, upper_left, lower_right)
    lower_left = value[HALF:, :HALF]
    main = (lower_left if first else both) if isinstance(first, bool) else jnp.where(first, lower_left, both)
    return main, jnp.broadcast_to(diagonal, (8, HALF))


def unpack_symmetric(from_first, from_second):
    rows, columns = triangle()
    lower_left, diagonal = from_first[:HALF], from_first[HALF : HALF + 1]
    both = from_second[:HALF]
    turned = both.T
    upper_left = jnp.where(rows >= columns, both, turned)
    lower_right = jnp.where(rows < columns, both, turned)
    lower_right = jnp.where(rows == columns, diagonal, lower_right)
    return jnp.concatenate(
        [
            jnp.concatenate([upper_left, lower_left.T], axis=1),
            jnp.concatenate([lower_left, lower_right], axis=1),
        ],
        axis=0,
    )


def send_separator(value, send):
    main, diagonal = pack_symmetric(value, on_first_core())
    send[:HALF, :] = main
    send[HALF:, :] = diagonal


def send_link(link, outer, send):
    first = on_first_core()
    rows = jnp.where(first, link[:HALF], link[HALF:])
    send[:HALF, :] = rows[:, :HALF]
    send[HALF : 2 * HALF, :] = rows[:, HALF:]
    main, diagonal = pack_symmetric(outer, first)
    send[2 * HALF : 3 * HALF, :] = main
    send[3 * HALF :, :] = diagonal


def received_separator(refs):
    if len(refs) == 1:
        value = refs[0][...]
        return value if value.shape[1] > HALF else unpack_symmetric(value[:PACKED], value[PACKED:])
    return unpack_symmetric(*ordered(refs[0][...], refs[1][...]))


def received_link(refs):
    if len(refs) == 1:
        order = refs[0].shape[1]
        return refs[0][:order, :], refs[0][order:, :]
    upper, lower = ordered(refs[0][...], refs[1][...])
    link = jnp.concatenate(
        [
            jnp.concatenate([upper[:HALF], upper[HALF : 2 * HALF]], axis=1),
            jnp.concatenate([lower[:HALF], lower[HALF : 2 * HALF]], axis=1),
        ],
        axis=0,
    )
    return link, unpack_symmetric(upper[2 * HALF :], lower[2 * HALF :])


def first_invert_kernel(diag, inv):
    inverse_into(diag[0], inv)


def first_merge_kernel(inv, diag, couple, gain_own, gain_other, ss, ps):
    order = inv.shape[0]
    start = chain_index() == 0
    above = jnp.where(start, 0.0, couple[0]).T
    below = couple[1]
    inverse = inv[...]
    gain_above = nn(above, inverse, HIGH)
    gain_below = nn(below, inverse, HIGH)
    own_above = -nt(gain_above, above, HIGH)
    own_below = diag[1] - nt(gain_below, below, HIGH)
    link = -nt(gain_above, below, HIGH)
    left = on_first_core()
    gain_own[...] = jnp.where(left, gain_above, gain_below)
    gain_other[...] = jnp.where(left, gain_below, gain_above)
    ss[...] = jnp.where(left, own_below, own_above)
    ps[order:, :] = jnp.where(left, own_above, own_below)
    ps[:order, :] = jnp.where(left, link, link.T)


def first_sources_kernel(source, inv, gain_own, gain_other, _, sources, partial):
    columns = partial.shape[1]
    held = source[0]
    left = on_first_core()
    sources[:, :columns] = jnp.where(left, 0.0, source[1]) - nn(gain_own[...], held, HIGH)
    sources[:, columns:] = jnp.where(left, source[1], 0.0) - nn(gain_other[...], held, HIGH)
    partial[...] = nn(inv[...], held, HIGH)


def first_factors_kernel(gain_own, gain_other, partial, _, factors, offset):
    order, columns = partial.shape
    rows = lax.broadcasted_iota(jnp.int32, (order, order), 0)
    identity = (rows == lax.broadcasted_iota(jnp.int32, (order, order), 1)).astype(f32)
    left = on_first_core()
    factors[0, :order, :] = gain_own[...].T
    factors[1, :order, :] = gain_other[...].T
    factors[0, order:, :] = jnp.where(left, 0.0, -identity)
    factors[1, order:, :] = jnp.where(left, -identity, 0.0)
    offset[:order, :] = partial[...]
    offset[order:, :] = jnp.zeros((order, columns), f32)


def invert_kernel(squarings, own_ss, _, *refs):
    inverse_into(own_ss[...] + received_separator(refs[:-1]), refs[-1], squarings)


def store_element(stays, own, other, cross, ss, ps, sends):
    order = cross.shape[0]
    separator = jnp.where(stays, other, own)
    outer = jnp.where(stays, own, other)
    link = jnp.where(stays, cross, cross.T)
    ss[...] = separator
    ps[order:, :] = outer
    ps[:order, :] = link
    if sends:
        send_separator(separator, sends[0])
        send_link(link, outer, sends[1])


def pair_kernel(level, inv, own_ps, other_ps, gain_own, gain_other, ss, ps, *sends):
    order = inv.shape[0]
    stays = own_stays(level)
    inverse = inv[...]
    link_own, link_other = own_ps[:order, :], other_ps[:order, :]
    own_gain = nn(link_own, inverse, HIGH)
    other_gain = nn(link_other, inverse, HIGH)
    gain_own[...] = own_gain
    gain_other[...] = other_gain
    own = own_ps[order:, :] - nt(own_gain, link_own, HIGH)
    other = other_ps[order:, :] - nt(other_gain, link_other, HIGH)
    cross = -nt(own_gain, link_other, HIGH)
    store_element(stays, own, other, cross, ss, ps, sends)


def pass_kernel(_, arrived, passed):
    passed[...] = arrived[...]


def own_kernel(inv, own_ps, _, gain_own, reduced_own):
    order = inv.shape[0]
    link_own = own_ps[:order, :]
    gain_own[...] = nn(link_own, inv[...], HIGH)
    reduced_own[...] = own_ps[order:, :] - nt(gain_own[...], link_own, HIGH)


def merge_kernel(level, count, inv, gain_own, reduced_own, *refs):
    others, (gain_other, ss, ps, *sends) = refs[:count], refs[count:]
    order = inv.shape[0]
    stays = own_stays(level)
    link_other, outer_other = received_link(others)
    gain = nn(link_other, inv[...], HIGH)
    gain_other[...] = gain
    cross = -nt(gain_own[...], link_other, HIGH)
    reduced_other = outer_other - nt(gain, link_other, HIGH)
    store_element(stays, reduced_own[...], reduced_other, cross, ss, ps, sends)


def sources_step(level, inv, gain_own, gain_other, own_f, other_f):
    columns = own_f.shape[1] // 2
    stays = own_stays(level)
    own, other = own_f[...], other_f[...]
    held = own[:, columns:] + other[:, columns:]
    after_own = own[:, :columns] - halves(gain_own[...], held, HIGH)
    after_other = other[:, :columns] - halves(gain_other[...], held, HIGH)
    partial = halves(inv[...], held, HIGH)
    return jnp.where(stays, after_own, after_other), jnp.where(stays, after_other, after_own), partial


def sources_kernel(level, inv, gain_own, gain_other, own_f, other_f, _, sources, partial):
    columns = partial.shape[1]
    outer, inner, found = sources_step(level, inv, gain_own, gain_other, own_f, other_f)
    sources[:, :columns] = outer
    sources[:, columns:] = inner
    partial[...] = found


def factors_step(level, gain_own, gain_other, partial, factors, offset):
    stays = own_stays(level)
    inner = split(factors[1])
    new_offset = offset[...] - three_pass(inner, split(partial[...]))
    own_end = factors[0] - three_pass(inner, split(gain_own[...]), nt)
    other_end = -three_pass(inner, split(gain_other[...]), nt)
    return jnp.where(stays, own_end, other_end), jnp.where(stays, other_end, own_end), new_offset


def factors_kernel(level, gain_own, gain_other, partial, _, factors, offset, new_factors, new_offset):
    outer, inner, moved = factors_step(level, gain_own, gain_other, partial, factors, offset)
    new_factors[0] = outer
    new_factors[1] = inner
    new_offset[...] = moved


def end_kernel(ss, ps, end_inv, end_gain, new_ss, send_ss):
    order = ss.shape[0]
    rows = lax.broadcasted_iota(jnp.int32, (order, order), 0)
    identity = (rows == lax.broadcasted_iota(jnp.int32, (order, order), 1)).astype(f32)
    right = bit(chain_index(), LEVELS - 1) == 1
    inverse_into(jnp.where(right, ps[order:, :], identity), end_inv, 6)
    turned = ps[:order, :].T
    gain = halves(turned, end_inv[...], HIGH)
    end_gain[...] = gain
    separator = ss[...] - halves(gain, ps[:order, :], HIGH)
    new_ss[...] = separator
    for place, first in ((0, True), (PACKED, False)):
        main, diagonal = pack_symmetric(separator, first)
        send_ss[place : place + HALF, :] = main
        send_ss[place + HALF : place + PACKED, :] = diagonal


def end_sources_kernel(
    level, inv, gain_own, gain_other, own_f, other_f, end_inv, end_gain, _, sources, partial, end_partial
):
    outer, inner, found = sources_step(level, inv, gain_own, gain_other, own_f, other_f)
    sources[...] = inner - halves(end_gain[...], outer, HIGH)
    partial[...] = found
    end_partial[...] = halves(end_inv[...], outer, HIGH)


def end_factors_kernel(
    level, gain_own, gain_other, partial, _, factors, offset, end_gain, end_partial,
    new_factors, new_offset,
):
    outer, inner, moved = factors_step(level, gain_own, gain_other, partial, factors, offset)
    outer = split(outer)
    new_offset[...] = moved - three_pass(outer, split(end_partial[...]))
    new_factors[...] = inner - three_pass(outer, split(end_gain[...]), nt)


def back_kernel(inv, own_f, other_f, factors, offset, result):
    order = inv.shape[0]
    middle = halves(inv[...], own_f[...] + other_f[...], HIGH)
    both = offset[...] - three_pass(split(factors[...]), split(middle), halves)
    result[0] = both[:order]
    result[1] = both[order:]


WEIGHTS = {"invert": 0.85, "own": 0.1, "merge": 0.1, "sources": 0.3, "factors": 0.1, "pass": 0.05, "end": 0.1, "begin": 4.0, "tail": 0.1, "last": 0.1, "first": 2.0}


def call(kernel, name, operands, shapes):
    vmem = pl.BlockSpec(memory_space=pltpu.VMEM)
    flops = int(WEIGHTS[name.split("_")[0]] * 1e9)
    return pl.pallas_call(
        kernel,
        out_shape=[jax.ShapeDtypeStruct(shape, f32) for shape in shapes],
        in_specs=[vmem] * len(operands),
        out_specs=[vmem] * len(shapes),
        name=name,
        compiler_params=pltpu.CompilerParams(vmem_limit_bytes=40 << 20),
        cost_estimate=pl.CostEstimate(flops=flops, bytes_accessed=4096, transcendentals=0),
    )(*operands)


def local(diag_blocks, coupling, rhs):
    order, columns = rhs.shape[2:]
    square, tall = (order, order), (2 * order, order)
    small, medium = (PACKED, HALF), (2 * HALF + PACKED, HALF)
    flat, slim = (order, 2 * columns), (order, columns)
    double, long = (2, 2 * order, order), (2 * order, columns)
    (inv,) = call(first_invert_kernel, "first_invert", (diag_blocks[0],), (square,))
    gain_own, gain_other, ss, ps = call(
        first_merge_kernel, "first_merge", (inv, diag_blocks[0], coupling[0]),
        (square, square, square, tall)
    )
    others_ss = (exchange(ss, 1),)
    others_ps = (exchange(ps, 1),)
    sources, partial = call(
        first_sources_kernel, "first_sources", (rhs[0], inv, gain_own, gain_other, ss),
        (flat, slim)
    )
    other_f = exchange(sources, 1)
    factors, offset = call(
        first_factors_kernel, "first_factors", (gain_own, gain_other, partial, ss),
        (double, long)
    )

    def swapped(direct, after, name):
        (passed,) = call(pass_kernel, name, (after, direct), (direct.shape,))
        return (direct, exchange(passed, 1))

    for level in range(1, LEVELS):
        last = level == LEVELS - 1
        (inv,) = call(
            functools.partial(invert_kernel, SQUARINGS[level]), "begin" if level == 1 else f"invert_{level}",
            (ss, offset) + others_ss, (square,)
        )
        if level > 1:
            others_ps = swapped(direct_ps, inv, f"pass_ps_{level}")
            gain_own, reduced_own = call(
                own_kernel, f"own_{level}", (inv, ps, others_ps[0]), (square, square)
            )
            gain_other, ss, ps, *sends = call(
                functools.partial(merge_kernel, level, len(others_ps)), f"merge_{level}",
                (inv, gain_own, reduced_own) + others_ps,
                (square, square, tall) + (() if last else (small, medium)),
            )
        else:
            gain_own, gain_other, ss, ps, *sends = call(
                functools.partial(pair_kernel, level), f"merge_{level}", (inv, ps) + others_ps,
                (square, square, square, tall, small, medium),
            )
        if last:
            end_inv, end_gain, ss, send_ss = call(
                end_kernel, "end", (ss, ps), (square, square, square, (2 * PACKED, HALF))
            )
        else:
            send_ss, send_ps = sends
        direct_ss = exchange(send_ss, level + 1)
        held = (inv, gain_own, gain_other, sources, other_f)
        after = send_ss
        if last:
            sources, partial, end_partial = call(
                functools.partial(end_sources_kernel, level), "tail_sources",
                held + (end_inv, end_gain, send_ss), (slim, slim, slim),
            )
            after = sources
        else:
            direct_ps = exchange(send_ps, level + 1)
        if level > 1:
            factors, offset = call(
                functools.partial(factors_kernel, level - 1), f"factors_{level - 1}",
                before + (after, factors, offset), (double, long),
            )
            after = offset
        if not last:
            sources, partial = call(
                functools.partial(sources_kernel, level), f"sources_{level}",
                held + (after,), (flat, slim),
            )
        before = (gain_own, gain_other, partial)
        other_f = exchange(sources, level + 1)
        others_ss = (direct_ss,) if last else swapped(direct_ss, sources, f"pass_ss_{level + 1}")
    factors, offset = call(
        functools.partial(end_factors_kernel, level), "tail_factors",
        before + (sources, factors, offset, end_gain, end_partial), (tall, long),
    )
    (inv,) = call(
        functools.partial(invert_kernel, SQUARINGS[LEVELS]), "last_invert", (ss, offset) + others_ss,
        (square,)
    )
    (result,) = call(
        back_kernel, "tail_back", (inv, sources, other_f, factors, offset), ((2, order, columns),)
    )
    return result[None]


def solution(mesh):
    spec = P("seg", "run", None, None)
    return jax.shard_map(
        local, mesh=mesh, in_specs=(spec, spec, spec), out_specs=spec, check_vma=False
    )
```

```python
import functools

import jax
import jax.numpy as jnp
from jax import lax
from jax.experimental import pallas as pl
from jax.experimental.pallas import tpu as pltpu
from jax.sharding import PartitionSpec as P

HIGH = lax.Precision.HIGHEST
f32 = jnp.float32
bf16 = jnp.bfloat16
LEVELS = 7
TOLERANCE = 4e-3
SQUARINGS = (5, 4, 3, 3, 2, 2, 2, 2)
AXES = ("run", "seg")


def chain_coords(flat):
    run, seg = flat >> 3, flat & 7
    return seg >> 1, ((seg & 1) << 1) | (run >> 3), (run >> 1) & 3, run & 1


def flat_index(x, z, y, core):
    return ((((z & 1) << 3) | (y << 1) | core) << 3) | (x << 1) | (z >> 1)


def partner(level, flat):
    x, z, y, core = chain_coords(flat)
    if level == 1:
        core = core ^ 1
    elif level == 2:
        y = y ^ 1
    elif level == 3:
        y = 3 - y
    elif level == 4:
        z = z ^ 1
    elif level == 5:
        z = 3 - z
    elif level == 6:
        x = x ^ 1
    else:
        x = 3 - x
    return flat_index(x, z, y, core)


def exchange(value, level):
    return lax.ppermute(value, AXES, [(flat, partner(level, flat)) for flat in range(128)])


def chain_index():
    run, seg = lax.axis_index("run"), lax.axis_index("seg")
    return seg * 16 + run


def bit(value, place):
    return lax.rem(lax.div(value, 1 << place), 2)


def own_stays(level):
    chain = chain_index()
    if level == LEVELS:
        return bit(chain, LEVELS - 1) == 0
    return bit(chain, level - 1) == bit(chain, level)


def nn(left, right, precision=None):
    return lax.dot_general(
        left, right, (((1,), (0,)), ((), ())), precision=precision, preferred_element_type=f32
    )


def nt(left, right, precision=None):
    return lax.dot_general(
        left, right, (((1,), (1,)), ((), ())), precision=precision, preferred_element_type=f32
    )


def halves(left, right, precision=None):
    half = left.shape[0] // 2
    return jnp.concatenate(
        [nn(left[:half], right, precision), nn(left[half:], right, precision)], axis=0
    )


def split(value):
    upper = value.astype(bf16)
    return upper, (value - upper.astype(f32)).astype(bf16)


def three_pass(left, right, dot=nn):
    lh, ll = left
    rh, rl = right
    return dot(lh, rh) + (dot(lh, rl) + dot(ll, rh))


def inverse_into(matrix, out_ref, squarings=5):
    order = matrix.shape[0]
    rows = lax.broadcasted_iota(jnp.int32, (order, order), 0)
    identity = (rows == lax.broadcasted_iota(jnp.int32, (order, order), 1)).astype(f32)
    norm = jnp.max(jnp.sum(jnp.abs(matrix), axis=0, keepdims=True), axis=1, keepdims=True)
    scale = 1.75 / norm
    rest = identity - matrix * scale
    found = (identity + rest) * scale
    rest = rest.astype(bf16)
    rest = halves(rest, rest).astype(bf16)
    for step in range(1, squarings):
        found = found + halves(found.astype(bf16), rest)
        if step < squarings - 1:
            rest = halves(rest, rest).astype(bf16)
    upper = split(found)
    rest = identity - three_pass(split(matrix), upper, halves)
    found = found + halves(upper[0], rest.astype(bf16))
    rest = identity - halves(matrix, found, HIGH)
    miss = jnp.sum(rest * rest)
    out_ref[...] = found + three_pass(split(found), split(rest), halves)

    @pl.when(jnp.logical_not(miss < TOLERANCE * TOLERANCE))
    def _():
        near = jnp.logical_and(miss < 0.25, scale > 0.0)
        out_ref[...] = jnp.where(near, out_ref[...], identity * scale)

        def unfinished(state):
            step, miss_now = state
            return jnp.logical_and(step < 64, miss_now >= TOLERANCE * TOLERANCE)

        def improve(state):
            now = out_ref[...]
            gap = identity - halves(matrix, now, HIGH)
            out_ref[...] = now + halves(now, gap, HIGH)
            return state[0] + 1, jnp.sum(gap * gap)

        lax.while_loop(unfinished, improve, (jnp.int32(0), jnp.float32(jnp.inf)))


HALF = 128
PACKED = HALF + 8


def on_first_core():
    return lax.rem(lax.axis_index("run"), 2) == 0


def ordered(direct, swapped):
    first = on_first_core()
    return jnp.where(first, direct, swapped), jnp.where(first, swapped, direct)


def triangle():
    rows = lax.broadcasted_iota(jnp.int32, (HALF, HALF), 0)
    columns = lax.broadcasted_iota(jnp.int32, (HALF, HALF), 1)
    return rows, columns


def pack_symmetric(value, first):
    rows, columns = triangle()
    upper_left, lower_right = value[:HALF, :HALF], value[HALF:, HALF:]
    diagonal = jnp.sum(jnp.where(rows == columns, lower_right, 0.0), axis=0, keepdims=True)
    both = jnp.where(rows >= columns, upper_left, lower_right)
    lower_left = value[HALF:, :HALF]
    main = (lower_left if first else both) if isinstance(first, bool) else jnp.where(first, lower_left, both)
    return main, jnp.broadcast_to(diagonal, (8, HALF))


def unpack_symmetric(from_first, from_second):
    rows, columns = triangle()
    lower_left, diagonal = from_first[:HALF], from_first[HALF : HALF + 1]
    both = from_second[:HALF]
    turned = both.T
    upper_left = jnp.where(rows >= columns, both, turned)
    lower_right = jnp.where(rows < columns, both, turned)
    lower_right = jnp.where(rows == columns, diagonal, lower_right)
    return jnp.concatenate(
        [
            jnp.concatenate([upper_left, lower_left.T], axis=1),
            jnp.concatenate([lower_left, lower_right], axis=1),
        ],
        axis=0,
    )


def send_separator(value, send):
    main, diagonal = pack_symmetric(value, on_first_core())
    send[:HALF, :] = main
    send[HALF:, :] = diagonal


def send_link(link, outer, send):
    first = on_first_core()
    rows = jnp.where(first, link[:HALF], link[HALF:])
    send[:HALF, :] = rows[:, :HALF]
    send[HALF : 2 * HALF, :] = rows[:, HALF:]
    main, diagonal = pack_symmetric(outer, first)
    send[2 * HALF : 3 * HALF, :] = main
    send[3 * HALF :, :] = diagonal


def received_separator(refs):
    if len(refs) == 1:
        value = refs[0][...]
        return value if value.shape[1] > HALF else unpack_symmetric(value[:PACKED], value[PACKED:])
    return unpack_symmetric(*ordered(refs[0][...], refs[1][...]))


def received_link(refs):
    if len(refs) == 1:
        order = refs[0].shape[1]
        return refs[0][:order, :], refs[0][order:, :]
    upper, lower = ordered(refs[0][...], refs[1][...])
    link = jnp.concatenate(
        [
            jnp.concatenate([upper[:HALF], upper[HALF : 2 * HALF]], axis=1),
            jnp.concatenate([lower[:HALF], lower[HALF : 2 * HALF]], axis=1),
        ],
        axis=0,
    )
    return link, unpack_symmetric(upper[2 * HALF :], lower[2 * HALF :])


def first_invert_kernel(diag, inv):
    inverse_into(diag[0], inv)


def first_merge_kernel(inv, diag, couple, gain_own, gain_other, ss, ps):
    order = inv.shape[0]
    start = chain_index() == 0
    above = jnp.where(start, 0.0, couple[0]).T
    below = couple[1]
    inverse = inv[...]
    gain_above = nn(above, inverse, HIGH)
    gain_below = nn(below, inverse, HIGH)
    own_above = -nt(gain_above, above, HIGH)
    own_below = diag[1] - nt(gain_below, below, HIGH)
    link = -nt(gain_above, below, HIGH)
    left = on_first_core()
    gain_own[...] = jnp.where(left, gain_above, gain_below)
    gain_other[...] = jnp.where(left, gain_below, gain_above)
    ss[...] = jnp.where(left, own_below, own_above)
    ps[order:, :] = jnp.where(left, own_above, own_below)
    ps[:order, :] = jnp.where(left, link, link.T)


def first_sources_kernel(source, inv, gain_own, gain_other, _, sources, partial):
    columns = partial.shape[1]
    held = source[0]
    left = on_first_core()
    sources[:, :columns] = jnp.where(left, 0.0, source[1]) - nn(gain_own[...], held, HIGH)
    sources[:, columns:] = jnp.where(left, source[1], 0.0) - nn(gain_other[...], held, HIGH)
    partial[...] = nn(inv[...], held, HIGH)


def first_factors_kernel(gain_own, gain_other, partial, _, factors, offset):
    order, columns = partial.shape
    rows = lax.broadcasted_iota(jnp.int32, (order, order), 0)
    identity = (rows == lax.broadcasted_iota(jnp.int32, (order, order), 1)).astype(f32)
    left = on_first_core()
    factors[0, :order, :] = gain_own[...].T
    factors[1, :order, :] = gain_other[...].T
    factors[0, order:, :] = jnp.where(left, 0.0, -identity)
    factors[1, order:, :] = jnp.where(left, -identity, 0.0)
    offset[:order, :] = partial[...]
    offset[order:, :] = jnp.zeros((order, columns), f32)


def invert_kernel(squarings, own_ss, _, *refs):
    inverse_into(own_ss[...] + received_separator(refs[:-1]), refs[-1], squarings)


def store_element(stays, own, other, cross, ss, ps, sends):
    order = cross.shape[0]
    separator = jnp.where(stays, other, own)
    outer = jnp.where(stays, own, other)
    link = jnp.where(stays, cross, cross.T)
    ss[...] = separator
    ps[order:, :] = outer
    ps[:order, :] = link
    if sends:
        send_separator(separator, sends[0])
        send_link(link, outer, sends[1])


def pair_kernel(level, inv, own_ps, other_ps, gain_own, gain_other, ss, ps, *sends):
    order = inv.shape[0]
    stays = own_stays(level)
    inverse = inv[...]
    link_own, link_other = own_ps[:order, :], other_ps[:order, :]
    own_gain = nn(link_own, inverse, HIGH)
    other_gain = nn(link_other, inverse, HIGH)
    gain_own[...] = own_gain
    gain_other[...] = other_gain
    own = own_ps[order:, :] - nt(own_gain, link_own, HIGH)
    other = other_ps[order:, :] - nt(other_gain, link_other, HIGH)
    cross = -nt(own_gain, link_other, HIGH)
    store_element(stays, own, other, cross, ss, ps, sends)


def pass_kernel(_, arrived, passed):
    passed[...] = arrived[...]


def own_kernel(inv, own_ps, _, gain_own, reduced_own):
    order = inv.shape[0]
    link_own = own_ps[:order, :]
    gain_own[...] = nn(link_own, inv[...], HIGH)
    reduced_own[...] = own_ps[order:, :] - nt(gain_own[...], link_own, HIGH)


def merge_kernel(level, count, inv, gain_own, reduced_own, *refs):
    others, (gain_other, ss, ps, *sends) = refs[:count], refs[count:]
    order = inv.shape[0]
    stays = own_stays(level)
    link_other, outer_other = received_link(others)
    gain = nn(link_other, inv[...], HIGH)
    gain_other[...] = gain
    cross = -nt(gain_own[...], link_other, HIGH)
    reduced_other = outer_other - nt(gain, link_other, HIGH)
    store_element(stays, reduced_own[...], reduced_other, cross, ss, ps, sends)


def sources_step(level, inv, gain_own, gain_other, own_f, other_f):
    columns = own_f.shape[1] // 2
    stays = own_stays(level)
    own, other = own_f[...], other_f[...]
    held = own[:, columns:] + other[:, columns:]
    after_own = own[:, :columns] - halves(gain_own[...], held, HIGH)
    after_other = other[:, :columns] - halves(gain_other[...], held, HIGH)
    partial = halves(inv[...], held, HIGH)
    return jnp.where(stays, after_own, after_other), jnp.where(stays, after_other, after_own), partial


def sources_kernel(level, inv, gain_own, gain_other, own_f, other_f, _, sources, partial):
    columns = partial.shape[1]
    outer, inner, found = sources_step(level, inv, gain_own, gain_other, own_f, other_f)
    sources[:, :columns] = outer
    sources[:, columns:] = inner
    partial[...] = found


def factors_step(level, gain_own, gain_other, partial, factors, offset):
    stays = own_stays(level)
    inner = split(factors[1])
    new_offset = offset[...] - three_pass(inner, split(partial[...]))
    own_end = factors[0] - three_pass(inner, split(gain_own[...]), nt)
    other_end = -three_pass(inner, split(gain_other[...]), nt)
    return jnp.where(stays, own_end, other_end), jnp.where(stays, other_end, own_end), new_offset


def factors_kernel(level, gain_own, gain_other, partial, _, factors, offset, new_factors, new_offset):
    outer, inner, moved = factors_step(level, gain_own, gain_other, partial, factors, offset)
    new_factors[0] = outer
    new_factors[1] = inner
    new_offset[...] = moved


def end_kernel(ss, ps, end_inv, end_gain, new_ss, send_ss):
    order = ss.shape[0]
    rows = lax.broadcasted_iota(jnp.int32, (order, order), 0)
    identity = (rows == lax.broadcasted_iota(jnp.int32, (order, order), 1)).astype(f32)
    right = bit(chain_index(), LEVELS - 1) == 1
    inverse_into(jnp.where(right, ps[order:, :], identity), end_inv, 6)
    turned = ps[:order, :].T
    gain = halves(turned, end_inv[...], HIGH)
    end_gain[...] = gain
    separator = ss[...] - halves(gain, ps[:order, :], HIGH)
    new_ss[...] = separator
    for place, first in ((0, True), (PACKED, False)):
        main, diagonal = pack_symmetric(separator, first)
        send_ss[place : place + HALF, :] = main
        send_ss[place + HALF : place + PACKED, :] = diagonal


def end_sources_kernel(
    level, inv, gain_own, gain_other, own_f, other_f, end_inv, end_gain, _, sources, partial, end_partial
):
    outer, inner, found = sources_step(level, inv, gain_own, gain_other, own_f, other_f)
    sources[...] = inner - halves(end_gain[...], outer, HIGH)
    partial[...] = found
    end_partial[...] = halves(end_inv[...], outer, HIGH)


def end_factors_kernel(
    level, gain_own, gain_other, partial, _, factors, offset, end_gain, end_partial,
    new_factors, new_offset,
):
    outer, inner, moved = factors_step(level, gain_own, gain_other, partial, factors, offset)
    outer = split(outer)
    new_offset[...] = moved - three_pass(outer, split(end_partial[...]))
    new_factors[...] = inner - three_pass(outer, split(end_gain[...]), nt)


def back_kernel(inv, own_f, other_f, factors, offset, result):
    order = inv.shape[0]
    middle = halves(inv[...], own_f[...] + other_f[...], HIGH)
    both = offset[...] - three_pass(split(factors[...]), split(middle), halves)
    result[0] = both[:order]
    result[1] = both[order:]


WEIGHTS = {"invert": 0.85, "own": 0.1, "merge": 0.1, "sources": 0.3, "factors": 0.1, "pass": 0.05, "end": 0.1, "begin": 4.0, "tail": 0.1, "last": 0.1, "first": 2.0}


def call(kernel, name, operands, shapes):
    vmem = pl.BlockSpec(memory_space=pltpu.VMEM)
    flops = int(WEIGHTS[name.split("_")[0]] * 1e9)
    return pl.pallas_call(
        kernel,
        out_shape=[jax.ShapeDtypeStruct(shape, f32) for shape in shapes],
        in_specs=[vmem] * len(operands),
        out_specs=[vmem] * len(shapes),
        name=name,
        compiler_params=pltpu.CompilerParams(vmem_limit_bytes=40 << 20),
        cost_estimate=pl.CostEstimate(flops=flops, bytes_accessed=4096, transcendentals=0),
    )(*operands)


def local(diag_blocks, coupling, rhs):
    order, columns = rhs.shape[2:]
    square, tall = (order, order), (2 * order, order)
    small, medium = (PACKED, HALF), (2 * HALF + PACKED, HALF)
    flat, slim = (order, 2 * columns), (order, columns)
    double, long = (2, 2 * order, order), (2 * order, columns)
    (inv,) = call(first_invert_kernel, "first_invert", (diag_blocks[0],), (square,))
    gain_own, gain_other, ss, ps = call(
        first_merge_kernel, "first_merge", (inv, diag_blocks[0], coupling[0]),
        (square, square, square, tall)
    )
    others_ss = (exchange(ss, 1),)
    others_ps = (exchange(ps, 1),)
    sources, partial = call(
        first_sources_kernel, "first_sources", (rhs[0], inv, gain_own, gain_other, ss),
        (flat, slim)
    )
    other_f = exchange(sources, 1)
    factors, offset = call(
        first_factors_kernel, "first_factors", (gain_own, gain_other, partial, ss),
        (double, long)
    )

    def swapped(direct, after, name):
        (passed,) = call(pass_kernel, name, (after, direct), (direct.shape,))
        return (direct, exchange(passed, 1))

    for level in range(1, LEVELS):
        last = level == LEVELS - 1
        (inv,) = call(
            functools.partial(invert_kernel, SQUARINGS[level]), "begin" if level == 1 else f"invert_{level}",
            (ss, offset) + others_ss, (square,)
        )
        if level > 1:
            others_ps = swapped(direct_ps, inv, f"pass_ps_{level}")
            gain_own, reduced_own = call(
                own_kernel, f"own_{level}", (inv, ps, others_ps[0]), (square, square)
            )
            gain_other, ss, ps, *sends = call(
                functools.partial(merge_kernel, level, len(others_ps)), f"merge_{level}",
                (inv, gain_own, reduced_own) + others_ps,
                (square, square, tall) + (() if last else (small, medium)),
            )
        else:
            gain_own, gain_other, ss, ps, *sends = call(
                functools.partial(pair_kernel, level), f"merge_{level}", (inv, ps) + others_ps,
                (square, square, square, tall, small, medium),
            )
        if last:
            end_inv, end_gain, ss, send_ss = call(
                end_kernel, "end", (ss, ps), (square, square, square, (2 * PACKED, HALF))
            )
        else:
            send_ss, send_ps = sends
        direct_ss = exchange(send_ss, level + 1)
        held = (inv, gain_own, gain_other, sources, other_f)
        if last:
            sources, partial, end_partial = call(
                functools.partial(end_sources_kernel, level), "tail_sources",
                held + (end_inv, end_gain, send_ss), (slim, slim, slim)
            )
        else:
            direct_ps = exchange(send_ps, level + 1)
            sources, partial = call(
                functools.partial(sources_kernel, level), f"sources_{level}",
                held + (send_ss,), (flat, slim)
            )
        other_f = exchange(sources, level + 1)
        before = (gain_own, gain_other, partial, send_ss, factors, offset)
        if last:
            factors, offset = call(
                functools.partial(end_factors_kernel, level), "tail_factors",
                before + (end_gain, end_partial), (tall, long)
            )
        else:
            factors, offset = call(
                functools.partial(factors_kernel, level), f"factors_{level}", before,
                (double, long)
            )
        others_ss = (direct_ss,) if last else swapped(direct_ss, offset, f"pass_ss_{level + 1}")
    (inv,) = call(
        functools.partial(invert_kernel, SQUARINGS[LEVELS]), "last_invert", (ss, offset) + others_ss,
        (square,)
    )
    (result,) = call(
        back_kernel, "tail_back", (inv, sources, other_f, factors, offset), ((2, order, columns),)
    )
    return result[None]


def solution(mesh):
    spec = P("seg", "run", None, None)
    return jax.shard_map(
        local, mesh=mesh, in_specs=(spec, spec, spec), out_specs=spec, check_vma=False
    )
```
